128 devices in a mesh: ex: 16 (over z, y), ey: 8 (over x, core).
Axes of the slice: x: 4, y: 4, z: 4, core: 2. Of those that a mesh axis runs over, the one named last changes fastest.
Arguments:
- fields: float32 [65536, 3, 512], P(('ex', 'ey')), may hold values from -6 to 6
- particles: float32 [65536, 128], P(('ex', 'ey')), as said below
- counts: int32 [65536], P(('ex', 'ey')), may hold values from 1 to 16
- new_place: int32 [65536], P(('ex', 'ey')), may hold values from 0 to 65535, as said below
Outputs:
- velocity_next: float32 [65536, 3, 512], P(('ex', 'ey'))
- particles_next: float32 [65536, 128], P(('ex', 'ey'))
The draws below stay inside these ranges and needn't reach their ends.
Inputs may be any that keep to these rules, and one draw needn't show every extreme that they name: new_place is a permutation of all elements; each device sends either none or exactly 4 of its elements to any other device, keeps the rest in place, and receives as many as it sends. `particles`: coordinates lie in [-1, 1], ratios in [0.1, 0.9], masses in [0.5, 2].
All inputs are finite; a program needn't handle non-finite values.
Results may differ from the reference program's by a relative error of at most 0.0003.
Values sent between devices are 32-bit elements; how exact they have to be, the bound alone decides.
No kernel may reach another device: no remote copies, remote signals or barrier semaphores. Data moves between devices by JAX's collectives and lax.ppermute only.
A program may use at most 128 MiB of HBM per device.

```python
import jax
import jax.numpy as jnp
import numpy as np
from jax import lax

NP = 8
SLOTS = 16
CAP = 4
BX = 4
BY = 8
BZ = 16
NODES = 512
EL_DEV = 512
ELEMENTS = 65536
PEERS = 64
N_EX = 16
N_EY = 8


def draw_particles(key, part):
    key = jax.random.fold_in(key, 5)
    keys = jax.random.split(key, 4)
    coords = jax.random.uniform(keys[0], (ELEMENTS, 3, SLOTS), jnp.float32, -1.0, 1.0)
    velocity = jax.random.normal(keys[1], (ELEMENTS, 3, SLOTS), jnp.float32)
    ratio = jax.random.uniform(keys[2], (ELEMENTS, 1, SLOTS), jnp.float32, 0.1, 0.9)
    mass = jnp.exp(jax.random.uniform(keys[3], (ELEMENTS, 1, SLOTS), jnp.float32, jnp.log(0.5), jnp.log(2.0)))
    record = jnp.concatenate([coords, velocity, ratio, mass], 1)
    return record.reshape(ELEMENTS, 8 * SLOTS)


def draw_new_place(key, part):
    key = jax.random.fold_in(key, 11)
    devices = ELEMENTS // EL_DEV
    first_key, second_key = jax.random.split(key)
    orders = jax.vmap(lambda k: jax.random.permutation(k, EL_DEV))(jax.random.split(first_key, devices))
    offsets = 1 + jax.random.permutation(second_key, devices - 1)[:PEERS]
    movers = jnp.arange(PEERS * CAP)
    device_ids = jnp.arange(devices)
    target = (device_ids[:, None] + offsets[movers // CAP][None, :]) % devices
    source_slot = orders[:, :PEERS * CAP]
    target_slot = orders[target, movers[None, :]]
    place = jnp.arange(ELEMENTS).reshape(devices, EL_DEV)
    place = place.at[device_ids[:, None], source_slot].set(target * EL_DEV + target_slot)
    return place.reshape(ELEMENTS).astype(jnp.int32)


def touch_ends(values, key, low, largest):
    longest = values.shape.index(max(values.shape))
    spots = []
    for shift in (0, 1):
        where = [jax.random.randint(jax.random.fold_in(key, axis), (), 0, length) for axis, length in enumerate(values.shape)]
        where[longest] = (where[longest] + shift) % values.shape[longest]
        spots.append(tuple(where))
    return values.at[spots[0]].set(low).at[spots[1]].set(largest)


def block_levels(stream_key, shape, cuts, least, largest):
    gain, own = 1.0, jax.random.fold_in(stream_key, 6)
    for axis_at, blocks in cuts:
        draws = jnp.exp(jax.random.uniform(jax.random.fold_in(own, axis_at), (blocks,), jnp.float32, least / len(cuts), largest / len(cuts)))
        gain = gain * jnp.repeat(draws, shape[axis_at] // blocks).reshape([-1 if axis == axis_at else 1 for axis in range(len(shape))])
    return gain


def bell_draw(stream_key, dims, deviation, limit, shards=(), held_as=jnp.bfloat16):
    level = block_levels(stream_key, dims, shards, -0.22, 0.18) if shards else 1.0
    entries = jax.random.normal(stream_key, dims, jnp.float32) * deviation * level
    return jnp.minimum(jnp.maximum(entries, -limit), limit).astype(held_as)


def setup_inputs(seed: int = 0) -> dict:
    streams_of = jax.random.split(jax.random.key(seed), 5)
    fields = bell_draw(streams_of[0], (ELEMENTS, 3, NODES), 1.0, 6.0, ((0, 128),), jnp.float32)
    particles = draw_particles(jax.random.fold_in(streams_of[4], 71), 0)
    counts = touch_ends(jax.random.randint(streams_of[2], (ELEMENTS,), 1, SLOTS + 1), jax.random.fold_in(streams_of[2], 1), 1, SLOTS).astype(jnp.int32)
    new_place = draw_new_place(jax.random.fold_in(streams_of[4], 71), 0)
    return dict(fields=fields, particles=particles, counts=counts, new_place=new_place)


def gll_points(count):
    table = {4: [-1.0, -0.4472135954999579, 0.4472135954999579, 1.0],
             8: [-1.0, -0.8717401485096066, -0.5917001814331423, -0.2092992179024789,
                 0.2092992179024789, 0.5917001814331423, 0.8717401485096066, 1.0]}
    return np.array(table[count])


def lagrange(coord):
    points = gll_points(NP)
    columns = []
    for first in range(NP):
        term = jnp.ones_like(coord)
        for second in range(NP):
            if second != first:
                term = term * ((coord - float(points[second])) / float(points[first] - points[second]))
        columns.append(term)
    return jnp.stack(columns, -1)


def gaussian(coord):
    points = jnp.asarray(gll_points(NP), jnp.float32).astype(coord.dtype)
    return jnp.exp(-((points[None, None, :] - coord[:, :, None]) ** 2) * (0.5 / 0.35 ** 2))


def tensor_basis(along_x, along_y, along_z):
    rows = along_x.shape[0]
    full = along_x[:, :, :, None, None] * along_y[:, :, None, :, None] * along_z[:, :, None, None, :]
    return full.reshape(rows, SLOTS, NP ** 3)


def element_section(fields, particles, counts):
    rows = fields.shape[0]
    highest = lax.Precision.HIGHEST
    record = particles.reshape(rows, 8, SLOTS)
    interp = tensor_basis(lagrange(record[:, 0]), lagrange(record[:, 1]), lagrange(record[:, 2]))
    fluid = jnp.einsum('nfk,npk->nfp', fields, interp, precision=highest)
    velocity = record[:, 3:6]
    ratio = record[:, 6:7]
    mass = record[:, 7:8]
    live = (jnp.arange(SLOTS)[None, :] < counts[:, None]).astype(fields.dtype)[:, None, :]
    gap = fluid - velocity
    velocity_new = velocity + live * ratio * gap
    push = -(live * mass * ratio * gap)
    spread = tensor_basis(gaussian(record[:, 0]), gaussian(record[:, 1]), gaussian(record[:, 2]))
    force = jnp.einsum('nfp,npk->nfk', push, spread, precision=highest)
    record_new = jnp.concatenate([record[:, 0:3], velocity_new, record[:, 6:8]], 1)
    return force, record_new.reshape(rows, 8 * SLOTS)


def section_blocks(fields, particles, counts):
    groups = fields.shape[0] // 64
    force, record = lax.map(lambda parts: element_section(*parts),
                            (fields.reshape(groups, 64, 3, NP ** 3),
                             particles.reshape(groups, 64, 8 * SLOTS),
                             counts.reshape(groups, 64)))
    return force.reshape(groups * 64, 3, NP, NP, NP), record.reshape(groups * 64, 8 * SLOTS)


def shared_faces(block, el_axis, node_axis, below, above):
    moved = jnp.moveaxis(block, (el_axis, node_axis), (0, 1))
    upper = moved[:, -1]
    lower = moved[:, 0]
    upper_ext = jnp.concatenate([below[None], upper], 0)
    lower_ext = jnp.concatenate([lower, above[None]], 0)
    summed = upper_ext + lower_ext
    moved = moved.at[:, -1].set(summed[1:]).at[:, 0].set(summed[:-1])
    return jnp.moveaxis(moved, (0, 1), (el_axis, node_axis))


def reference(fields, particles, counts, new_place):
    moved_fields = jnp.zeros_like(fields).at[new_place].set(fields)
    moved_particles = jnp.zeros_like(particles).at[new_place].set(particles)
    moved_counts = jnp.zeros_like(counts).at[new_place].set(counts)
    force, particles_next = section_blocks(moved_fields, moved_particles, moved_counts)
    order = (0, 2, 1, 3, 4, 5, 6, 7, 8)
    brick = force.reshape(N_EX, N_EY, BX, BY, BZ, 3, NP, NP, NP).transpose(order)
    brick = brick.reshape(N_EX * BX, N_EY * BY, BZ, 3, NP, NP, NP)
    for el_axis, node_axis in ((0, 4), (1, 5), (2, 6)):
        edge = jnp.moveaxis(brick, (el_axis, node_axis), (0, 1))[0, 0]
        zero = jnp.zeros_like(edge)
        brick = shared_faces(brick, el_axis, node_axis, zero, zero)
    force = brick.reshape(N_EX, BX, N_EY, BY, BZ, 3, NP, NP, NP).transpose(order)
    force = force.reshape(ELEMENTS, 3, NP ** 3)
    velocity_next = moved_fields + 0.5 * force
    return velocity_next, particles_next
```

```python
import functools

import jax
import jax.numpy as jnp
import numpy as np
from jax import lax
from jax.experimental import pallas as pl
from jax.experimental.pallas import tpu as pltpu
from jax.sharding import PartitionSpec as P

NP = 8
SLOTS = 16
CAP = 4
BX = 4
BY = 8
BZ = 16
NODES = NP**3
EL = BX * BY * BZ
LANES = 128
PARTS = 8 * SLOTS
HEAD = 8
COMP = 16
AXES = ("ex", "ey")
POINTS = [
    -1.0,
    -0.8717401485096066,
    -0.5917001814331423,
    -0.2092992179024789,
    0.2092992179024789,
    0.5917001814331423,
    0.8717401485096066,
    1.0,
]
F32 = jnp.float32
BF16 = jnp.bfloat16
VMEM_LIMIT = 56 * 1024 * 1024


def iota(shape, axis):
    return lax.broadcasted_iota(jnp.int32, shape, axis)


def split(x):
    high = x.astype(BF16)
    return high, (x - high.astype(F32)).astype(BF16)


def picked(onehot, x):
    high, low = split(x)
    return jnp.dot(onehot, high, preferred_element_type=F32) + jnp.dot(
        onehot, low, preferred_element_type=F32
    )


def as_column(row):
    return jnp.broadcast_to(row, (LANES, EL)).T


def pack_positions(place, rank):
    target = place // EL
    moving = target != rank
    key = jnp.where(moving, target, -1).astype(F32)
    key_col = as_column(key)
    order = []
    for j in range(EL // LANES):
        piece = key[:, j * LANES : (j + 1) * LANES]
        earlier = iota((EL, LANES), 0) < iota((EL, LANES), 1) + j * LANES
        same = (key_col == piece) & earlier
        order.append(jnp.sum(same.astype(F32), axis=0, keepdims=True))
    order = jnp.concatenate(order, axis=1).astype(jnp.int32)
    return jnp.where(moving, target * CAP + order, -1)


def interleave(first, second):
    devices = first.shape[0] // CAP
    low = iota((devices // 2, 8, LANES), 1) < CAP
    first = first.reshape(devices // 2, 8, LANES)
    second = second.reshape(devices // 2, 8, LANES)
    even = jnp.where(low, first, pltpu.roll(second, CAP, 1))
    odd = jnp.where(low, pltpu.roll(first, CAP, 1), second)
    return jnp.stack([even, odd], axis=1).reshape(devices, 8, LANES)


def deinterleave(blocks):
    devices = blocks.shape[0]
    pairs = blocks.reshape(devices // 2, 2, 8, LANES)
    even, odd = pairs[:, 0], pairs[:, 1]
    low = iota((devices // 2, 8, LANES), 1) < CAP
    first = jnp.where(low, even, pltpu.roll(odd, CAP, 1))
    second = jnp.where(low, pltpu.roll(even, CAP, 1), odd)
    return first.reshape(devices * CAP, LANES), second.reshape(devices * CAP, LANES)


def pack_kernel(rank_ref, place_ref, count_ref, fields_ref, part_ref, out_ref):
    devices = out_ref.shape[0]
    place = place_ref[...]
    position = pack_positions(place, rank_ref[0])
    onehot = (iota((devices * CAP, EL), 0) == position).astype(BF16)
    extra = jnp.concatenate(
        [count_ref[...], place % EL + 1, jnp.zeros((LANES - 2, EL), jnp.int32)], axis=0
    )
    extra = extra.astype(F32).T
    rows = picked(onehot, jnp.concatenate([part_ref[...], extra], axis=1))
    out_ref[:, 0:HEAD, :] = interleave(rows[:, :LANES], rows[:, LANES:])
    for f in range(3):
        rows = picked(onehot, fields_ref[f])
        for h in range(2):
            at = HEAD + COMP * f + 8 * h
            left = 2 * h * LANES
            out_ref[:, at : at + 8, :] = interleave(
                rows[:, left : left + LANES], rows[:, left + LANES : left + 2 * LANES]
            )


def lagrange_rows(coord):
    diffs = [coord - p for p in POINTS]
    left = [None] * NP
    right = [None] * NP
    for i in range(1, NP):
        left[i] = diffs[i - 1] if i == 1 else left[i - 1] * diffs[i - 1]
    for i in range(NP - 2, -1, -1):
        right[i] = diffs[i + 1] if i == NP - 2 else right[i + 1] * diffs[i + 1]
    out = []
    for i in range(NP):
        scale = 1.0
        for m in range(NP):
            if m != i:
                scale /= POINTS[i] - POINTS[m]
        if i == 0:
            term = right[0]
        elif i == NP - 1:
            term = left[i]
        else:
            term = left[i] * right[i]
        out.append(term * float(scale))
    return out


def gaussian_rows(coord):
    return [jnp.exp(-((p - coord) ** 2) * (0.5 / 0.35**2)) for p in POINTS]


def shift_z(x):
    n = x.shape[0] // NP
    x = x.reshape(n, NP, LANES)
    node = iota((n, NP, LANES), 1)
    bz = iota((n, NP, LANES), 2) % BZ
    down = pltpu.roll(pltpu.roll(x, 1, 1), 1, 2)
    up = pltpu.roll(pltpu.roll(x, NP - 1, 1), LANES - 1, 2)
    x = x + jnp.where((node == 0) & (bz > 0), down, 0.0)
    x = x + jnp.where((node == NP - 1) & (bz < BZ - 1), up, 0.0)
    return x.reshape(n * NP, LANES)


def section_kernel(
    rank_ref,
    place_ref,
    count_ref,
    fields_ref,
    part_ref,
    recv_ref,
    z_ref,
    xup_ref,
    xdn_ref,
    yup_ref,
    ydn_ref,
    part_out_ref,
    onehot_ref,
    stay_ref,
    tp_ref,
    basis_ref,
    t_ref,
    force_ref,
    work_ref,
    push_ref,
    live_ref,
):
    tiles = EL // LANES
    particles, extra = deinterleave(recv_ref[:, 0:HEAD, :])
    slot_row = extra.T[1:2, :]
    onehot = (iota((EL, EL), 0) + 1 == slot_row.astype(jnp.int32)).astype(BF16)
    onehot_ref[...] = onehot
    stay = (place_ref[...] // EL == rank_ref[0]).astype(F32)
    stay_col = as_column(stay)
    stay_ref[...] = stay_col
    both = picked(onehot, jnp.concatenate([particles, extra], axis=1))
    moved_part = jnp.where(stay_col > 0, part_ref[...], both[:, :LANES]).T
    moved_count = jnp.where(stay > 0, count_ref[...].astype(F32), both[:, LANES:].T[0:1, :])
    for t in range(tiles):
        tp_ref[t] = moved_part[:, t * LANES : (t + 1) * LANES]
        slot = iota((SLOTS, LANES), 0).astype(F32)
        live_ref[t] = (slot < moved_count[:, t * LANES : (t + 1) * LANES]).astype(F32)

    def make_basis(t, carry):
        for d in range(3):
            coord = tp_ref[t, d * SLOTS : (d + 1) * SLOTS, :]
            for kind, rows in ((0, lagrange_rows(coord)), (1, gaussian_rows(coord))):
                for n in range(NP):
                    basis_ref[t, 2 * d + kind, n * SLOTS : (n + 1) * SLOTS, :] = rows[n]
        return carry

    lax.fori_loop(0, tiles, make_basis, 0)

    for f in range(3):
        pieces = []
        for h in range(2):
            at = HEAD + COMP * f + 8 * h
            pieces += list(deinterleave(recv_ref[:, at : at + 8, :]))
        rows = picked(onehot_ref[...], jnp.concatenate(pieces, axis=1))
        for j in range(NODES // LANES):
            cols = slice(j * LANES, (j + 1) * LANES)
            moved = jnp.where(stay_ref[...] > 0, fields_ref[f, :, cols], rows[:, cols]).T
            for t in range(tiles):
                t_ref[f, t, cols, :] = moved[:, t * LANES : (t + 1) * LANES]

    def step(index, carry):
        f = index // tiles
        t = index % tiles

        def basis(which, n, p):
            return basis_ref[t, which, pl.ds(n * SLOTS + p, 1), :]

        total = [None] * SLOTS
        for pair in range(NP // 2):
            nodes = [
                [t_ref[f, t, pl.ds(a * 64 + (2 * pair + i) * 8, 8), :] for a in range(NP)]
                for i in range(2)
            ]
            for p in range(SLOTS):
                sums = [None, None]
                for a in range(NP):
                    weight = basis(0, a, p)
                    for i in range(2):
                        term = nodes[i][a] * weight
                        sums[i] = term if sums[i] is None else sums[i] + term
                for i in range(2):
                    term = sums[i] * basis(2, 2 * pair + i, p)
                    total[p] = term if total[p] is None else total[p] + term
        for p in range(SLOTS):
            along_z = basis_ref[t, 4, pl.ds(p, NP, stride=SLOTS), :]
            work_ref[p * NP : (p + 1) * NP, :] = total[p] * along_z
        fluid = work_ref[pl.ds(0, SLOTS, stride=NP), :]
        for c in range(1, NP):
            fluid = fluid + work_ref[pl.ds(c, SLOTS, stride=NP), :]
        where = pl.ds(pl.multiple_of((3 + f) * SLOTS, SLOTS), SLOTS)
        velocity = tp_ref[t, where, :]
        ratio = tp_ref[t, 6 * SLOTS : 7 * SLOTS, :]
        mass = tp_ref[t, 7 * SLOTS : 8 * SLOTS, :]
        drag = live_ref[t] * ratio * (fluid - velocity)
        tp_ref[t, where, :] = velocity + drag
        push_ref[...] = -(mass * drag)
        for p in range(SLOTS):
            along_z = basis_ref[t, 5, pl.ds(p, NP, stride=SLOTS), :]
            work_ref[p * NP : (p + 1) * NP, :] = push_ref[pl.ds(p, 1), :] * along_z
        for pair in range(NP // 2):
            acc = [[None] * NP for _ in range(2)]
            for p in range(SLOTS):
                base = work_ref[p * NP : (p + 1) * NP, :]
                lines = [base * basis(3, 2 * pair + i, p) for i in range(2)]
                for a in range(NP):
                    weight = basis(1, a, p)
                    for i in range(2):
                        term = lines[i] * weight
                        acc[i][a] = term if acc[i][a] is None else acc[i][a] + term
            for i in range(2):
                for a in range(NP):
                    force_ref[f, t, pl.ds(a * 64 + (2 * pair + i) * 8, 8), :] = acc[i][a]
        return carry

    lax.fori_loop(0, 3 * tiles, step, 0)

    lane = iota((NP, LANES), 1)
    for f in range(3):
        xup_ref[f] = force_ref[f, tiles - 1, 448:512, :]
        xdn_ref[f] = force_ref[f, 0, 0:64, :]
        for t in range(tiles - 1):
            summed = force_ref[f, t, 448:512, :] + force_ref[f, t + 1, 0:64, :]
            force_ref[f, t, 448:512, :] = summed
            force_ref[f, t + 1, 0:64, :] = summed
        for a in range(NP):
            first = slice(a * 64, a * 64 + 8)
            last = slice(a * 64 + 56, a * 64 + 64)
            up_line = jnp.zeros((NP, LANES), F32)
            down_line = jnp.zeros((NP, LANES), F32)
            for t in range(tiles):
                upper = force_ref[f, t, last, :]
                lower = force_ref[f, t, first, :]
                take = lane // BZ == t
                up_line = jnp.where(take, pltpu.roll(upper, (16 * t + 16) % LANES, 1), up_line)
                down_line = jnp.where(take, pltpu.roll(lower, (16 * t) % LANES, 1) if t else lower, down_line)
                force_ref[f, t, first, :] = lower + jnp.where(lane >= BZ, pltpu.roll(upper, BZ, 1), 0.0)
                force_ref[f, t, last, :] = upper + jnp.where(
                    lane < LANES - BZ, pltpu.roll(lower, LANES - BZ, 1), 0.0
                )
            yup_ref[f, a * 8 : a * 8 + 8, :] = up_line
            ydn_ref[f, a * 8 : a * 8 + 8, :] = down_line
        bz = iota((64, LANES), 1) % BZ
        for t in range(tiles):
            lower = force_ref[f, t, pl.ds(0, 64, stride=NP), :]
            upper = force_ref[f, t, pl.ds(NP - 1, 64, stride=NP), :]
            force_ref[f, t, pl.ds(0, 64, stride=NP), :] = lower + jnp.where(
                bz > 0, pltpu.roll(upper, 1, 1), 0.0
            )
            force_ref[f, t, pl.ds(NP - 1, 64, stride=NP), :] = upper + jnp.where(
                bz < BZ - 1, pltpu.roll(lower, LANES - 1, 1), 0.0
            )
            z_ref[f, t] = t_ref[f, t] + 0.5 * force_ref[f, t]
    for t in range(tiles):
        part_out_ref[t * LANES : (t + 1) * LANES, :] = tp_ref[t].T


def edge_kernel(below_ref, above_ref, yup_ref, ydn_ref, up_ref, down_ref):
    lane = iota((NP, LANES), 1)
    first = lane < BZ
    last = (lane >= 3 * BZ) & (lane < 4 * BZ)
    for f in range(3):
        up_ref[f] = yup_ref[f]
        down_ref[f] = ydn_ref[f]
        up_ref[f, 0:8, :] += jnp.where(first, pltpu.roll(below_ref[f, 56:64, :], BZ, 1), 0.0)
        up_ref[f, 56:64, :] += jnp.where(last, pltpu.roll(above_ref[f, 56:64, :], 4 * BZ, 1), 0.0)
        down_ref[f, 0:8, :] += jnp.where(first, below_ref[f, 0:8, :], 0.0)
        down_ref[f, 56:64, :] += jnp.where(last, pltpu.roll(above_ref[f, 0:8, :], 3 * BZ, 1), 0.0)


def face_delta(face):
    lane = iota((NP, LANES), 1)
    upper = face[56:64]
    lower = face[0:8]
    new_lower = lower + jnp.where(lane >= BZ, pltpu.roll(upper, BZ, 1), 0.0)
    new_upper = upper + jnp.where(lane < LANES - BZ, pltpu.roll(lower, LANES - BZ, 1), 0.0)
    return shift_z(0.5 * jnp.concatenate([new_lower, face[8:56], new_upper], axis=0))


def finish_kernel(z_ref, xb_ref, xa_ref, yb_ref, ya_ref, out_ref, zs_ref):
    tiles = EL // LANES
    zs_ref[...] = z_ref[0]
    zs_ref[0, 0:64, :] += face_delta(xb_ref[0])
    zs_ref[tiles - 1, 448:512, :] += face_delta(xa_ref[0])
    lane = iota((64, LANES), 1)
    for t in range(tiles):
        moved = pltpu.roll(yb_ref[0], LANES - BZ * t, 1) if t else yb_ref[0]
        below = shift_z(0.5 * jnp.where(lane < BZ, moved, 0.0))
        moved = pltpu.roll(ya_ref[0], LANES - BZ - BZ * t, 1)
        above = shift_z(0.5 * jnp.where(lane >= LANES - BZ, moved, 0.0))
        for a in range(NP):
            zs_ref[t, a * 64 : a * 64 + 8, :] += below[a * 8 : a * 8 + 8]
            zs_ref[t, a * 64 + 56 : a * 64 + 64, :] += above[a * 8 : a * 8 + 8]
        out_ref[0, t * LANES : (t + 1) * LANES, :] = zs_ref[t].T


def passed_along(x, axis, by):
    size = lax.axis_size(axis)
    pairs = [(i, i + by) for i in range(size) if 0 <= i + by < size]
    return lax.ppermute(x, axis, pairs)


def whole(n):
    return [pl.BlockSpec(memory_space=pltpu.VMEM)] * n


def params():
    return pltpu.CompilerParams(vmem_limit_bytes=VMEM_LIMIT)


def body(fields, particles, counts, new_place):
    devices = lax.axis_size(AXES)
    rank = lax.axis_index(AXES).astype(jnp.int32).reshape(1)
    fields = jnp.transpose(fields, (1, 0, 2))
    place = new_place.reshape(1, EL)
    counts = counts.reshape(1, EL)
    smem = [pl.BlockSpec(memory_space=pltpu.SMEM)]
    rows = HEAD + 3 * COMP
    struct = jax.ShapeDtypeStruct
    send = pl.pallas_call(
        pack_kernel,
        out_shape=struct((devices, rows, LANES), F32),
        in_specs=smem + whole(4),
        out_specs=whole(1)[0],
        compiler_params=params(),
        name="pack",
    )(rank, place, counts, fields, particles)
    recv = lax.all_to_all(send, AXES, split_axis=0, concat_axis=0, tiled=True)
    tiles = EL // LANES
    face = struct((3, 64, LANES), F32)
    z, xup, xdn, yup, ydn, particles_next = pl.pallas_call(
        section_kernel,
        out_shape=(struct((3, tiles, NODES, LANES), F32), face, face, face, face, struct((EL, PARTS), F32)),
        in_specs=smem + whole(5),
        out_specs=tuple(whole(6)),
        scratch_shapes=[
            pltpu.VMEM((EL, EL), BF16),
            pltpu.VMEM((EL, LANES), F32),
            pltpu.VMEM((tiles, LANES, LANES), F32),
            pltpu.VMEM((tiles, 6, LANES, LANES), F32),
            pltpu.VMEM((3, tiles, NODES, LANES), F32),
            pltpu.VMEM((3, tiles, NODES, LANES), F32),
            pltpu.VMEM((LANES, LANES), F32),
            pltpu.VMEM((SLOTS, LANES), F32),
            pltpu.VMEM((tiles, SLOTS, LANES), F32),
        ],
        compiler_params=params(),
        name="section",
    )(rank, place, counts, fields, particles, recv)
    below_x = passed_along(xup, "ex", 1)
    above_x = passed_along(xdn, "ex", -1)
    up, down = pl.pallas_call(
        edge_kernel,
        out_shape=(face, face),
        in_specs=whole(4),
        out_specs=tuple(whole(2)),
        compiler_params=params(),
        name="edge",
    )(below_x, above_x, yup, ydn)
    below_y = passed_along(up, "ey", 1)
    above_y = passed_along(down, "ey", -1)
    halo = pl.BlockSpec((1, 64, LANES), lambda f: (f, 0, 0))
    out = pl.pallas_call(
        finish_kernel,
        grid=(3,),
        out_shape=struct((3, EL, NODES), F32),
        in_specs=[pl.BlockSpec((1, tiles, NODES, LANES), lambda f: (f, 0, 0, 0)), halo, halo, halo, halo],
        out_specs=pl.BlockSpec((1, EL, NODES), lambda f: (f, 0, 0)),
        scratch_shapes=[pltpu.VMEM((tiles, NODES, LANES), F32)],
        compiler_params=params(),
        name="finish",
    )(z, below_x, above_x, below_y, above_y)
    return jnp.transpose(out, (1, 0, 2)), particles_next


def solution(mesh):
    return jax.shard_map(
        body,
        mesh=mesh,
        in_specs=(P(AXES, None, None), P(AXES, None), P(AXES), P(AXES)),
        out_specs=(P(AXES, None, None), P(AXES, None)),
        check_vma=False,
    )
```

```python
import functools

import jax
import jax.numpy as jnp
import numpy as np
from jax import lax
from jax.experimental import pallas as pl
from jax.experimental.pallas import tpu as pltpu
from jax.sharding import PartitionSpec as P

NP = 8
SLOTS = 16
CAP = 4
PEERS = 64
BX = 4
BY = 8
BZ = 16
NODES = NP**3
EL = BX * BY * BZ
MOVERS = PEERS * CAP
LANES = 128
PARTS = 8 * SLOTS
HEAD = 8
COMP = 16
AXES = ("ex", "ey")
POINTS = [
    -1.0,
    -0.8717401485096066,
    -0.5917001814331423,
    -0.2092992179024789,
    0.2092992179024789,
    0.5917001814331423,
    0.8717401485096066,
    1.0,
]
F32 = jnp.float32
BF16 = jnp.bfloat16
MIB = 1024 * 1024


def iota(shape, axis):
    return lax.broadcasted_iota(jnp.int32, shape, axis)


def split(x):
    high = x.astype(BF16)
    return high, (x - high.astype(F32)).astype(BF16)


def picked(onehot, x):
    high, low = split(x)
    return jnp.dot(onehot, high, preferred_element_type=F32) + jnp.dot(
        onehot, low, preferred_element_type=F32
    )


def as_column(row):
    return jnp.broadcast_to(row, (LANES, EL)).T


def pack_positions(place, rank):
    target = place // EL
    moving = target != rank
    key = jnp.where(moving, target, -1).astype(F32)
    key_col = as_column(key)
    order = []
    for j in range(EL // LANES):
        piece = key[:, j * LANES : (j + 1) * LANES]
        earlier = iota((EL, LANES), 0) < iota((EL, LANES), 1) + j * LANES
        same = (key_col == piece) & earlier
        order.append(jnp.sum(same.astype(F32), axis=0, keepdims=True))
    order = jnp.concatenate(order, axis=1).astype(jnp.int32)
    return jnp.where(moving, target * CAP + order, -1)


def interleave(first, second):
    devices = first.shape[0] // CAP
    low = iota((devices // 2, 8, LANES), 1) < CAP
    first = first.reshape(devices // 2, 8, LANES)
    second = second.reshape(devices // 2, 8, LANES)
    even = jnp.where(low, first, pltpu.roll(second, CAP, 1))
    odd = jnp.where(low, pltpu.roll(first, CAP, 1), second)
    return jnp.stack([even, odd], axis=1).reshape(devices, 8, LANES)


def deinterleave(blocks):
    devices = blocks.shape[0]
    pairs = blocks.reshape(devices // 2, 2, 8, LANES)
    even, odd = pairs[:, 0], pairs[:, 1]
    low = iota((devices // 2, 8, LANES), 1) < CAP
    first = jnp.where(low, even, pltpu.roll(odd, CAP, 1))
    second = jnp.where(low, pltpu.roll(even, CAP, 1), odd)
    return first.reshape(devices * CAP, LANES), second.reshape(devices * CAP, LANES)


def picked_row(row, onehot):
    high, low = split(jnp.broadcast_to(row.astype(F32), (8, row.shape[1])))
    dims = (((1,), (1,)), ((), ()))
    out = lax.dot_general(high, onehot, dims, preferred_element_type=F32)
    out = out + lax.dot_general(low, onehot, dims, preferred_element_type=F32)
    return out[0:1]


def interp_kernel(moves, *refs):
    rank_ref, place_ref, count_ref, fields_ref, part_ref = refs[:5]
    out_refs = refs[5:7]
    tp_ref, push_ref, basis_ref, t_ref, work_ref, count_row_ref, held_ref = refs[7:14]
    place_held, count_held, part_held, arrived = refs[14:]
    tiles = MOVERS // LANES
    pairs = [(place_ref, place_held), (count_ref, count_held), (part_ref, part_held)]
    pairs += [(fields_ref.at[f], held_ref.at[f]) for f in range(3)]
    copies = [pltpu.make_async_copy(*pair, arrived.at[i]) for i, pair in enumerate(pairs)]
    for copy in copies:
        copy.start()
    earlier = (iota((EL, EL), 0) < iota((EL, EL), 1)).astype(BF16)
    copies[0].wait()
    place = place_held[...]
    moving = place // EL != rank_ref[0]
    chosen = moving if moves else jnp.logical_not(moving)
    order = jnp.dot(
        jnp.broadcast_to(chosen.astype(F32), (8, EL)).astype(BF16),
        earlier,
        preferred_element_type=F32,
    )[0:1]
    key = jnp.where(chosen, order.astype(jnp.int32), -1)
    onehot = (iota((MOVERS, EL), 0) == key).astype(BF16)
    slot_row = picked_row(place % EL + 1, onehot)
    copies[1].wait()
    count_row_ref[...] = picked_row(count_held[...], onehot).astype(jnp.int32)
    copies[2].wait()
    records = picked(onehot, part_held[...])
    for t in range(tiles):
        tp_ref[t] = records[t * LANES : (t + 1) * LANES, :].T

    def make_basis(t, carry):
        for d in range(3):
            rows = lagrange_rows(tp_ref[t, d * SLOTS : (d + 1) * SLOTS, :])
            for n in range(NP):
                basis_ref[t, d, n * SLOTS : (n + 1) * SLOTS, :] = rows[n]
        return carry

    lax.fori_loop(0, tiles, make_basis, 0)

    def step(t, f):
        def basis(which, n, p):
            return basis_ref[t, which, pl.ds(n * SLOTS + p, 1), :]

        total = [None] * SLOTS
        for pair in range(NP // 2):
            nodes = [
                [t_ref[f, t, pl.ds(a * 64 + (2 * pair + i) * 8, 8), :] for a in range(NP)]
                for i in range(2)
            ]
            for p in range(SLOTS):
                sums = [None, None]
                for a in range(NP):
                    weight = basis(0, a, p)
                    for i in range(2):
                        term = nodes[i][a] * weight
                        sums[i] = term if sums[i] is None else sums[i] + term
                for i in range(2):
                    term = sums[i] * basis(1, 2 * pair + i, p)
                    total[p] = term if total[p] is None else total[p] + term
        for p in range(SLOTS):
            along_z = basis_ref[t, 2, pl.ds(p, NP, stride=SLOTS), :]
            work_ref[p * NP : (p + 1) * NP, :] = total[p] * along_z
        fluid = work_ref[pl.ds(0, SLOTS, stride=NP), :]
        for c in range(1, NP):
            fluid = fluid + work_ref[pl.ds(c, SLOTS, stride=NP), :]
        where = pl.ds(pl.multiple_of((3 + f) * SLOTS, SLOTS), SLOTS)
        velocity = tp_ref[t, where, :]
        ratio = tp_ref[t, 6 * SLOTS : 7 * SLOTS, :]
        mass = tp_ref[t, 7 * SLOTS : 8 * SLOTS, :]
        count = count_row_ref[:, pl.ds(pl.multiple_of(t * LANES, LANES), LANES)]
        drag = jnp.where(iota((SLOTS, LANES), 0) < count, ratio * (fluid - velocity), 0.0)
        tp_ref[t, where, :] = velocity + drag
        push_ref[t, pl.ds(pl.multiple_of((1 + f) * SLOTS, SLOTS), SLOTS), :] = -(mass * drag)
        return f

    for f in range(3):
        copies[3 + f].wait()
        rows = picked(onehot, held_ref[f])
        for t in range(tiles):
            for j in range(NODES // LANES):
                cols = slice(j * LANES, (j + 1) * LANES)
                t_ref[f, t, cols, :] = rows[t * LANES : (t + 1) * LANES, cols].T
        lax.fori_loop(0, tiles, step, f)

    heads = []
    for t in range(tiles):
        rows = slice(t * LANES, (t + 1) * LANES)
        push_ref[t, 0:SLOTS, :] = jnp.broadcast_to(slot_row[:, rows], (SLOTS, LANES))
        push_ref[t, 4 * SLOTS :, :] = jnp.zeros((LANES - 4 * SLOTS, LANES), F32)
        heads.append(jnp.concatenate([tp_ref[t].T, push_ref[t].T], axis=1))
    head = jnp.concatenate(heads, axis=0)
    if moves:
        send_ref, position_ref = out_refs
        devices = send_ref.shape[0]
        position = pack_positions(place, rank_ref[0])
        position_ref[...] = position
        goes_to = picked_row(position, onehot).astype(jnp.int32)
        scatter = (iota((devices * CAP, MOVERS), 0) == goes_to).astype(BF16)
        rows = picked(scatter, head)
        send_ref[...] = interleave(rows[:, :LANES], rows[:, LANES:])
    else:
        head_ref, slot_ref = out_refs
        head_ref[...] = head
        slot_ref[...] = slot_row.astype(jnp.int32)


def pack_kernel(position_ref, fields_ref, out_ref):
    devices = out_ref.shape[0]
    onehot = (iota((devices * CAP, EL), 0) == position_ref[...]).astype(BF16)
    for f in range(3):
        rows = picked(onehot, fields_ref[f])
        for h in range(2):
            at = COMP * f + 8 * h
            left = 2 * h * LANES
            out_ref[:, at : at + 8, :] = interleave(
                rows[:, left : left + LANES], rows[:, left + LANES : left + 2 * LANES]
            )


def lagrange_rows(coord):
    diffs = [coord - p for p in POINTS]
    left = [None] * NP
    right = [None] * NP
    for i in range(1, NP):
        left[i] = diffs[i - 1] if i == 1 else left[i - 1] * diffs[i - 1]
    for i in range(NP - 2, -1, -1):
        right[i] = diffs[i + 1] if i == NP - 2 else right[i + 1] * diffs[i + 1]
    out = []
    for i in range(NP):
        scale = 1.0
        for m in range(NP):
            if m != i:
                scale /= POINTS[i] - POINTS[m]
        if i == 0:
            term = right[0]
        elif i == NP - 1:
            term = left[i]
        else:
            term = left[i] * right[i]
        out.append(term * float(scale))
    return out


def gaussian_rows(coord):
    return [jnp.exp(-((p - coord) ** 2) * (0.5 / 0.35**2)) for p in POINTS]


def shift_z(x):
    n = x.shape[0] // NP
    x = x.reshape(n, NP, LANES)
    node = iota((n, NP, LANES), 1)
    bz = iota((n, NP, LANES), 2) % BZ
    down = pltpu.roll(pltpu.roll(x, 1, 1), 1, 2)
    up = pltpu.roll(pltpu.roll(x, NP - 1, 1), LANES - 1, 2)
    x = x + jnp.where((node == 0) & (bz > 0), down, 0.0)
    x = x + jnp.where((node == NP - 1) & (bz < BZ - 1), up, 0.0)
    return x.reshape(n * NP, LANES)


def force_kernel(
    head_ref,
    stay_slot_ref,
    recv_ref,
    force_ref,
    xup_ref,
    xdn_ref,
    yup_ref,
    ydn_ref,
    part_ref,
    slot_ref,
    tp_ref,
    push_ref,
    basis_ref,
    work_ref,
):
    tiles = EL // LANES
    particles, extra = deinterleave(recv_ref[...])
    slot_row = extra.T[0:1, :].astype(jnp.int32)
    slot_ref[...] = slot_row
    slots = jnp.concatenate([slot_row, stay_slot_ref[...]], axis=1)
    onehot = (iota((EL, EL + MOVERS), 0) + 1 == slots).astype(BF16)
    arrived = jnp.concatenate([particles, extra], axis=1)
    both = picked(onehot, jnp.concatenate([arrived, head_ref[...]], axis=0))
    record = both[:, :LANES]
    push = both[:, LANES:]
    part_ref[...] = record
    for t in range(tiles):
        rows = slice(t * LANES, (t + 1) * LANES)
        tp_ref[t] = record[rows].T
        push_ref[t] = push[rows].T

    def make_basis(t, carry):
        for d in range(3):
            rows = gaussian_rows(tp_ref[t, d * SLOTS : (d + 1) * SLOTS, :])
            for n in range(NP):
                basis_ref[t, d, n * SLOTS : (n + 1) * SLOTS, :] = rows[n]
        return carry

    lax.fori_loop(0, tiles, make_basis, 0)

    def step(index, carry):
        f = index // tiles
        t = index % tiles

        def basis(which, n, p):
            return basis_ref[t, which, pl.ds(n * SLOTS + p, 1), :]

        for p in range(SLOTS):
            along_z = basis_ref[t, 2, pl.ds(p, NP, stride=SLOTS), :]
            value = push_ref[t, pl.ds((1 + f) * SLOTS + p, 1), :]
            work_ref[p * NP : (p + 1) * NP, :] = (0.5 * value) * along_z
        for pair in range(NP // 2):
            acc = [[None] * NP for _ in range(2)]
            for p in range(SLOTS):
                base = work_ref[p * NP : (p + 1) * NP, :]
                lines = [base * basis(1, 2 * pair + i, p) for i in range(2)]
                for a in range(NP):
                    weight = basis(0, a, p)
                    for i in range(2):
                        term = lines[i] * weight
                        acc[i][a] = term if acc[i][a] is None else acc[i][a] + term
            for i in range(2):
                for a in range(NP):
                    force_ref[f, t, pl.ds(a * 64 + (2 * pair + i) * 8, 8), :] = acc[i][a]
        return carry

    lax.fori_loop(0, 3 * tiles, step, 0)

    lane = iota((NP, LANES), 1)
    bz = iota((64, LANES), 1) % BZ
    for f in range(3):
        xup_ref[f] = force_ref[f, tiles - 1, 448:512, :]
        xdn_ref[f] = force_ref[f, 0, 0:64, :]
        for t in range(tiles - 1):
            summed = force_ref[f, t, 448:512, :] + force_ref[f, t + 1, 0:64, :]
            force_ref[f, t, 448:512, :] = summed
            force_ref[f, t + 1, 0:64, :] = summed
        for a in range(NP):
            first = slice(a * 64, a * 64 + 8)
            last = slice(a * 64 + 56, a * 64 + 64)
            up_line = jnp.zeros((NP, LANES), F32)
            down_line = jnp.zeros((NP, LANES), F32)
            for t in range(tiles):
                upper = force_ref[f, t, last, :]
                lower = force_ref[f, t, first, :]
                take = lane // BZ == t
                up_line = jnp.where(take, pltpu.roll(upper, 16 * t + 16, 1), up_line)
                moved = pltpu.roll(lower, 16 * t, 1) if t else lower
                down_line = jnp.where(take, moved, down_line)
                force_ref[f, t, first, :] = lower + jnp.where(
                    lane >= BZ, pltpu.roll(upper, BZ, 1), 0.0
                )
                force_ref[f, t, last, :] = upper + jnp.where(
                    lane < LANES - BZ, pltpu.roll(lower, LANES - BZ, 1), 0.0
                )
            yup_ref[f, a * 8 : a * 8 + 8, :] = up_line
            ydn_ref[f, a * 8 : a * 8 + 8, :] = down_line
        for t in range(tiles):
            lower = force_ref[f, t, pl.ds(0, 64, stride=NP), :]
            upper = force_ref[f, t, pl.ds(NP - 1, 64, stride=NP), :]
            force_ref[f, t, pl.ds(0, 64, stride=NP), :] = lower + jnp.where(
                bz > 0, pltpu.roll(upper, 1, 1), 0.0
            )
            force_ref[f, t, pl.ds(NP - 1, 64, stride=NP), :] = upper + jnp.where(
                bz < BZ - 1, pltpu.roll(lower, LANES - 1, 1), 0.0
            )


def edge_kernel(below_ref, above_ref, yup_ref, ydn_ref, token_ref, up_ref, down_ref):
    lane = iota((NP, LANES), 1)
    first = lane < BZ
    last = (lane >= 3 * BZ) & (lane < 4 * BZ)
    for f in range(3):
        up_ref[f] = yup_ref[f]
        down_ref[f] = ydn_ref[f]
        up_ref[f, 0:8, :] += jnp.where(first, pltpu.roll(below_ref[f, 56:64, :], BZ, 1), 0.0)
        up_ref[f, 56:64, :] += jnp.where(last, pltpu.roll(above_ref[f, 56:64, :], 4 * BZ, 1), 0.0)
        down_ref[f, 0:8, :] += jnp.where(first, below_ref[f, 0:8, :], 0.0)
        down_ref[f, 56:64, :] += jnp.where(last, pltpu.roll(above_ref[f, 0:8, :], 3 * BZ, 1), 0.0)


def face_delta(face):
    lane = iota((NP, LANES), 1)
    upper = face[56:64]
    lower = face[0:8]
    new_lower = lower + jnp.where(lane >= BZ, pltpu.roll(upper, BZ, 1), 0.0)
    new_upper = upper + jnp.where(lane < LANES - BZ, pltpu.roll(lower, LANES - BZ, 1), 0.0)
    return shift_z(0.5 * jnp.concatenate([new_lower, face[8:56], new_upper], axis=0))


def face_delta(face):
    lane = iota((NP, LANES), 1)
    upper = face[56:64]
    lower = face[0:8]
    new_lower = lower + jnp.where(lane >= BZ, pltpu.roll(upper, BZ, 1), 0.0)
    new_upper = upper + jnp.where(lane < LANES - BZ, pltpu.roll(lower, LANES - BZ, 1), 0.0)
    return shift_z(jnp.concatenate([new_lower, face[8:56], new_upper], axis=0))


def base_kernel(rank_ref, place_ref, fields_ref, force_ref, out_ref, token_ref):
    tiles = EL // LANES
    stay_col = as_column((place_ref[...] // EL == rank_ref[0]).astype(F32)) > 0
    for f in range(3):
        for t in range(tiles):
            rows = slice(t * LANES, (t + 1) * LANES)
            for j in range(NODES // LANES):
                cols = slice(j * LANES, (j + 1) * LANES)
                own = jnp.where(stay_col[rows], fields_ref[f, rows, cols], 0.0)
                out_ref[f, rows, cols] = own + force_ref[f, t, cols, :].T
    token_ref[...] = jnp.zeros((8, LANES), F32)


def place_kernel(
    slot_ref,
    recv_ref,
    base_ref,
    xb_ref,
    xa_ref,
    out_ref,
    ends_ref,
    recv_held,
    held_ref,
    arrived,
    left,
):
    devices = recv_ref.shape[0]
    tiles = EL // LANES
    loads = []
    for f in range(3):
        part = (pl.ds(0, devices), pl.ds(COMP * f, COMP))
        loads.append(
            (
                pltpu.make_async_copy(recv_ref.at[part], recv_held.at[f], arrived.at[f, 0]),
                pltpu.make_async_copy(base_ref.at[f], held_ref.at[f], arrived.at[f, 1]),
            )
        )
        for load in loads[f]:
            load.start()
    onehot = (iota((EL, EL), 0) + 1 == slot_ref[...]).astype(BF16)
    blank = jnp.zeros((64, LANES), F32)
    copies = []
    for f in range(3):
        loads[f][0].wait()
        pieces = []
        for h in range(2):
            pieces += list(deinterleave(recv_held[f, :, 8 * h : 8 * h + 8, :]))
        rows = picked(onehot, jnp.concatenate(pieces, axis=1))
        loads[f][1].wait()
        held_ref[f] += rows
        delta = jnp.concatenate([face_delta(xb_ref[f]), blank], axis=0)
        held_ref[f, 0:LANES, 0:LANES] += delta.T
        delta = jnp.concatenate([blank, face_delta(xa_ref[f])], axis=0)
        held_ref[f, EL - LANES :, NODES - LANES :] += delta.T
        for t in range(tiles):
            inner = pl.ds(t * LANES + BZ, LANES - 2 * BZ)
            copies.append(
                pltpu.make_async_copy(held_ref.at[f, inner], out_ref.at[f, inner], left.at[f, t])
            )
            copies[-1].start()
            ends_ref[f, 0, t * BZ : (t + 1) * BZ, :] = held_ref[f, t * LANES : t * LANES + BZ, :]
            last = (t + 1) * LANES
            ends_ref[f, 1, t * BZ : (t + 1) * BZ, :] = held_ref[f, last - BZ : last, :]
    for copy in copies:
        copy.wait()


def lines_kernel(ends_ref, yb_ref, ya_ref, inner_ref, out_ref, line_ref, held_ref, left):
    tiles = EL // LANES
    lane = iota((64, LANES), 1)
    line_ref[...] = jnp.zeros((NODES, LANES), F32)
    copies = []
    for f in range(3):
        low = shift_z(jnp.where(lane < tiles * BZ, yb_ref[f], 0.0))
        high = shift_z(jnp.where(lane < tiles * BZ, ya_ref[f], 0.0))
        high = pltpu.roll(high, LANES // 2, 1)
        for a in range(NP):
            line_ref[a * 64 : a * 64 + 8, :] = low[a * 8 : a * 8 + 8]
            line_ref[a * 64 + 56 : a * 64 + 64, :] = high[a * 8 : a * 8 + 8]
        for j in range(NODES // LANES):
            cols = slice(j * LANES, (j + 1) * LANES)
            lines = line_ref[cols, :].T
            held_ref[f, 0, :, cols] = ends_ref[f, 0, :, cols] + lines[:64]
            held_ref[f, 1, :, cols] = ends_ref[f, 1, :, cols] + lines[64:]
        for side in range(2):
            for t in range(tiles):
                at = pl.ds(t * LANES + side * (LANES - BZ), BZ)
                copies.append(
                    pltpu.make_async_copy(
                        held_ref.at[f, side, pl.ds(t * BZ, BZ)],
                        out_ref.at[f, at],
                        left.at[f, side, t],
                    )
                )
                copies[-1].start()
    for copy in copies:
        copy.wait()


def passed_along(x, along_ex, along_ey):
    rows, cols = lax.axis_size("ex"), lax.axis_size("ey")
    pairs = []
    for i in range(rows):
        for j in range(cols):
            to_i, to_j = i + along_ex, j + along_ey
            if 0 <= to_i < rows and 0 <= to_j < cols:
                pairs.append((i * cols + j, to_i * cols + to_j))
    return lax.ppermute(x, AXES, pairs)


def whole(n):
    return [pl.BlockSpec(memory_space=pltpu.VMEM)] * n


def params(mib):
    return pltpu.CompilerParams(vmem_limit_bytes=mib * MIB)


def cost(micros):
    return pl.CostEstimate(flops=0, bytes_accessed=int(micros * 3_000_000), transcendentals=0)


def body(fields, particles, counts, new_place):
    devices = lax.axis_size(AXES)
    rank = lax.axis_index(AXES).astype(jnp.int32).reshape(1)
    fields = jnp.transpose(fields, (1, 0, 2))
    place = new_place.reshape(1, EL)
    counts = counts.reshape(1, EL)
    smem = [pl.BlockSpec(memory_space=pltpu.SMEM)]
    anywhere = pl.BlockSpec(memory_space=pl.ANY)
    in_hbm = pl.BlockSpec(memory_space=pltpu.HBM)
    struct = jax.ShapeDtypeStruct
    tiles = EL // LANES
    tile_scratch = pltpu.VMEM((tiles, LANES, LANES), F32)
    basis_scratch = pltpu.VMEM((tiles, 3, LANES, LANES), F32)
    work_scratch = pltpu.VMEM((LANES, LANES), F32)
    half = MOVERS // LANES

    def interp(moves, out_shape, mib, name):
        return pl.pallas_call(
            functools.partial(interp_kernel, moves),
            out_shape=out_shape,
            in_specs=smem + [anywhere] * 4,
            out_specs=tuple(whole(2)),
            scratch_shapes=[
                pltpu.VMEM((half, LANES, LANES), F32),
                pltpu.VMEM((half, LANES, LANES), F32),
                pltpu.VMEM((half, 3, LANES, LANES), F32),
                pltpu.VMEM((3, half, NODES, LANES), F32),
                work_scratch,
                pltpu.VMEM((1, MOVERS), jnp.int32),
                pltpu.VMEM((3, EL, NODES), F32),
                pltpu.VMEM((1, EL), jnp.int32),
                pltpu.VMEM((1, EL), jnp.int32),
                pltpu.VMEM((EL, PARTS), F32),
                pltpu.SemaphoreType.DMA((6,)),
            ],
            compiler_params=params(mib),
            cost_estimate=cost(6),
            name=name,
        )(rank, place, counts, fields, particles)

    send_head, position = interp(
        True, (struct((devices, HEAD, LANES), F32), struct((1, EL), jnp.int32)), 58, "moving"
    )
    head, stay_slots = interp(
        False, (struct((MOVERS, 2 * LANES), F32), struct((1, MOVERS), jnp.int32)), 40, "staying"
    )
    recv_head = lax.all_to_all(send_head, AXES, split_axis=0, concat_axis=0, tiled=True)
    send = pl.pallas_call(
        pack_kernel,
        out_shape=struct((devices, 3 * COMP, LANES), F32),
        in_specs=whole(2),
        out_specs=whole(1)[0],
        compiler_params=params(58),
        cost_estimate=cost(5),
        name="pack",
    )(position, fields)
    recv = lax.all_to_all(send, AXES, split_axis=0, concat_axis=0, tiled=True)
    face = struct((3, 64, LANES), F32)
    force, xup, xdn, yup, ydn, particles_next, slots = pl.pallas_call(
        force_kernel,
        out_shape=(
            struct((3, tiles, NODES, LANES), F32),
            face,
            face,
            face,
            face,
            struct((EL, PARTS), F32),
            struct((1, EL), jnp.int32),
        ),
        in_specs=whole(3),
        out_specs=tuple(whole(7)),
        scratch_shapes=[tile_scratch, tile_scratch, basis_scratch, work_scratch],
        compiler_params=params(40),
        cost_estimate=cost(8),
        name="force",
    )(head, stay_slots, recv_head)
    base, token = pl.pallas_call(
        base_kernel,
        out_shape=(pltpu.HBM((3, EL, NODES), F32), struct((8, LANES), F32)),
        in_specs=smem + whole(3),
        out_specs=tuple(whole(2)),
        compiler_params=params(20),
        cost_estimate=cost(5),
        name="base",
    )(rank, place, fields, force)
    below_x = passed_along(xup, 1, 0)
    above_x = passed_along(xdn, -1, 0)
    up, down = pl.pallas_call(
        edge_kernel,
        out_shape=(face, face),
        in_specs=whole(5),
        out_specs=tuple(whole(2)),
        compiler_params=params(8),
        cost_estimate=cost(1),
        name="edge",
    )(below_x, above_x, yup, ydn, token)
    below_y = passed_along(up, 0, 1)
    above_y = passed_along(down, 0, -1)
    ends = (3, 2, tiles * BZ, NODES)
    inner, ends_out = pl.pallas_call(
        place_kernel,
        out_shape=(struct((3, EL, NODES), F32), struct(ends, F32)),
        in_specs=whole(1) + [in_hbm, in_hbm] + whole(2),
        out_specs=(in_hbm, whole(1)[0]),
        scratch_shapes=[
            pltpu.VMEM((3, devices, COMP, LANES), F32),
            pltpu.VMEM((3, EL, NODES), F32),
            pltpu.SemaphoreType.DMA((3, 2)),
            pltpu.SemaphoreType.DMA((3, tiles)),
        ],
        compiler_params=params(20),
        cost_estimate=cost(3),
        name="place",
    )(slots, recv, pltpu.with_memory_space_constraint(base, pltpu.HBM), below_x, above_x)
    out = pl.pallas_call(
        lines_kernel,
        out_shape=struct((3, EL, NODES), F32),
        in_specs=whole(3) + [anywhere],
        out_specs=anywhere,
        scratch_shapes=[
            pltpu.VMEM((NODES, LANES), F32),
            pltpu.VMEM(ends, F32),
            pltpu.SemaphoreType.DMA((3, 2, tiles)),
        ],
        input_output_aliases={3: 0},
        compiler_params=params(10),
        cost_estimate=cost(1),
        name="lines",
    )(ends_out, below_y, above_y, inner)
    return jnp.transpose(out, (1, 0, 2)), particles_next


def solution(mesh):
    return jax.shard_map(
        body,
        mesh=mesh,
        in_specs=(P(AXES, None, None), P(AXES, None), P(AXES), P(AXES)),
        out_specs=(P(AXES, None, None), P(AXES, None)),
        check_vma=False,
    )
```

```python
import functools

import jax
import jax.numpy as jnp
import numpy as np
from jax import lax
from jax.experimental import pallas as pl
from jax.experimental.pallas import tpu as pltpu
from jax.sharding import PartitionSpec as P

NP = 8
SLOTS = 16
CAP = 4
PEERS = 64
BX = 4
BY = 8
BZ = 16
NODES = NP**3
EL = BX * BY * BZ
MOVERS = PEERS * CAP
LANES = 128
PARTS = 8 * SLOTS
HEAD = 6
COMP = 16
AXES = ("ex", "ey")
POINTS = [
    -1.0,
    -0.8717401485096066,
    -0.5917001814331423,
    -0.2092992179024789,
    0.2092992179024789,
    0.5917001814331423,
    0.8717401485096066,
    1.0,
]
F32 = jnp.float32
BF16 = jnp.bfloat16
MIB = 1024 * 1024


def iota(shape, axis):
    return lax.broadcasted_iota(jnp.int32, shape, axis)


def split(x):
    high = x.astype(BF16)
    return high, (x - high.astype(F32)).astype(BF16)


def picked(onehot, x):
    high, low = split(x)
    return jnp.dot(onehot, high, preferred_element_type=F32) + jnp.dot(
        onehot, low, preferred_element_type=F32
    )


def as_column(row):
    return jnp.broadcast_to(row, (LANES, EL)).T


def pack_positions(place, rank):
    target = place // EL
    moving = target != rank
    key = jnp.where(moving, target, -1).astype(F32)
    key_col = as_column(key)
    order = []
    for j in range(EL // LANES):
        piece = key[:, j * LANES : (j + 1) * LANES]
        earlier = iota((EL, LANES), 0) < iota((EL, LANES), 1) + j * LANES
        same = (key_col == piece) & earlier
        order.append(jnp.sum(same.astype(F32), axis=0, keepdims=True))
    order = jnp.concatenate(order, axis=1).astype(jnp.int32)
    return jnp.where(moving, target * CAP + order, -1)


def interleave(first, second):
    devices = first.shape[0] // CAP
    low = iota((devices // 2, 8, LANES), 1) < CAP
    first = first.reshape(devices // 2, 8, LANES)
    second = second.reshape(devices // 2, 8, LANES)
    even = jnp.where(low, first, pltpu.roll(second, CAP, 1))
    odd = jnp.where(low, pltpu.roll(first, CAP, 1), second)
    return jnp.stack([even, odd], axis=1).reshape(devices, 8, LANES)


def deinterleave(blocks):
    devices = blocks.shape[0]
    pairs = blocks.reshape(devices // 2, 2, 8, LANES)
    even, odd = pairs[:, 0], pairs[:, 1]
    low = iota((devices // 2, 8, LANES), 1) < CAP
    first = jnp.where(low, even, pltpu.roll(odd, CAP, 1))
    second = jnp.where(low, pltpu.roll(even, CAP, 1), odd)
    return first.reshape(devices * CAP, LANES), second.reshape(devices * CAP, LANES)


def picked_row(row, onehot):
    high, low = split(jnp.broadcast_to(row.astype(F32), (8, row.shape[1])))
    dims = (((1,), (1,)), ((), ()))
    out = lax.dot_general(high, onehot, dims, preferred_element_type=F32)
    out = out + lax.dot_general(low, onehot, dims, preferred_element_type=F32)
    return out[0:1]


def interp_kernel(moves, *refs):
    rank_ref, place_ref, count_ref, fields_ref, part_ref = refs[:5]
    out_refs = refs[5:7]
    tp_ref, push_ref, basis_ref, t_ref, work_ref, count_row_ref, held_ref = refs[7:14]
    place_held, count_held, part_held, arrived = refs[14:]
    tiles = MOVERS // LANES
    pairs = [(place_ref, place_held), (count_ref, count_held), (part_ref, part_held)]
    pairs += [(fields_ref.at[f], held_ref.at[f]) for f in range(3)]
    copies = [pltpu.make_async_copy(*pair, arrived.at[i]) for i, pair in enumerate(pairs)]
    for copy in copies:
        copy.start()
    earlier = (iota((EL, EL), 0) < iota((EL, EL), 1)).astype(BF16)
    copies[0].wait()
    place = place_held[...]
    moving = place // EL != rank_ref[0]
    chosen = moving if moves else jnp.logical_not(moving)
    order = jnp.dot(
        jnp.broadcast_to(chosen.astype(F32), (8, EL)).astype(BF16),
        earlier,
        preferred_element_type=F32,
    )[0:1]
    key = jnp.where(chosen, order.astype(jnp.int32), -1)
    onehot = (iota((MOVERS, EL), 0) == key).astype(BF16)
    slot_row = picked_row(place % EL + 1, onehot)
    copies[1].wait()
    count_row_ref[...] = picked_row(count_held[...], onehot).astype(jnp.int32)
    copies[2].wait()
    records = picked(onehot, part_held[...])
    for t in range(tiles):
        tp_ref[t] = records[t * LANES : (t + 1) * LANES, :].T

    def make_basis(t, carry):
        for d in range(3):
            rows = lagrange_rows(tp_ref[t, d * SLOTS : (d + 1) * SLOTS, :])
            for n in range(NP):
                basis_ref[t, d, n * SLOTS : (n + 1) * SLOTS, :] = rows[n]
        return carry

    lax.fori_loop(0, tiles, make_basis, 0)

    def step(t, f):
        def basis(which, n, p):
            return basis_ref[t, which, pl.ds(n * SLOTS + p, 1), :]

        total = [None] * SLOTS
        for pair in range(NP // 2):
            nodes = [
                [t_ref[f, t, pl.ds(a * 64 + (2 * pair + i) * 8, 8), :] for a in range(NP)]
                for i in range(2)
            ]
            for p in range(SLOTS):
                sums = [None, None]
                for a in range(NP):
                    weight = basis(0, a, p)
                    for i in range(2):
                        term = nodes[i][a] * weight
                        sums[i] = term if sums[i] is None else sums[i] + term
                for i in range(2):
                    term = sums[i] * basis(1, 2 * pair + i, p)
                    total[p] = term if total[p] is None else total[p] + term
        for p in range(SLOTS):
            along_z = basis_ref[t, 2, pl.ds(p, NP, stride=SLOTS), :]
            work_ref[p * NP : (p + 1) * NP, :] = total[p] * along_z
        fluid = work_ref[pl.ds(0, SLOTS, stride=NP), :]
        for c in range(1, NP):
            fluid = fluid + work_ref[pl.ds(c, SLOTS, stride=NP), :]
        where = pl.ds(pl.multiple_of((3 + f) * SLOTS, SLOTS), SLOTS)
        velocity = tp_ref[t, where, :]
        ratio = tp_ref[t, 6 * SLOTS : 7 * SLOTS, :]
        mass = tp_ref[t, 7 * SLOTS : 8 * SLOTS, :]
        count = count_row_ref[:, pl.ds(pl.multiple_of(t * LANES, LANES), LANES)]
        drag = jnp.where(iota((SLOTS, LANES), 0) < count, ratio * (fluid - velocity), 0.0)
        tp_ref[t, where, :] = velocity + drag
        push_ref[t, pl.ds(pl.multiple_of((1 + f) * SLOTS, SLOTS), SLOTS), :] = -(mass * drag)
        return f

    for f in range(3):
        copies[3 + f].wait()
        rows = picked(onehot, held_ref[f])
        for t in range(tiles):
            for j in range(NODES // LANES):
                cols = slice(j * LANES, (j + 1) * LANES)
                t_ref[f, t, cols, :] = rows[t * LANES : (t + 1) * LANES, cols].T
        lax.fori_loop(0, tiles, step, f)

    heads = []
    for t in range(tiles):
        rows = slice(t * LANES, (t + 1) * LANES)
        push_ref[t, 0:SLOTS, :] = jnp.broadcast_to(slot_row[:, rows], (SLOTS, LANES))
        push_ref[t, 4 * SLOTS :, :] = jnp.zeros((LANES - 4 * SLOTS, LANES), F32)
        heads.append(jnp.concatenate([tp_ref[t].T, push_ref[t].T], axis=1))
    head = jnp.concatenate(heads, axis=0)
    if moves:
        send_ref, position_ref = out_refs
        devices = send_ref.shape[0] // HEAD
        position = pack_positions(place, rank_ref[0])
        position_ref[...] = position
        goes_to = picked_row(position, onehot).astype(jnp.int32)
        goes_to = goes_to % CAP * devices + goes_to // CAP
        scatter = (iota((devices * CAP, MOVERS), 0) == goes_to).astype(BF16)
        rows = picked(scatter, head)
        lane = iota((devices, LANES), 1)
        for q in range(CAP):
            mine = slice(q * devices, (q + 1) * devices)
            send_ref[pl.ds(q, devices, stride=HEAD), :] = rows[mine, :LANES]
            if q % 2:
                both = jnp.where(lane < LANES // 2, before, pltpu.roll(rows[mine, LANES:], LANES // 2, 1))
                send_ref[pl.ds(CAP + q // 2, devices, stride=HEAD), :] = both
            before = rows[mine, LANES:]
    else:
        head_ref, slot_ref = out_refs
        head_ref[...] = head
        slot_ref[...] = slot_row.astype(jnp.int32)


def pack_kernel(position_ref, fields_ref, out_ref):
    devices = out_ref.shape[0]
    onehot = (iota((devices * CAP, EL), 0) == position_ref[...]).astype(BF16)
    for f in range(3):
        rows = picked(onehot, fields_ref[f])
        for h in range(2):
            at = COMP * f + 8 * h
            left = 2 * h * LANES
            out_ref[:, at : at + 8, :] = interleave(
                rows[:, left : left + LANES], rows[:, left + LANES : left + 2 * LANES]
            )


def lagrange_rows(coord):
    diffs = [coord - p for p in POINTS]
    left = [None] * NP
    right = [None] * NP
    for i in range(1, NP):
        left[i] = diffs[i - 1] if i == 1 else left[i - 1] * diffs[i - 1]
    for i in range(NP - 2, -1, -1):
        right[i] = diffs[i + 1] if i == NP - 2 else right[i + 1] * diffs[i + 1]
    out = []
    for i in range(NP):
        scale = 1.0
        for m in range(NP):
            if m != i:
                scale /= POINTS[i] - POINTS[m]
        if i == 0:
            term = right[0]
        elif i == NP - 1:
            term = left[i]
        else:
            term = left[i] * right[i]
        out.append(term * float(scale))
    return out


def gaussian_rows(coord):
    return [jnp.exp(-((p - coord) ** 2) * (0.5 / 0.35**2)) for p in POINTS]


def shift_z(x):
    n = x.shape[0] // NP
    x = x.reshape(n, NP, LANES)
    node = iota((n, NP, LANES), 1)
    bz = iota((n, NP, LANES), 2) % BZ
    down = pltpu.roll(pltpu.roll(x, 1, 1), 1, 2)
    up = pltpu.roll(pltpu.roll(x, NP - 1, 1), LANES - 1, 2)
    x = x + jnp.where((node == 0) & (bz > 0), down, 0.0)
    x = x + jnp.where((node == NP - 1) & (bz < BZ - 1), up, 0.0)
    return x.reshape(n * NP, LANES)


def force_kernel(
    head_ref,
    stay_slot_ref,
    recv_ref,
    force_ref,
    xup_ref,
    xdn_ref,
    yup_ref,
    ydn_ref,
    part_ref,
    slot_ref,
    tp_ref,
    push_ref,
    basis_ref,
    work_ref,
):
    tiles = EL // LANES
    devices = recv_ref.shape[0] // HEAD
    particles, extra = [], []
    for q in range(CAP):
        particles.append(recv_ref[pl.ds(q, devices, stride=HEAD), :])
        both = recv_ref[pl.ds(CAP + q // 2, devices, stride=HEAD), :]
        extra.append(pltpu.roll(both, LANES // 2, 1) if q % 2 else both)
    particles = jnp.concatenate(particles, axis=0)
    extra = jnp.concatenate(extra, axis=0)
    slot_row = extra.T[0:1, :].astype(jnp.int32)
    at = iota((devices * CAP, devices * CAP), 0)
    turned = at // devices + at % devices * CAP == iota((devices * CAP, devices * CAP), 1)
    high, low = split(jnp.broadcast_to(slot_row.astype(F32), (8, devices * CAP)))
    order = turned.astype(BF16)
    row = jnp.dot(high, order, preferred_element_type=F32)
    row = row + jnp.dot(low, order, preferred_element_type=F32)
    slot_ref[...] = row[0:1].astype(jnp.int32)
    slots = jnp.concatenate([slot_row, stay_slot_ref[...]], axis=1)
    onehot = (iota((EL, EL + MOVERS), 0) + 1 == slots).astype(BF16)
    arrived = jnp.concatenate([particles, extra], axis=1)
    both = picked(onehot, jnp.concatenate([arrived, head_ref[...]], axis=0))
    record = both[:, :LANES]
    push = both[:, LANES:]
    part_ref[...] = record
    for t in range(tiles):
        rows = slice(t * LANES, (t + 1) * LANES)
        tp_ref[t] = record[rows].T
        push_ref[t] = push[rows].T

    def make_basis(t, carry):
        for d in range(3):
            rows = gaussian_rows(tp_ref[t, d * SLOTS : (d + 1) * SLOTS, :])
            for n in range(NP):
                basis_ref[t, d, n * SLOTS : (n + 1) * SLOTS, :] = rows[n]
        return carry

    lax.fori_loop(0, tiles, make_basis, 0)

    def step(index, carry):
        f = index // tiles
        t = index % tiles

        def basis(which, n, p):
            return basis_ref[t, which, pl.ds(n * SLOTS + p, 1), :]

        for p in range(SLOTS):
            along_z = basis_ref[t, 2, pl.ds(p, NP, stride=SLOTS), :]
            value = push_ref[t, pl.ds((1 + f) * SLOTS + p, 1), :]
            work_ref[p * NP : (p + 1) * NP, :] = (0.5 * value) * along_z
        for pair in range(NP // 2):
            acc = [[None] * NP for _ in range(2)]
            for p in range(SLOTS):
                base = work_ref[p * NP : (p + 1) * NP, :]
                lines = [base * basis(1, 2 * pair + i, p) for i in range(2)]
                for a in range(NP):
                    weight = basis(0, a, p)
                    for i in range(2):
                        term = lines[i] * weight
                        acc[i][a] = term if acc[i][a] is None else acc[i][a] + term
            for i in range(2):
                for a in range(NP):
                    force_ref[f, t, pl.ds(a * 64 + (2 * pair + i) * 8, 8), :] = acc[i][a]
        return carry

    lax.fori_loop(0, 3 * tiles, step, 0)

    lane = iota((NP, LANES), 1)
    bz = iota((64, LANES), 1) % BZ
    for f in range(3):
        xup_ref[f] = force_ref[f, tiles - 1, 448:512, :]
        xdn_ref[f] = force_ref[f, 0, 0:64, :]
        for t in range(tiles - 1):
            summed = force_ref[f, t, 448:512, :] + force_ref[f, t + 1, 0:64, :]
            force_ref[f, t, 448:512, :] = summed
            force_ref[f, t + 1, 0:64, :] = summed
        for a in range(NP):
            first = slice(a * 64, a * 64 + 8)
            last = slice(a * 64 + 56, a * 64 + 64)
            up_line = jnp.zeros((NP, LANES), F32)
            down_line = jnp.zeros((NP, LANES), F32)
            for t in range(tiles):
                upper = force_ref[f, t, last, :]
                lower = force_ref[f, t, first, :]
                take = lane // BZ == t
                up_line = jnp.where(take, pltpu.roll(upper, 16 * t + 16, 1), up_line)
                moved = pltpu.roll(lower, 16 * t, 1) if t else lower
                down_line = jnp.where(take, moved, down_line)
                force_ref[f, t, first, :] = lower + jnp.where(
                    lane >= BZ, pltpu.roll(upper, BZ, 1), 0.0
                )
                force_ref[f, t, last, :] = upper + jnp.where(
                    lane < LANES - BZ, pltpu.roll(lower, LANES - BZ, 1), 0.0
                )
            yup_ref[f, a * 8 : a * 8 + 8, :] = up_line
            ydn_ref[f, a * 8 : a * 8 + 8, :] = down_line
        for t in range(tiles):
            lower = force_ref[f, t, pl.ds(0, 64, stride=NP), :]
            upper = force_ref[f, t, pl.ds(NP - 1, 64, stride=NP), :]
            force_ref[f, t, pl.ds(0, 64, stride=NP), :] = lower + jnp.where(
                bz > 0, pltpu.roll(upper, 1, 1), 0.0
            )
            force_ref[f, t, pl.ds(NP - 1, 64, stride=NP), :] = upper + jnp.where(
                bz < BZ - 1, pltpu.roll(lower, LANES - 1, 1), 0.0
            )


def edge_kernel(below_ref, above_ref, yup_ref, ydn_ref, token_ref, up_ref, down_ref):
    lane = iota((NP, LANES), 1)
    first = lane < BZ
    last = (lane >= 3 * BZ) & (lane < 4 * BZ)
    for f in range(3):
        up_ref[f] = yup_ref[f]
        down_ref[f] = ydn_ref[f]
        up_ref[f, 0:8, :] += jnp.where(first, pltpu.roll(below_ref[f, 56:64, :], BZ, 1), 0.0)
        up_ref[f, 56:64, :] += jnp.where(last, pltpu.roll(above_ref[f, 56:64, :], 4 * BZ, 1), 0.0)
        down_ref[f, 0:8, :] += jnp.where(first, below_ref[f, 0:8, :], 0.0)
        down_ref[f, 56:64, :] += jnp.where(last, pltpu.roll(above_ref[f, 0:8, :], 3 * BZ, 1), 0.0)


def face_delta(face):
    lane = iota((NP, LANES), 1)
    upper = face[56:64]
    lower = face[0:8]
    new_lower = lower + jnp.where(lane >= BZ, pltpu.roll(upper, BZ, 1), 0.0)
    new_upper = upper + jnp.where(lane < LANES - BZ, pltpu.roll(lower, LANES - BZ, 1), 0.0)
    return shift_z(0.5 * jnp.concatenate([new_lower, face[8:56], new_upper], axis=0))


def face_delta(face):
    lane = iota((NP, LANES), 1)
    upper = face[56:64]
    lower = face[0:8]
    new_lower = lower + jnp.where(lane >= BZ, pltpu.roll(upper, BZ, 1), 0.0)
    new_upper = upper + jnp.where(lane < LANES - BZ, pltpu.roll(lower, LANES - BZ, 1), 0.0)
    return shift_z(jnp.concatenate([new_lower, face[8:56], new_upper], axis=0))


def base_kernel(rank_ref, place_ref, fields_ref, force_ref, out_ref, token_ref):
    tiles = EL // LANES
    stay_col = as_column((place_ref[...] // EL == rank_ref[0]).astype(F32)) > 0
    for f in range(3):
        for t in range(tiles):
            rows = slice(t * LANES, (t + 1) * LANES)
            for j in range(NODES // LANES):
                cols = slice(j * LANES, (j + 1) * LANES)
                own = jnp.where(stay_col[rows], fields_ref[f, rows, cols], 0.0)
                out_ref[f, rows, cols] = own + force_ref[f, t, cols, :].T
    token_ref[...] = jnp.zeros((8, LANES), F32)


def place_kernel(
    slot_ref,
    recv_ref,
    base_ref,
    xb_ref,
    xa_ref,
    out_ref,
    ends_ref,
    recv_held,
    held_ref,
    arrived,
    left,
):
    devices = recv_ref.shape[0]
    tiles = EL // LANES
    loads = []
    for f in range(3):
        part = (pl.ds(0, devices), pl.ds(COMP * f, COMP))
        loads.append(
            (
                pltpu.make_async_copy(recv_ref.at[part], recv_held.at[f], arrived.at[f, 0]),
                pltpu.make_async_copy(base_ref.at[f], held_ref.at[f], arrived.at[f, 1]),
            )
        )
        for load in loads[f]:
            load.start()
    onehot = (iota((EL, EL), 0) + 1 == slot_ref[...]).astype(BF16)
    blank = jnp.zeros((64, LANES), F32)
    copies = []
    for f in range(3):
        loads[f][0].wait()
        pieces = []
        for h in range(2):
            pieces += list(deinterleave(recv_held[f, :, 8 * h : 8 * h + 8, :]))
        rows = picked(onehot, jnp.concatenate(pieces, axis=1))
        loads[f][1].wait()
        held_ref[f] += rows
        delta = jnp.concatenate([face_delta(xb_ref[f]), blank], axis=0)
        held_ref[f, 0:LANES, 0:LANES] += delta.T
        delta = jnp.concatenate([blank, face_delta(xa_ref[f])], axis=0)
        held_ref[f, EL - LANES :, NODES - LANES :] += delta.T
        for t in range(tiles):
            inner = pl.ds(t * LANES + BZ, LANES - 2 * BZ)
            copies.append(
                pltpu.make_async_copy(held_ref.at[f, inner], out_ref.at[f, inner], left.at[f, t])
            )
            copies[-1].start()
            ends_ref[f, 0, t * BZ : (t + 1) * BZ, :] = held_ref[f, t * LANES : t * LANES + BZ, :]
            last = (t + 1) * LANES
            ends_ref[f, 1, t * BZ : (t + 1) * BZ, :] = held_ref[f, last - BZ : last, :]
    for copy in copies:
        copy.wait()


def lines_kernel(ends_ref, yb_ref, ya_ref, inner_ref, out_ref, line_ref, held_ref, left):
    tiles = EL // LANES
    lane = iota((64, LANES), 1)
    line_ref[...] = jnp.zeros((NODES, LANES), F32)
    copies = []
    for f in range(3):
        low = shift_z(jnp.where(lane < tiles * BZ, yb_ref[f], 0.0))
        high = shift_z(jnp.where(lane < tiles * BZ, ya_ref[f], 0.0))
        high = pltpu.roll(high, LANES // 2, 1)
        for a in range(NP):
            line_ref[a * 64 : a * 64 + 8, :] = low[a * 8 : a * 8 + 8]
            line_ref[a * 64 + 56 : a * 64 + 64, :] = high[a * 8 : a * 8 + 8]
        for j in range(NODES // LANES):
            cols = slice(j * LANES, (j + 1) * LANES)
            lines = line_ref[cols, :].T
            held_ref[f, 0, :, cols] = ends_ref[f, 0, :, cols] + lines[:64]
            held_ref[f, 1, :, cols] = ends_ref[f, 1, :, cols] + lines[64:]
        for side in range(2):
            for t in range(tiles):
                at = pl.ds(t * LANES + side * (LANES - BZ), BZ)
                copies.append(
                    pltpu.make_async_copy(
                        held_ref.at[f, side, pl.ds(t * BZ, BZ)],
                        out_ref.at[f, at],
                        left.at[f, side, t],
                    )
                )
                copies[-1].start()
    for copy in copies:
        copy.wait()


def passed_along(x, along_ex, along_ey):
    rows, cols = lax.axis_size("ex"), lax.axis_size("ey")
    pairs = []
    for i in range(rows):
        for j in range(cols):
            to_i, to_j = i + along_ex, j + along_ey
            if 0 <= to_i < rows and 0 <= to_j < cols:
                pairs.append((i * cols + j, to_i * cols + to_j))
    return lax.ppermute(x, AXES, pairs)


def whole(n):
    return [pl.BlockSpec(memory_space=pltpu.VMEM)] * n


def params(mib):
    return pltpu.CompilerParams(vmem_limit_bytes=mib * MIB)


def cost(micros):
    return pl.CostEstimate(flops=0, bytes_accessed=int(micros * 3_000_000), transcendentals=0)


def body(fields, particles, counts, new_place):
    devices = lax.axis_size(AXES)
    rank = lax.axis_index(AXES).astype(jnp.int32).reshape(1)
    fields = jnp.transpose(fields, (1, 0, 2))
    place = new_place.reshape(1, EL)
    counts = counts.reshape(1, EL)
    smem = [pl.BlockSpec(memory_space=pltpu.SMEM)]
    anywhere = pl.BlockSpec(memory_space=pl.ANY)
    in_hbm = pl.BlockSpec(memory_space=pltpu.HBM)
    struct = jax.ShapeDtypeStruct
    tiles = EL // LANES
    tile_scratch = pltpu.VMEM((tiles, LANES, LANES), F32)
    basis_scratch = pltpu.VMEM((tiles, 3, LANES, LANES), F32)
    work_scratch = pltpu.VMEM((LANES, LANES), F32)
    half = MOVERS // LANES

    def interp(moves, out_shape, mib, name):
        return pl.pallas_call(
            functools.partial(interp_kernel, moves),
            out_shape=out_shape,
            in_specs=smem + [anywhere] * 4,
            out_specs=tuple(whole(2)),
            scratch_shapes=[
                pltpu.VMEM((half, LANES, LANES), F32),
                pltpu.VMEM((half, LANES, LANES), F32),
                pltpu.VMEM((half, 3, LANES, LANES), F32),
                pltpu.VMEM((3, half, NODES, LANES), F32),
                work_scratch,
                pltpu.VMEM((1, MOVERS), jnp.int32),
                pltpu.VMEM((3, EL, NODES), F32),
                pltpu.VMEM((1, EL), jnp.int32),
                pltpu.VMEM((1, EL), jnp.int32),
                pltpu.VMEM((EL, PARTS), F32),
                pltpu.SemaphoreType.DMA((6,)),
            ],
            compiler_params=params(mib),
            cost_estimate=cost(6),
            name=name,
        )(rank, place, counts, fields, particles)

    send_head, position = interp(
        True, (struct((devices * HEAD, LANES), F32), struct((1, EL), jnp.int32)), 58, "moving"
    )
    head, stay_slots = interp(
        False, (struct((MOVERS, 2 * LANES), F32), struct((1, MOVERS), jnp.int32)), 40, "staying"
    )
    recv_head = lax.all_to_all(send_head.reshape(-1), AXES, split_axis=0, concat_axis=0, tiled=True)
    recv_head = recv_head.reshape(devices * HEAD, LANES)
    send = pl.pallas_call(
        pack_kernel,
        out_shape=struct((devices, 3 * COMP, LANES), F32),
        in_specs=whole(2),
        out_specs=whole(1)[0],
        compiler_params=params(58),
        cost_estimate=cost(5),
        name="pack",
    )(position, fields)
    recv = lax.all_to_all(send, AXES, split_axis=0, concat_axis=0, tiled=True)
    face = struct((3, 64, LANES), F32)
    force, xup, xdn, yup, ydn, particles_next, slots = pl.pallas_call(
        force_kernel,
        out_shape=(
            struct((3, tiles, NODES, LANES), F32),
            face,
            face,
            face,
            face,
            struct((EL, PARTS), F32),
            struct((1, EL), jnp.int32),
        ),
        in_specs=whole(3),
        out_specs=tuple(whole(7)),
        scratch_shapes=[tile_scratch, tile_scratch, basis_scratch, work_scratch],
        compiler_params=params(40),
        cost_estimate=cost(8),
        name="force",
    )(head, stay_slots, recv_head)
    base, token = pl.pallas_call(
        base_kernel,
        out_shape=(pltpu.HBM((3, EL, NODES), F32), struct((8, LANES), F32)),
        in_specs=smem + whole(3),
        out_specs=tuple(whole(2)),
        compiler_params=params(20),
        cost_estimate=cost(5),
        name="base",
    )(rank, place, fields, force)
    below_x = passed_along(xup, 1, 0)
    above_x = passed_along(xdn, -1, 0)
    up, down = pl.pallas_call(
        edge_kernel,
        out_shape=(face, face),
        in_specs=whole(5),
        out_specs=tuple(whole(2)),
        compiler_params=params(8),
        cost_estimate=cost(1),
        name="edge",
    )(below_x, above_x, yup, ydn, token)
    below_y = passed_along(up, 0, 1)
    above_y = passed_along(down, 0, -1)
    ends = (3, 2, tiles * BZ, NODES)
    inner, ends_out = pl.pallas_call(
        place_kernel,
        out_shape=(struct((3, EL, NODES), F32), struct(ends, F32)),
        in_specs=whole(1) + [in_hbm, in_hbm] + whole(2),
        out_specs=(in_hbm, whole(1)[0]),
        scratch_shapes=[
            pltpu.VMEM((3, devices, COMP, LANES), F32),
            pltpu.VMEM((3, EL, NODES), F32),
            pltpu.SemaphoreType.DMA((3, 2)),
            pltpu.SemaphoreType.DMA((3, tiles)),
        ],
        compiler_params=params(20),
        cost_estimate=cost(3),
        name="place",
    )(slots, recv, pltpu.with_memory_space_constraint(base, pltpu.HBM), below_x, above_x)
    out = pl.pallas_call(
        lines_kernel,
        out_shape=struct((3, EL, NODES), F32),
        in_specs=whole(3) + [anywhere],
        out_specs=anywhere,
        scratch_shapes=[
            pltpu.VMEM((NODES, LANES), F32),
            pltpu.VMEM(ends, F32),
            pltpu.SemaphoreType.DMA((3, 2, tiles)),
        ],
        input_output_aliases={3: 0},
        compiler_params=params(10),
        cost_estimate=cost(1),
        name="lines",
    )(ends_out, below_y, above_y, inner)
    return jnp.transpose(out, (1, 0, 2)), particles_next


def solution(mesh):
    return jax.shard_map(
        body,
        mesh=mesh,
        in_specs=(P(AXES, None, None), P(AXES, None), P(AXES), P(AXES)),
        out_specs=(P(AXES, None, None), P(AXES, None)),
        check_vma=False,
    )
```

```python
import functools

import jax
import jax.numpy as jnp
import numpy as np
from jax import lax
from jax.experimental import pallas as pl
from jax.experimental.pallas import tpu as pltpu
from jax.sharding import PartitionSpec as P

NP = 8
SLOTS = 16
CAP = 4
PEERS = 64
BX = 4
BY = 8
BZ = 16
NODES = NP**3
EL = BX * BY * BZ
MOVERS = PEERS * CAP
LANES = 128
PARTS = 8 * SLOTS
HEAD = 6
COMP = 16
AXES = ("ex", "ey")
POINTS = [
    -1.0,
    -0.8717401485096066,
    -0.5917001814331423,
    -0.2092992179024789,
    0.2092992179024789,
    0.5917001814331423,
    0.8717401485096066,
    1.0,
]
F32 = jnp.float32
BF16 = jnp.bfloat16
MIB = 1024 * 1024


def iota(shape, axis):
    return lax.broadcasted_iota(jnp.int32, shape, axis)


def split(x):
    high = x.astype(BF16)
    return high, (x - high.astype(F32)).astype(BF16)


def picked(onehot, x):
    high, low = split(x)
    return jnp.dot(onehot, high, preferred_element_type=F32) + jnp.dot(
        onehot, low, preferred_element_type=F32
    )


def as_column(row):
    return jnp.broadcast_to(row, (LANES, EL)).T


def pack_positions(place, rank):
    target = place // EL
    moving = target != rank
    key = jnp.where(moving, target, -1).astype(F32)
    key_col = as_column(key)
    order = []
    for j in range(EL // LANES):
        piece = key[:, j * LANES : (j + 1) * LANES]
        earlier = iota((EL, LANES), 0) < iota((EL, LANES), 1) + j * LANES
        same = (key_col == piece) & earlier
        order.append(jnp.sum(same.astype(F32), axis=0, keepdims=True))
    order = jnp.concatenate(order, axis=1).astype(jnp.int32)
    return jnp.where(moving, target * CAP + order, -1)


def interleave(first, second):
    devices = first.shape[0] // CAP
    low = iota((devices // 2, 8, LANES), 1) < CAP
    first = first.reshape(devices // 2, 8, LANES)
    second = second.reshape(devices // 2, 8, LANES)
    even = jnp.where(low, first, pltpu.roll(second, CAP, 1))
    odd = jnp.where(low, pltpu.roll(first, CAP, 1), second)
    return jnp.stack([even, odd], axis=1).reshape(devices, 8, LANES)


def deinterleave(blocks):
    devices = blocks.shape[0]
    pairs = blocks.reshape(devices // 2, 2, 8, LANES)
    even, odd = pairs[:, 0], pairs[:, 1]
    low = iota((devices // 2, 8, LANES), 1) < CAP
    first = jnp.where(low, even, pltpu.roll(odd, CAP, 1))
    second = jnp.where(low, pltpu.roll(even, CAP, 1), odd)
    return first.reshape(devices * CAP, LANES), second.reshape(devices * CAP, LANES)


def picked_row(row, onehot):
    high, low = split(jnp.broadcast_to(row.astype(F32), (8, row.shape[1])))
    dims = (((1,), (1,)), ((), ()))
    out = lax.dot_general(high, onehot, dims, preferred_element_type=F32)
    out = out + lax.dot_general(low, onehot, dims, preferred_element_type=F32)
    return out[0:1]


def interp_kernel(moves, *refs):
    rank_ref, place_ref, count_ref, fields_ref, part_ref = refs[:5]
    out_refs = refs[5:7]
    tp_ref, push_ref, basis_ref, t_ref, work_ref, count_row_ref, held_ref = refs[7:14]
    place_held, count_held, part_held, arrived = refs[14:]
    tiles = MOVERS // LANES
    pairs = [(place_ref, place_held), (count_ref, count_held), (part_ref, part_held)]
    pairs += [(fields_ref.at[f], held_ref.at[f]) for f in range(3)]
    copies = [pltpu.make_async_copy(*pair, arrived.at[i]) for i, pair in enumerate(pairs)]
    for copy in copies:
        copy.start()
    earlier = (iota((EL, EL), 0) < iota((EL, EL), 1)).astype(BF16)
    copies[0].wait()
    place = place_held[...]
    moving = place // EL != rank_ref[0]
    chosen = moving if moves else jnp.logical_not(moving)
    order = jnp.dot(
        jnp.broadcast_to(chosen.astype(F32), (8, EL)).astype(BF16),
        earlier,
        preferred_element_type=F32,
    )[0:1]
    key = jnp.where(chosen, order.astype(jnp.int32), -1)
    onehot = (iota((MOVERS, EL), 0) == key).astype(BF16)
    slot_row = picked_row(place % EL + 1, onehot)
    copies[1].wait()
    count_row_ref[...] = picked_row(count_held[...], onehot).astype(jnp.int32)
    copies[2].wait()
    records = picked(onehot, part_held[...])
    for t in range(tiles):
        tp_ref[t] = records[t * LANES : (t + 1) * LANES, :].T

    def make_basis(t, carry):
        for d in range(3):
            rows = lagrange_rows(tp_ref[t, d * SLOTS : (d + 1) * SLOTS, :])
            for n in range(NP):
                basis_ref[t, d, n * SLOTS : (n + 1) * SLOTS, :] = rows[n]
        return carry

    lax.fori_loop(0, tiles, make_basis, 0)

    def step(t, f):
        def basis(which, n, p):
            return basis_ref[t, which, pl.ds(n * SLOTS + p, 1), :]

        total = [None] * SLOTS
        for pair in range(NP // 2):
            nodes = [
                [t_ref[f, t, pl.ds(a * 64 + (2 * pair + i) * 8, 8), :] for a in range(NP)]
                for i in range(2)
            ]
            for p in range(SLOTS):
                sums = [None, None]
                for a in range(NP):
                    weight = basis(0, a, p)
                    for i in range(2):
                        term = nodes[i][a] * weight
                        sums[i] = term if sums[i] is None else sums[i] + term
                for i in range(2):
                    term = sums[i] * basis(1, 2 * pair + i, p)
                    total[p] = term if total[p] is None else total[p] + term
        for p in range(SLOTS):
            along_z = basis_ref[t, 2, pl.ds(p, NP, stride=SLOTS), :]
            work_ref[p * NP : (p + 1) * NP, :] = total[p] * along_z
        fluid = work_ref[pl.ds(0, SLOTS, stride=NP), :]
        for c in range(1, NP):
            fluid = fluid + work_ref[pl.ds(c, SLOTS, stride=NP), :]
        where = pl.ds(pl.multiple_of((3 + f) * SLOTS, SLOTS), SLOTS)
        velocity = tp_ref[t, where, :]
        ratio = tp_ref[t, 6 * SLOTS : 7 * SLOTS, :]
        mass = tp_ref[t, 7 * SLOTS : 8 * SLOTS, :]
        count = count_row_ref[:, pl.ds(pl.multiple_of(t * LANES, LANES), LANES)]
        drag = jnp.where(iota((SLOTS, LANES), 0) < count, ratio * (fluid - velocity), 0.0)
        tp_ref[t, where, :] = velocity + drag
        push_ref[t, pl.ds(pl.multiple_of((1 + f) * SLOTS, SLOTS), SLOTS), :] = -(mass * drag)
        return f

    for f in range(3):
        copies[3 + f].wait()
        rows = picked(onehot, held_ref[f])
        for t in range(tiles):
            for j in range(NODES // LANES):
                cols = slice(j * LANES, (j + 1) * LANES)
                t_ref[f, t, cols, :] = rows[t * LANES : (t + 1) * LANES, cols].T
        lax.fori_loop(0, tiles, step, f)

    heads = []
    for t in range(tiles):
        rows = slice(t * LANES, (t + 1) * LANES)
        push_ref[t, 0:SLOTS, :] = jnp.broadcast_to(slot_row[:, rows], (SLOTS, LANES))
        push_ref[t, 4 * SLOTS :, :] = jnp.zeros((LANES - 4 * SLOTS, LANES), F32)
        heads.append(jnp.concatenate([tp_ref[t].T, push_ref[t].T], axis=1))
    head = jnp.concatenate(heads, axis=0)
    if moves:
        send_ref, position_ref = out_refs
        devices = send_ref.shape[0] // HEAD
        position = pack_positions(place, rank_ref[0])
        position_ref[...] = position
        goes_to = picked_row(position, onehot).astype(jnp.int32)
        goes_to = goes_to % CAP * devices + goes_to // CAP
        scatter = (iota((devices * CAP, MOVERS), 0) == goes_to).astype(BF16)
        rows = picked(scatter, head)
        lane = iota((devices, LANES), 1)
        for q in range(CAP):
            mine = slice(q * devices, (q + 1) * devices)
            send_ref[pl.ds(q, devices, stride=HEAD), :] = rows[mine, :LANES]
            if q % 2:
                both = jnp.where(lane < LANES // 2, before, pltpu.roll(rows[mine, LANES:], LANES // 2, 1))
                send_ref[pl.ds(CAP + q // 2, devices, stride=HEAD), :] = both
            before = rows[mine, LANES:]
    else:
        head_ref, slot_ref = out_refs
        head_ref[...] = head
        slot_ref[...] = slot_row.astype(jnp.int32)


def pack_kernel(position_ref, fields_ref, out_ref):
    devices = out_ref.shape[0]
    onehot = (iota((devices * CAP, EL), 0) == position_ref[...]).astype(BF16)
    for f in range(3):
        rows = picked(onehot, fields_ref[f])
        for h in range(2):
            at = COMP * f + 8 * h
            left = 2 * h * LANES
            out_ref[:, at : at + 8, :] = interleave(
                rows[:, left : left + LANES], rows[:, left + LANES : left + 2 * LANES]
            )


def lagrange_rows(coord):
    diffs = [coord - p for p in POINTS]
    left = [None] * NP
    right = [None] * NP
    for i in range(1, NP):
        left[i] = diffs[i - 1] if i == 1 else left[i - 1] * diffs[i - 1]
    for i in range(NP - 2, -1, -1):
        right[i] = diffs[i + 1] if i == NP - 2 else right[i + 1] * diffs[i + 1]
    out = []
    for i in range(NP):
        scale = 1.0
        for m in range(NP):
            if m != i:
                scale /= POINTS[i] - POINTS[m]
        if i == 0:
            term = right[0]
        elif i == NP - 1:
            term = left[i]
        else:
            term = left[i] * right[i]
        out.append(term * float(scale))
    return out


def gaussian_rows(coord):
    return [jnp.exp(-((p - coord) ** 2) * (0.5 / 0.35**2)) for p in POINTS]


def shift_z(x):
    n = x.shape[0] // NP
    x = x.reshape(n, NP, LANES)
    node = iota((n, NP, LANES), 1)
    bz = iota((n, NP, LANES), 2) % BZ
    down = pltpu.roll(pltpu.roll(x, 1, 1), 1, 2)
    up = pltpu.roll(pltpu.roll(x, NP - 1, 1), LANES - 1, 2)
    x = x + jnp.where((node == 0) & (bz > 0), down, 0.0)
    x = x + jnp.where((node == NP - 1) & (bz < BZ - 1), up, 0.0)
    return x.reshape(n * NP, LANES)


def force_kernel(
    head_ref,
    stay_slot_ref,
    recv_ref,
    force_ref,
    xup_ref,
    xdn_ref,
    yup_ref,
    ydn_ref,
    left_ref,
    right_ref,
    part_ref,
    slot_ref,
    tp_ref,
    push_ref,
    basis_ref,
    work_ref,
):
    tiles = EL // LANES
    devices = recv_ref.shape[0] // HEAD
    particles, extra = [], []
    for q in range(CAP):
        particles.append(recv_ref[pl.ds(q, devices, stride=HEAD), :])
        both = recv_ref[pl.ds(CAP + q // 2, devices, stride=HEAD), :]
        extra.append(pltpu.roll(both, LANES // 2, 1) if q % 2 else both)
    particles = jnp.concatenate(particles, axis=0)
    extra = jnp.concatenate(extra, axis=0)
    slot_row = extra.T[0:1, :].astype(jnp.int32)
    at = iota((devices * CAP, devices * CAP), 0)
    turned = at // devices + at % devices * CAP == iota((devices * CAP, devices * CAP), 1)
    high, low = split(jnp.broadcast_to(slot_row.astype(F32), (8, devices * CAP)))
    order = turned.astype(BF16)
    row = jnp.dot(high, order, preferred_element_type=F32)
    row = row + jnp.dot(low, order, preferred_element_type=F32)
    slot_ref[...] = row[0:1].astype(jnp.int32)
    slots = jnp.concatenate([slot_row, stay_slot_ref[...]], axis=1)
    onehot = (iota((EL, EL + MOVERS), 0) + 1 == slots).astype(BF16)
    arrived = jnp.concatenate([particles, extra], axis=1)
    both = picked(onehot, jnp.concatenate([arrived, head_ref[...]], axis=0))
    record = both[:, :LANES]
    push = both[:, LANES:]
    part_ref[...] = record
    for t in range(tiles):
        rows = slice(t * LANES, (t + 1) * LANES)
        tp_ref[t] = record[rows].T
        push_ref[t] = push[rows].T

    def make_basis(t, carry):
        for d in range(3):
            rows = gaussian_rows(tp_ref[t, d * SLOTS : (d + 1) * SLOTS, :])
            for n in range(NP):
                basis_ref[t, d, n * SLOTS : (n + 1) * SLOTS, :] = rows[n]
        return carry

    lax.fori_loop(0, tiles, make_basis, 0)

    def step(index, carry):
        f = index // tiles
        t = index % tiles

        def basis(which, n, p):
            return basis_ref[t, which, pl.ds(n * SLOTS + p, 1), :]

        for p in range(SLOTS):
            along_z = basis_ref[t, 2, pl.ds(p, NP, stride=SLOTS), :]
            value = push_ref[t, pl.ds((1 + f) * SLOTS + p, 1), :]
            work_ref[p * NP : (p + 1) * NP, :] = (0.5 * value) * along_z
        for pair in range(NP // 2):
            acc = [[None] * NP for _ in range(2)]
            for p in range(SLOTS):
                base = work_ref[p * NP : (p + 1) * NP, :]
                lines = [base * basis(1, 2 * pair + i, p) for i in range(2)]
                for a in range(NP):
                    weight = basis(0, a, p)
                    for i in range(2):
                        term = lines[i] * weight
                        acc[i][a] = term if acc[i][a] is None else acc[i][a] + term
            for i in range(2):
                for a in range(NP):
                    force_ref[f, t, pl.ds(a * 64 + (2 * pair + i) * 8, 8), :] = acc[i][a]
        return carry

    lax.fori_loop(0, 3 * tiles, step, 0)

    lane = iota((NP, LANES), 1)
    bz = iota((64, LANES), 1) % BZ
    for f in range(3):
        xup_ref[f] = force_ref[f, tiles - 1, 448:512, :]
        xdn_ref[f] = force_ref[f, 0, 0:64, :]
        left_ref[f] = pltpu.roll(force_ref[f, tiles - 1, 504:512, :], BZ, 1)
        right_ref[f] = pltpu.roll(force_ref[f, 0, 56:64, :], BZ, 1)
        for t in range(tiles - 1):
            summed = force_ref[f, t, 448:512, :] + force_ref[f, t + 1, 0:64, :]
            force_ref[f, t, 448:512, :] = summed
            force_ref[f, t + 1, 0:64, :] = summed
        for a in range(NP):
            first = slice(a * 64, a * 64 + 8)
            last = slice(a * 64 + 56, a * 64 + 64)
            up_line = jnp.zeros((NP, LANES), F32)
            down_line = jnp.zeros((NP, LANES), F32)
            for t in range(tiles):
                upper = force_ref[f, t, last, :]
                lower = force_ref[f, t, first, :]
                take = lane // BZ == t
                up_line = jnp.where(take, pltpu.roll(upper, 16 * t + 16, 1), up_line)
                moved = pltpu.roll(lower, 16 * t, 1) if t else lower
                down_line = jnp.where(take, moved, down_line)
                force_ref[f, t, first, :] = lower + jnp.where(
                    lane >= BZ, pltpu.roll(upper, BZ, 1), 0.0
                )
                force_ref[f, t, last, :] = upper + jnp.where(
                    lane < LANES - BZ, pltpu.roll(lower, LANES - BZ, 1), 0.0
                )
            yup_ref[f, a * 8 : a * 8 + 8, :] = up_line
            ydn_ref[f, a * 8 : a * 8 + 8, :] = down_line
        for t in range(tiles):
            lower = force_ref[f, t, pl.ds(0, 64, stride=NP), :]
            upper = force_ref[f, t, pl.ds(NP - 1, 64, stride=NP), :]
            force_ref[f, t, pl.ds(0, 64, stride=NP), :] = lower + jnp.where(
                bz > 0, pltpu.roll(upper, 1, 1), 0.0
            )
            force_ref[f, t, pl.ds(NP - 1, 64, stride=NP), :] = upper + jnp.where(
                bz < BZ - 1, pltpu.roll(lower, LANES - 1, 1), 0.0
            )


def edge_kernel(below_ref, above_ref, ydn_ref, yb_ref, cb_ref, ca_ref, token_ref, down_ref, low_ref):
    lane = iota((NP, LANES), 1)
    first = lane < BZ
    last = (lane >= 3 * BZ) & (lane < 4 * BZ)
    for f in range(3):
        down_ref[f] = ydn_ref[f]
        down_ref[f, 0:8, :] += jnp.where(first, below_ref[f, 0:8, :], 0.0)
        down_ref[f, 56:64, :] += jnp.where(last, pltpu.roll(above_ref[f, 0:8, :], 3 * BZ, 1), 0.0)
        low_ref[f] = yb_ref[f]
        low_ref[f, 0:8, :] += jnp.where(first, cb_ref[f], 0.0)
        low_ref[f, 56:64, :] += jnp.where(last, pltpu.roll(ca_ref[f], 3 * BZ, 1), 0.0)


def face_delta(face):
    lane = iota((NP, LANES), 1)
    upper = face[56:64]
    lower = face[0:8]
    new_lower = lower + jnp.where(lane >= BZ, pltpu.roll(upper, BZ, 1), 0.0)
    new_upper = upper + jnp.where(lane < LANES - BZ, pltpu.roll(lower, LANES - BZ, 1), 0.0)
    return shift_z(0.5 * jnp.concatenate([new_lower, face[8:56], new_upper], axis=0))


def face_delta(face):
    lane = iota((NP, LANES), 1)
    upper = face[56:64]
    lower = face[0:8]
    new_lower = lower + jnp.where(lane >= BZ, pltpu.roll(upper, BZ, 1), 0.0)
    new_upper = upper + jnp.where(lane < LANES - BZ, pltpu.roll(lower, LANES - BZ, 1), 0.0)
    return shift_z(jnp.concatenate([new_lower, face[8:56], new_upper], axis=0))


def base_kernel(rank_ref, place_ref, fields_ref, force_ref, out_ref, token_ref):
    tiles = EL // LANES
    stay_col = as_column((place_ref[...] // EL == rank_ref[0]).astype(F32)) > 0
    for f in range(3):
        for t in range(tiles):
            rows = slice(t * LANES, (t + 1) * LANES)
            for j in range(NODES // LANES):
                cols = slice(j * LANES, (j + 1) * LANES)
                own = jnp.where(stay_col[rows], fields_ref[f, rows, cols], 0.0)
                out_ref[f, rows, cols] = own + force_ref[f, t, cols, :].T
    token_ref[...] = jnp.zeros((8, LANES), F32)


def lines_of(values, node, line_ref):
    values = shift_z(jnp.where(iota((64, LANES), 1) < BX * BZ, values, 0.0))
    for a in range(NP):
        at = a * 64 + node * 8
        line_ref[at : at + 8, :] = values[a * 8 : a * 8 + 8]
    cols = [line_ref[j * LANES : (j + 1) * LANES, :].T for j in range(NODES // LANES)]
    return jnp.concatenate(cols, axis=1)[: BX * BZ]


def place_kernel(
    slot_ref,
    recv_ref,
    base_ref,
    xb_ref,
    xa_ref,
    low_ref,
    out_ref,
    ends_ref,
    recv_held,
    held_ref,
    line_ref,
    lows_ref,
    arrived,
    left,
):
    devices = recv_ref.shape[0]
    tiles = EL // LANES
    loads = []
    for f in range(3):
        part = (pl.ds(0, devices), pl.ds(COMP * f, COMP))
        loads.append(
            (
                pltpu.make_async_copy(recv_ref.at[part], recv_held.at[f], arrived.at[f, 0]),
                pltpu.make_async_copy(base_ref.at[f], held_ref.at[f], arrived.at[f, 1]),
            )
        )
        for load in loads[f]:
            load.start()
    onehot = (iota((EL, EL), 0) + 1 == slot_ref[...]).astype(BF16)
    blank = jnp.zeros((64, LANES), F32)
    line_ref[...] = jnp.zeros((NODES, LANES), F32)
    for f in range(3):
        lows_ref[f] = lines_of(low_ref[f], 0, line_ref)
    copies = []
    for f in range(3):
        loads[f][0].wait()
        pieces = []
        for h in range(2):
            pieces += list(deinterleave(recv_held[f, :, 8 * h : 8 * h + 8, :]))
        rows = picked(onehot, jnp.concatenate(pieces, axis=1))
        loads[f][1].wait()
        held_ref[f] += rows
        delta = jnp.concatenate([face_delta(xb_ref[f]), blank], axis=0)
        held_ref[f, 0:LANES, 0:LANES] += delta.T
        delta = jnp.concatenate([blank, face_delta(xa_ref[f])], axis=0)
        held_ref[f, EL - LANES :, NODES - LANES :] += delta.T
        for t in range(tiles):
            mine = slice(t * BZ, (t + 1) * BZ)
            held_ref[f, t * LANES : t * LANES + BZ, :] += lows_ref[f, mine, :]
            inner = pl.ds(t * LANES, LANES - BZ)
            copies.append(
                pltpu.make_async_copy(held_ref.at[f, inner], out_ref.at[f, inner], left.at[f, t])
            )
            copies[-1].start()
            last = (t + 1) * LANES
            ends_ref[f, mine, :] = held_ref[f, last - BZ : last, :]
    for copy in copies:
        copy.wait()


def lines_kernel(ends_ref, ya_ref, inner_ref, out_ref, line_ref, held_ref, left):
    tiles = EL // LANES
    line_ref[...] = jnp.zeros((NODES, LANES), F32)
    copies = []
    for f in range(3):
        held_ref[f] = ends_ref[f] + lines_of(ya_ref[f], NP - 1, line_ref)
        for t in range(tiles):
            at = pl.ds((t + 1) * LANES - BZ, BZ)
            mine = pl.ds(t * BZ, BZ)
            copies.append(
                pltpu.make_async_copy(held_ref.at[f, mine], out_ref.at[f, at], left.at[f, t])
            )
            copies[-1].start()
    for copy in copies:
        copy.wait()


def passed_along(x, along_ex, along_ey):
    rows, cols = lax.axis_size("ex"), lax.axis_size("ey")
    pairs = []
    for i in range(rows):
        for j in range(cols):
            to_i, to_j = i + along_ex, j + along_ey
            if 0 <= to_i < rows and 0 <= to_j < cols:
                pairs.append((i * cols + j, to_i * cols + to_j))
    return lax.ppermute(x, AXES, pairs)


def whole(n):
    return [pl.BlockSpec(memory_space=pltpu.VMEM)] * n


def params(mib):
    return pltpu.CompilerParams(vmem_limit_bytes=mib * MIB)


def cost(micros):
    return pl.CostEstimate(flops=0, bytes_accessed=int(micros * 3_000_000), transcendentals=0)


def body(fields, particles, counts, new_place):
    devices = lax.axis_size(AXES)
    rank = lax.axis_index(AXES).astype(jnp.int32).reshape(1)
    fields = jnp.transpose(fields, (1, 0, 2))
    place = new_place.reshape(1, EL)
    counts = counts.reshape(1, EL)
    smem = [pl.BlockSpec(memory_space=pltpu.SMEM)]
    anywhere = pl.BlockSpec(memory_space=pl.ANY)
    in_hbm = pl.BlockSpec(memory_space=pltpu.HBM)
    struct = jax.ShapeDtypeStruct
    tiles = EL // LANES
    tile_scratch = pltpu.VMEM((tiles, LANES, LANES), F32)
    basis_scratch = pltpu.VMEM((tiles, 3, LANES, LANES), F32)
    work_scratch = pltpu.VMEM((LANES, LANES), F32)
    half = MOVERS // LANES

    def interp(moves, out_shape, mib, name):
        return pl.pallas_call(
            functools.partial(interp_kernel, moves),
            out_shape=out_shape,
            in_specs=smem + [anywhere] * 4,
            out_specs=tuple(whole(2)),
            scratch_shapes=[
                pltpu.VMEM((half, LANES, LANES), F32),
                pltpu.VMEM((half, LANES, LANES), F32),
                pltpu.VMEM((half, 3, LANES, LANES), F32),
                pltpu.VMEM((3, half, NODES, LANES), F32),
                work_scratch,
                pltpu.VMEM((1, MOVERS), jnp.int32),
                pltpu.VMEM((3, EL, NODES), F32),
                pltpu.VMEM((1, EL), jnp.int32),
                pltpu.VMEM((1, EL), jnp.int32),
                pltpu.VMEM((EL, PARTS), F32),
                pltpu.SemaphoreType.DMA((6,)),
            ],
            compiler_params=params(mib),
            cost_estimate=cost(6),
            name=name,
        )(rank, place, counts, fields, particles)

    send_head, position = interp(
        True, (struct((devices * HEAD, LANES), F32), struct((1, EL), jnp.int32)), 58, "moving"
    )
    head, stay_slots = interp(
        False, (struct((MOVERS, 2 * LANES), F32), struct((1, MOVERS), jnp.int32)), 40, "staying"
    )
    recv_head = lax.all_to_all(send_head.reshape(-1), AXES, split_axis=0, concat_axis=0, tiled=True)
    recv_head = recv_head.reshape(devices * HEAD, LANES)
    send = pl.pallas_call(
        pack_kernel,
        out_shape=struct((devices, 3 * COMP, LANES), F32),
        in_specs=whole(2),
        out_specs=whole(1)[0],
        compiler_params=params(58),
        cost_estimate=cost(5),
        name="pack",
    )(position, fields)
    recv = lax.all_to_all(send, AXES, split_axis=0, concat_axis=0, tiled=True)
    face = struct((3, 64, LANES), F32)
    corner = struct((3, NP, LANES), F32)
    force, xup, xdn, yup, ydn, left, right, particles_next, slots = pl.pallas_call(
        force_kernel,
        out_shape=(
            struct((3, tiles, NODES, LANES), F32),
            face,
            face,
            face,
            face,
            corner,
            corner,
            struct((EL, PARTS), F32),
            struct((1, EL), jnp.int32),
        ),
        in_specs=whole(3),
        out_specs=tuple(whole(9)),
        scratch_shapes=[tile_scratch, tile_scratch, basis_scratch, work_scratch],
        compiler_params=params(40),
        cost_estimate=cost(8),
        name="force",
    )(head, stay_slots, recv_head)
    base, token = pl.pallas_call(
        base_kernel,
        out_shape=(pltpu.HBM((3, EL, NODES), F32), struct((8, LANES), F32)),
        in_specs=smem + whole(3),
        out_specs=tuple(whole(2)),
        compiler_params=params(20),
        cost_estimate=cost(5),
        name="base",
    )(rank, place, fields, force)
    below_x = passed_along(xup, 1, 0)
    above_x = passed_along(xdn, -1, 0)
    below_y = passed_along(yup, 0, 1)
    corner_below = passed_along(left, 1, 1)
    corner_above = passed_along(right, -1, 1)
    down, low = pl.pallas_call(
        edge_kernel,
        out_shape=(face, face),
        in_specs=whole(7),
        out_specs=tuple(whole(2)),
        compiler_params=params(8),
        cost_estimate=cost(1),
        name="edge",
    )(below_x, above_x, ydn, below_y, corner_below, corner_above, token)
    above_y = passed_along(down, 0, -1)
    ends = (3, tiles * BZ, NODES)
    inner, ends_out = pl.pallas_call(
        place_kernel,
        out_shape=(struct((3, EL, NODES), F32), struct(ends, F32)),
        in_specs=whole(1) + [in_hbm, in_hbm] + whole(3),
        out_specs=(in_hbm, whole(1)[0]),
        scratch_shapes=[
            pltpu.VMEM((3, devices, COMP, LANES), F32),
            pltpu.VMEM((3, EL, NODES), F32),
            pltpu.VMEM((NODES, LANES), F32),
            pltpu.VMEM(ends, F32),
            pltpu.SemaphoreType.DMA((3, 2)),
            pltpu.SemaphoreType.DMA((3, tiles)),
        ],
        compiler_params=params(20),
        cost_estimate=cost(3),
        name="place",
    )(
        slots,
        recv,
        pltpu.with_memory_space_constraint(base, pltpu.HBM),
        below_x,
        above_x,
        low,
    )
    out = pl.pallas_call(
        lines_kernel,
        out_shape=struct((3, EL, NODES), F32),
        in_specs=whole(2) + [anywhere],
        out_specs=anywhere,
        scratch_shapes=[
            pltpu.VMEM((NODES, LANES), F32),
            pltpu.VMEM(ends, F32),
            pltpu.SemaphoreType.DMA((3, tiles)),
        ],
        input_output_aliases={2: 0},
        compiler_params=params(10),
        cost_estimate=cost(1),
        name="lines",
    )(ends_out, above_y, inner)
    return jnp.transpose(out, (1, 0, 2)), particles_next


def solution(mesh):
    return jax.shard_map(
        body,
        mesh=mesh,
        in_specs=(P(AXES, None, None), P(AXES, None), P(AXES), P(AXES)),
        out_specs=(P(AXES, None, None), P(AXES, None)),
        check_vma=False,
    )
```

```python
import functools

import jax
import jax.numpy as jnp
import numpy as np
from jax import lax
from jax.experimental import pallas as pl
from jax.experimental.pallas import tpu as pltpu
from jax.sharding import PartitionSpec as P

NP = 8
SLOTS = 16
CAP = 4
PEERS = 64
BX = 4
BY = 8
BZ = 16
NODES = NP**3
EL = BX * BY * BZ
MOVERS = PEERS * CAP
LANES = 128
PARTS = 8 * SLOTS
HEAD = 6
COMP = 16
AXES = ("ex", "ey")
POINTS = [
    -1.0,
    -0.8717401485096066,
    -0.5917001814331423,
    -0.2092992179024789,
    0.2092992179024789,
    0.5917001814331423,
    0.8717401485096066,
    1.0,
]
F32 = jnp.float32
BF16 = jnp.bfloat16
MIB = 1024 * 1024


def iota(shape, axis):
    return lax.broadcasted_iota(jnp.int32, shape, axis)


def split(x):
    high = x.astype(BF16)
    return high, (x - high.astype(F32)).astype(BF16)


def picked(onehot, x):
    high, low = split(x)
    return jnp.dot(onehot, high, preferred_element_type=F32) + jnp.dot(
        onehot, low, preferred_element_type=F32
    )


def as_column(row):
    return jnp.broadcast_to(row, (LANES, EL)).T


def pack_positions(place, rank):
    target = place // EL
    moving = target != rank
    key = jnp.where(moving, target, -1).astype(F32)
    key_col = as_column(key)
    order = []
    for j in range(EL // LANES):
        piece = key[:, j * LANES : (j + 1) * LANES]
        earlier = iota((EL, LANES), 0) < iota((EL, LANES), 1) + j * LANES
        same = (key_col == piece) & earlier
        order.append(jnp.sum(same.astype(F32), axis=0, keepdims=True))
    order = jnp.concatenate(order, axis=1).astype(jnp.int32)
    return jnp.where(moving, target * CAP + order, -1)


def interleave(first, second):
    devices = first.shape[0] // CAP
    low = iota((devices // 2, 8, LANES), 1) < CAP
    first = first.reshape(devices // 2, 8, LANES)
    second = second.reshape(devices // 2, 8, LANES)
    even = jnp.where(low, first, pltpu.roll(second, CAP, 1))
    odd = jnp.where(low, pltpu.roll(first, CAP, 1), second)
    return jnp.stack([even, odd], axis=1).reshape(devices, 8, LANES)


def deinterleave(blocks):
    devices = blocks.shape[0]
    pairs = blocks.reshape(devices // 2, 2, 8, LANES)
    even, odd = pairs[:, 0], pairs[:, 1]
    low = iota((devices // 2, 8, LANES), 1) < CAP
    first = jnp.where(low, even, pltpu.roll(odd, CAP, 1))
    second = jnp.where(low, pltpu.roll(even, CAP, 1), odd)
    return first.reshape(devices * CAP, LANES), second.reshape(devices * CAP, LANES)


def picked_row(row, onehot):
    high, low = split(jnp.broadcast_to(row.astype(F32), (8, row.shape[1])))
    dims = (((1,), (1,)), ((), ()))
    out = lax.dot_general(high, onehot, dims, preferred_element_type=F32)
    out = out + lax.dot_general(low, onehot, dims, preferred_element_type=F32)
    return out[0:1]


def interp_kernel(moves, *refs):
    rank_ref, place_ref, count_ref, fields_ref, part_ref = refs[:5]
    out_refs = refs[5:7]
    tp_ref, push_ref, basis_ref, t_ref, work_ref, count_row_ref, held_ref = refs[7:14]
    place_held, count_held, part_held, arrived = refs[14:]
    tiles = MOVERS // LANES
    pairs = [(place_ref, place_held), (count_ref, count_held), (part_ref, part_held)]
    pairs += [(fields_ref.at[f], held_ref.at[f]) for f in range(3)]
    copies = [pltpu.make_async_copy(*pair, arrived.at[i]) for i, pair in enumerate(pairs)]
    for copy in copies:
        copy.start()
    earlier = (iota((EL, EL), 0) < iota((EL, EL), 1)).astype(BF16)
    copies[0].wait()
    place = place_held[...]
    moving = place // EL != rank_ref[0]
    chosen = moving if moves else jnp.logical_not(moving)
    order = jnp.dot(
        jnp.broadcast_to(chosen.astype(F32), (8, EL)).astype(BF16),
        earlier,
        preferred_element_type=F32,
    )[0:1]
    key = jnp.where(chosen, order.astype(jnp.int32), -1)
    onehot = (iota((MOVERS, EL), 0) == key).astype(BF16)
    slot_row = picked_row(place % EL + 1, onehot)
    copies[1].wait()
    count_row_ref[...] = picked_row(count_held[...], onehot).astype(jnp.int32)
    copies[2].wait()
    records = picked(onehot, part_held[...])
    for t in range(tiles):
        tp_ref[t] = records[t * LANES : (t + 1) * LANES, :].T

    def make_basis(t, carry):
        for d in range(3):
            rows = lagrange_rows(tp_ref[t, d * SLOTS : (d + 1) * SLOTS, :])
            for n in range(NP):
                basis_ref[t, d, n * SLOTS : (n + 1) * SLOTS, :] = rows[n]
        return carry

    lax.fori_loop(0, tiles, make_basis, 0)

    def step(t, f):
        def basis(which, n, p):
            return basis_ref[t, which, pl.ds(n * SLOTS + p, 1), :]

        total = [None] * SLOTS
        for pair in range(NP // 2):
            nodes = [
                [t_ref[f, t, pl.ds(a * 64 + (2 * pair + i) * 8, 8), :] for a in range(NP)]
                for i in range(2)
            ]
            for p in range(SLOTS):
                sums = [None, None]
                for a in range(NP):
                    weight = basis(0, a, p)
                    for i in range(2):
                        term = nodes[i][a] * weight
                        sums[i] = term if sums[i] is None else sums[i] + term
                for i in range(2):
                    term = sums[i] * basis(1, 2 * pair + i, p)
                    total[p] = term if total[p] is None else total[p] + term
        for p in range(SLOTS):
            along_z = basis_ref[t, 2, pl.ds(p, NP, stride=SLOTS), :]
            work_ref[p * NP : (p + 1) * NP, :] = total[p] * along_z
        fluid = work_ref[pl.ds(0, SLOTS, stride=NP), :]
        for c in range(1, NP):
            fluid = fluid + work_ref[pl.ds(c, SLOTS, stride=NP), :]
        where = pl.ds(pl.multiple_of((3 + f) * SLOTS, SLOTS), SLOTS)
        velocity = tp_ref[t, where, :]
        ratio = tp_ref[t, 6 * SLOTS : 7 * SLOTS, :]
        mass = tp_ref[t, 7 * SLOTS : 8 * SLOTS, :]
        count = count_row_ref[:, pl.ds(pl.multiple_of(t * LANES, LANES), LANES)]
        drag = jnp.where(iota((SLOTS, LANES), 0) < count, ratio * (fluid - velocity), 0.0)
        tp_ref[t, where, :] = velocity + drag
        push_ref[t, pl.ds(pl.multiple_of((1 + f) * SLOTS, SLOTS), SLOTS), :] = -(mass * drag)
        return f

    for f in range(3):
        copies[3 + f].wait()
        rows = picked(onehot, held_ref[f])
        for t in range(tiles):
            for j in range(NODES // LANES):
                cols = slice(j * LANES, (j + 1) * LANES)
                t_ref[f, t, cols, :] = rows[t * LANES : (t + 1) * LANES, cols].T
        lax.fori_loop(0, tiles, step, f)

    heads = []
    for t in range(tiles):
        rows = slice(t * LANES, (t + 1) * LANES)
        push_ref[t, 0:SLOTS, :] = jnp.broadcast_to(slot_row[:, rows], (SLOTS, LANES))
        push_ref[t, 4 * SLOTS :, :] = jnp.zeros((LANES - 4 * SLOTS, LANES), F32)
        heads.append(jnp.concatenate([tp_ref[t].T, push_ref[t].T], axis=1))
    head = jnp.concatenate(heads, axis=0)
    if moves:
        send_ref, position_ref = out_refs
        devices = send_ref.shape[0] // HEAD
        position = pack_positions(place, rank_ref[0])
        position_ref[...] = position
        goes_to = picked_row(position, onehot).astype(jnp.int32)
        goes_to = goes_to % CAP * devices + goes_to // CAP
        scatter = (iota((devices * CAP, MOVERS), 0) == goes_to).astype(BF16)
        rows = picked(scatter, head)
        lane = iota((devices, LANES), 1)
        for q in range(CAP):
            mine = slice(q * devices, (q + 1) * devices)
            send_ref[pl.ds(q, devices, stride=HEAD), :] = rows[mine, :LANES]
            if q % 2:
                both = jnp.where(lane < LANES // 2, before, pltpu.roll(rows[mine, LANES:], LANES // 2, 1))
                send_ref[pl.ds(CAP + q // 2, devices, stride=HEAD), :] = both
            before = rows[mine, LANES:]
    else:
        head_ref, slot_ref = out_refs
        head_ref[...] = head
        slot_ref[...] = slot_row.astype(jnp.int32)


def pack_kernel(position_ref, fields_ref, out_ref):
    devices = out_ref.shape[0]
    onehot = (iota((devices * CAP, EL), 0) == position_ref[...]).astype(BF16)
    for f in range(3):
        rows = picked(onehot, fields_ref[f])
        for h in range(2):
            at = COMP * f + 8 * h
            left = 2 * h * LANES
            out_ref[:, at : at + 8, :] = interleave(
                rows[:, left : left + LANES], rows[:, left + LANES : left + 2 * LANES]
            )


def lagrange_rows(coord):
    diffs = [coord - p for p in POINTS]
    left = [None] * NP
    right = [None] * NP
    for i in range(1, NP):
        left[i] = diffs[i - 1] if i == 1 else left[i - 1] * diffs[i - 1]
    for i in range(NP - 2, -1, -1):
        right[i] = diffs[i + 1] if i == NP - 2 else right[i + 1] * diffs[i + 1]
    out = []
    for i in range(NP):
        scale = 1.0
        for m in range(NP):
            if m != i:
                scale /= POINTS[i] - POINTS[m]
        if i == 0:
            term = right[0]
        elif i == NP - 1:
            term = left[i]
        else:
            term = left[i] * right[i]
        out.append(term * float(scale))
    return out


def gaussian_rows(coord):
    return [jnp.exp(-((p - coord) ** 2) * (0.5 / 0.35**2)) for p in POINTS]


def shift_z(x):
    n = x.shape[0] // NP
    x = x.reshape(n, NP, LANES)
    node = iota((n, NP, LANES), 1)
    bz = iota((n, NP, LANES), 2) % BZ
    down = pltpu.roll(pltpu.roll(x, 1, 1), 1, 2)
    up = pltpu.roll(pltpu.roll(x, NP - 1, 1), LANES - 1, 2)
    x = x + jnp.where((node == 0) & (bz > 0), down, 0.0)
    x = x + jnp.where((node == NP - 1) & (bz < BZ - 1), up, 0.0)
    return x.reshape(n * NP, LANES)


def force_kernel(
    head_ref,
    stay_slot_ref,
    recv_ref,
    force_ref,
    xup_ref,
    xdn_ref,
    yup_ref,
    ydn_ref,
    left_ref,
    right_ref,
    part_ref,
    slot_ref,
    peers_ref,
    tp_ref,
    push_ref,
    basis_ref,
    work_ref,
):
    tiles = EL // LANES
    devices = recv_ref.shape[0] // HEAD
    particles, extra = [], []
    for q in range(CAP):
        particles.append(recv_ref[pl.ds(q, devices, stride=HEAD), :])
        both = recv_ref[pl.ds(CAP + q // 2, devices, stride=HEAD), :]
        extra.append(pltpu.roll(both, LANES // 2, 1) if q % 2 else both)
    particles = jnp.concatenate(particles, axis=0)
    extra = jnp.concatenate(extra, axis=0)
    slot_row = extra.T[0:1, :].astype(jnp.int32)
    at = iota((devices * CAP, devices * CAP), 0)
    turned = at // devices + at % devices * CAP == iota((devices * CAP, devices * CAP), 1)
    high, low = split(jnp.broadcast_to(slot_row.astype(F32), (8, devices * CAP)))
    order = turned.astype(BF16)
    row = jnp.dot(high, order, preferred_element_type=F32)
    row = row + jnp.dot(low, order, preferred_element_type=F32)
    row = row[0:1].astype(jnp.int32)
    filled = row > 0
    earlier = (iota((devices * CAP, devices * CAP), 0) < iota((devices * CAP, devices * CAP), 1)).astype(BF16)
    rank = jnp.dot(
        jnp.broadcast_to(filled.astype(F32), (8, devices * CAP)).astype(BF16),
        earlier,
        preferred_element_type=F32,
    )[0:1]
    key = jnp.where(filled, rank.astype(jnp.int32), -1)
    packed = (iota((MOVERS, devices * CAP), 0) == key).astype(BF16)
    slot_ref[...] = picked_row(row, packed).astype(jnp.int32)
    peers_ref[...] = picked_row(iota((1, devices * CAP), 1) // CAP, packed).astype(jnp.int32)
    slots = jnp.concatenate([slot_row, stay_slot_ref[...]], axis=1)
    onehot = (iota((EL, EL + MOVERS), 0) + 1 == slots).astype(BF16)
    arrived = jnp.concatenate([particles, extra], axis=1)
    both = picked(onehot, jnp.concatenate([arrived, head_ref[...]], axis=0))
    record = both[:, :LANES]
    push = both[:, LANES:]
    part_ref[...] = record
    for t in range(tiles):
        rows = slice(t * LANES, (t + 1) * LANES)
        tp_ref[t] = record[rows].T
        push_ref[t] = push[rows].T

    def make_basis(t, carry):
        for d in range(3):
            rows = gaussian_rows(tp_ref[t, d * SLOTS : (d + 1) * SLOTS, :])
            for n in range(NP):
                basis_ref[t, d, n * SLOTS : (n + 1) * SLOTS, :] = rows[n]
        return carry

    lax.fori_loop(0, tiles, make_basis, 0)

    def step(index, carry):
        f = index // tiles
        t = index % tiles

        def basis(which, n, p):
            return basis_ref[t, which, pl.ds(n * SLOTS + p, 1), :]

        for p in range(SLOTS):
            along_z = basis_ref[t, 2, pl.ds(p, NP, stride=SLOTS), :]
            value = push_ref[t, pl.ds((1 + f) * SLOTS + p, 1), :]
            work_ref[p * NP : (p + 1) * NP, :] = (0.5 * value) * along_z
        for pair in range(NP // 2):
            acc = [[None] * NP for _ in range(2)]
            for p in range(SLOTS):
                base = work_ref[p * NP : (p + 1) * NP, :]
                lines = [base * basis(1, 2 * pair + i, p) for i in range(2)]
                for a in range(NP):
                    weight = basis(0, a, p)
                    for i in range(2):
                        term = lines[i] * weight
                        acc[i][a] = term if acc[i][a] is None else acc[i][a] + term
            for i in range(2):
                for a in range(NP):
                    force_ref[f, t, pl.ds(a * 64 + (2 * pair + i) * 8, 8), :] = acc[i][a]
        return carry

    lax.fori_loop(0, 3 * tiles, step, 0)

    lane = iota((NP, LANES), 1)
    bz = iota((64, LANES), 1) % BZ
    for f in range(3):
        xup_ref[f] = force_ref[f, tiles - 1, 448:512, :]
        xdn_ref[f] = force_ref[f, 0, 0:64, :]
        left_ref[f] = pltpu.roll(force_ref[f, tiles - 1, 504:512, :], BZ, 1)
        right_ref[f] = pltpu.roll(force_ref[f, 0, 56:64, :], BZ, 1)
        for t in range(tiles - 1):
            summed = force_ref[f, t, 448:512, :] + force_ref[f, t + 1, 0:64, :]
            force_ref[f, t, 448:512, :] = summed
            force_ref[f, t + 1, 0:64, :] = summed
        for a in range(NP):
            first = slice(a * 64, a * 64 + 8)
            last = slice(a * 64 + 56, a * 64 + 64)
            up_line = jnp.zeros((NP, LANES), F32)
            down_line = jnp.zeros((NP, LANES), F32)
            for t in range(tiles):
                upper = force_ref[f, t, last, :]
                lower = force_ref[f, t, first, :]
                take = lane // BZ == t
                up_line = jnp.where(take, pltpu.roll(upper, 16 * t + 16, 1), up_line)
                moved = pltpu.roll(lower, 16 * t, 1) if t else lower
                down_line = jnp.where(take, moved, down_line)
                force_ref[f, t, first, :] = lower + jnp.where(
                    lane >= BZ, pltpu.roll(upper, BZ, 1), 0.0
                )
                force_ref[f, t, last, :] = upper + jnp.where(
                    lane < LANES - BZ, pltpu.roll(lower, LANES - BZ, 1), 0.0
                )
            yup_ref[f, a * 8 : a * 8 + 8, :] = up_line
            ydn_ref[f, a * 8 : a * 8 + 8, :] = down_line
        for t in range(tiles):
            lower = force_ref[f, t, pl.ds(0, 64, stride=NP), :]
            upper = force_ref[f, t, pl.ds(NP - 1, 64, stride=NP), :]
            force_ref[f, t, pl.ds(0, 64, stride=NP), :] = lower + jnp.where(
                bz > 0, pltpu.roll(upper, 1, 1), 0.0
            )
            force_ref[f, t, pl.ds(NP - 1, 64, stride=NP), :] = upper + jnp.where(
                bz < BZ - 1, pltpu.roll(lower, LANES - 1, 1), 0.0
            )


def edge_kernel(below_ref, above_ref, ydn_ref, yb_ref, cb_ref, ca_ref, token_ref, down_ref, low_ref):
    lane = iota((NP, LANES), 1)
    first = lane < BZ
    last = (lane >= 3 * BZ) & (lane < 4 * BZ)
    for f in range(3):
        down_ref[f] = ydn_ref[f]
        down_ref[f, 0:8, :] += jnp.where(first, below_ref[f, 0:8, :], 0.0)
        down_ref[f, 56:64, :] += jnp.where(last, pltpu.roll(above_ref[f, 0:8, :], 3 * BZ, 1), 0.0)
        low_ref[f] = yb_ref[f]
        low_ref[f, 0:8, :] += jnp.where(first, cb_ref[f], 0.0)
        low_ref[f, 56:64, :] += jnp.where(last, pltpu.roll(ca_ref[f], 3 * BZ, 1), 0.0)


def face_delta(face):
    lane = iota((NP, LANES), 1)
    upper = face[56:64]
    lower = face[0:8]
    new_lower = lower + jnp.where(lane >= BZ, pltpu.roll(upper, BZ, 1), 0.0)
    new_upper = upper + jnp.where(lane < LANES - BZ, pltpu.roll(lower, LANES - BZ, 1), 0.0)
    return shift_z(0.5 * jnp.concatenate([new_lower, face[8:56], new_upper], axis=0))


def face_delta(face):
    lane = iota((NP, LANES), 1)
    upper = face[56:64]
    lower = face[0:8]
    new_lower = lower + jnp.where(lane >= BZ, pltpu.roll(upper, BZ, 1), 0.0)
    new_upper = upper + jnp.where(lane < LANES - BZ, pltpu.roll(lower, LANES - BZ, 1), 0.0)
    return shift_z(jnp.concatenate([new_lower, face[8:56], new_upper], axis=0))


def base_kernel(rank_ref, place_ref, fields_ref, force_ref, out_ref, token_ref):
    tiles = EL // LANES
    stay_col = as_column((place_ref[...] // EL == rank_ref[0]).astype(F32)) > 0
    for f in range(3):
        for t in range(tiles):
            rows = slice(t * LANES, (t + 1) * LANES)
            for j in range(NODES // LANES):
                cols = slice(j * LANES, (j + 1) * LANES)
                own = jnp.where(stay_col[rows], fields_ref[f, rows, cols], 0.0)
                out_ref[f, rows, cols] = own + force_ref[f, t, cols, :].T
    token_ref[...] = jnp.zeros((8, LANES), F32)


def lines_of(values, node, line_ref):
    values = shift_z(jnp.where(iota((64, LANES), 1) < BX * BZ, values, 0.0))
    for a in range(NP):
        at = a * 64 + node * 8
        line_ref[at : at + 8, :] = values[a * 8 : a * 8 + 8]
    cols = [line_ref[j * LANES : (j + 1) * LANES, :].T for j in range(NODES // LANES)]
    return jnp.concatenate(cols, axis=1)[: BX * BZ]


def place_kernel(
    peers_ref,
    slot_ref,
    recv_ref,
    base_ref,
    xb_ref,
    xa_ref,
    low_ref,
    out_ref,
    ends_ref,
    recv_held,
    held_ref,
    line_ref,
    lows_ref,
    arrived,
    left,
):
    tiles = EL // LANES

    def fetch(c, carry):
        peer = peers_ref[0, CAP * c]
        pltpu.make_async_copy(recv_ref.at[peer], recv_held.at[c], arrived.at[0, 0]).start()
        return carry

    lax.fori_loop(0, PEERS, fetch, 0, unroll=8)

    whole_recv = pltpu.make_async_copy(recv_ref.at[pl.ds(0, PEERS)], recv_held, arrived.at[0, 0])
    loads = []
    for f in range(3):
        loads.append(pltpu.make_async_copy(base_ref.at[f], held_ref.at[f], arrived.at[f, 1]))
        loads[f].start()
    onehot = (iota((EL, MOVERS), 0) + 1 == slot_ref[...]).astype(BF16)
    blank = jnp.zeros((64, LANES), F32)
    line_ref[...] = jnp.zeros((NODES, LANES), F32)
    for f in range(3):
        lows_ref[f] = lines_of(low_ref[f], 0, line_ref)
    copies = []
    for f in range(3):
        if f == 0:
            whole_recv.wait()
        pieces = []
        for h in range(2):
            pieces += list(deinterleave(recv_held[:, COMP * f + 8 * h : COMP * f + 8 * h + 8, :]))
        rows = picked(onehot, jnp.concatenate(pieces, axis=1))
        loads[f].wait()
        held_ref[f] += rows
        delta = jnp.concatenate([face_delta(xb_ref[f]), blank], axis=0)
        held_ref[f, 0:LANES, 0:LANES] += delta.T
        delta = jnp.concatenate([blank, face_delta(xa_ref[f])], axis=0)
        held_ref[f, EL - LANES :, NODES - LANES :] += delta.T
        for t in range(tiles):
            mine = slice(t * BZ, (t + 1) * BZ)
            held_ref[f, t * LANES : t * LANES + BZ, :] += lows_ref[f, mine, :]
            inner = pl.ds(t * LANES, LANES - BZ)
            copies.append(
                pltpu.make_async_copy(held_ref.at[f, inner], out_ref.at[f, inner], left.at[f, t])
            )
            copies[-1].start()
            last = (t + 1) * LANES
            ends_ref[f, mine, :] = held_ref[f, last - BZ : last, :]
    for copy in copies:
        copy.wait()


def lines_kernel(ends_ref, ya_ref, inner_ref, out_ref, line_ref, held_ref, left):
    tiles = EL // LANES
    line_ref[...] = jnp.zeros((NODES, LANES), F32)
    copies = []
    for f in range(3):
        held_ref[f] = ends_ref[f] + lines_of(ya_ref[f], NP - 1, line_ref)
        for t in range(tiles):
            at = pl.ds((t + 1) * LANES - BZ, BZ)
            mine = pl.ds(t * BZ, BZ)
            copies.append(
                pltpu.make_async_copy(held_ref.at[f, mine], out_ref.at[f, at], left.at[f, t])
            )
            copies[-1].start()
    for copy in copies:
        copy.wait()


def passed_along(x, along_ex, along_ey):
    rows, cols = lax.axis_size("ex"), lax.axis_size("ey")
    pairs = []
    for i in range(rows):
        for j in range(cols):
            to_i, to_j = i + along_ex, j + along_ey
            if 0 <= to_i < rows and 0 <= to_j < cols:
                pairs.append((i * cols + j, to_i * cols + to_j))
    return lax.ppermute(x, AXES, pairs)


def whole(n):
    return [pl.BlockSpec(memory_space=pltpu.VMEM)] * n


def params(mib):
    return pltpu.CompilerParams(vmem_limit_bytes=mib * MIB)


def cost(micros):
    return pl.CostEstimate(flops=0, bytes_accessed=int(micros * 3_000_000), transcendentals=0)


def body(fields, particles, counts, new_place):
    devices = lax.axis_size(AXES)
    rank = lax.axis_index(AXES).astype(jnp.int32).reshape(1)
    fields = jnp.transpose(fields, (1, 0, 2))
    place = new_place.reshape(1, EL)
    counts = counts.reshape(1, EL)
    smem = [pl.BlockSpec(memory_space=pltpu.SMEM)]
    anywhere = pl.BlockSpec(memory_space=pl.ANY)
    in_hbm = pl.BlockSpec(memory_space=pltpu.HBM)
    struct = jax.ShapeDtypeStruct
    tiles = EL // LANES
    tile_scratch = pltpu.VMEM((tiles, LANES, LANES), F32)
    basis_scratch = pltpu.VMEM((tiles, 3, LANES, LANES), F32)
    work_scratch = pltpu.VMEM((LANES, LANES), F32)
    half = MOVERS // LANES

    def interp(moves, out_shape, mib, name):
        return pl.pallas_call(
            functools.partial(interp_kernel, moves),
            out_shape=out_shape,
            in_specs=smem + [anywhere] * 4,
            out_specs=tuple(whole(2)),
            scratch_shapes=[
                pltpu.VMEM((half, LANES, LANES), F32),
                pltpu.VMEM((half, LANES, LANES), F32),
                pltpu.VMEM((half, 3, LANES, LANES), F32),
                pltpu.VMEM((3, half, NODES, LANES), F32),
                work_scratch,
                pltpu.VMEM((1, MOVERS), jnp.int32),
                pltpu.VMEM((3, EL, NODES), F32),
                pltpu.VMEM((1, EL), jnp.int32),
                pltpu.VMEM((1, EL), jnp.int32),
                pltpu.VMEM((EL, PARTS), F32),
                pltpu.SemaphoreType.DMA((6,)),
            ],
            compiler_params=params(mib),
            cost_estimate=cost(6),
            name=name,
        )(rank, place, counts, fields, particles)

    send_head, position = interp(
        True, (struct((devices * HEAD, LANES), F32), struct((1, EL), jnp.int32)), 58, "moving"
    )
    head, stay_slots = interp(
        False, (struct((MOVERS, 2 * LANES), F32), struct((1, MOVERS), jnp.int32)), 40, "staying"
    )
    recv_head = lax.all_to_all(send_head.reshape(-1), AXES, split_axis=0, concat_axis=0, tiled=True)
    recv_head = recv_head.reshape(devices * HEAD, LANES)
    send = pl.pallas_call(
        pack_kernel,
        out_shape=struct((devices, 3 * COMP, LANES), F32),
        in_specs=whole(2),
        out_specs=whole(1)[0],
        compiler_params=params(58),
        cost_estimate=cost(5),
        name="pack",
    )(position, fields)
    recv = lax.all_to_all(send, AXES, split_axis=0, concat_axis=0, tiled=True)
    face = struct((3, 64, LANES), F32)
    corner = struct((3, NP, LANES), F32)
    force, xup, xdn, yup, ydn, left, right, particles_next, slots, peers = pl.pallas_call(
        force_kernel,
        out_shape=(
            struct((3, tiles, NODES, LANES), F32),
            face,
            face,
            face,
            face,
            corner,
            corner,
            struct((EL, PARTS), F32),
            struct((1, MOVERS), jnp.int32),
            struct((1, MOVERS), jnp.int32),
        ),
        in_specs=whole(3),
        out_specs=tuple(whole(10)),
        scratch_shapes=[tile_scratch, tile_scratch, basis_scratch, work_scratch],
        compiler_params=params(40),
        cost_estimate=cost(8),
        name="force",
    )(head, stay_slots, recv_head)
    base, token = pl.pallas_call(
        base_kernel,
        out_shape=(pltpu.HBM((3, EL, NODES), F32), struct((8, LANES), F32)),
        in_specs=smem + whole(3),
        out_specs=tuple(whole(2)),
        compiler_params=params(20),
        cost_estimate=cost(5),
        name="base",
    )(rank, place, fields, force)
    below_x = passed_along(xup, 1, 0)
    above_x = passed_along(xdn, -1, 0)
    below_y = passed_along(yup, 0, 1)
    corner_below = passed_along(left, 1, 1)
    corner_above = passed_along(right, -1, 1)
    down, low = pl.pallas_call(
        edge_kernel,
        out_shape=(face, face),
        in_specs=whole(7),
        out_specs=tuple(whole(2)),
        compiler_params=params(8),
        cost_estimate=cost(1),
        name="edge",
    )(below_x, above_x, ydn, below_y, corner_below, corner_above, token)
    above_y = passed_along(down, 0, -1)
    ends = (3, tiles * BZ, NODES)
    inner, ends_out = pl.pallas_call(
        place_kernel,
        out_shape=(struct((3, EL, NODES), F32), struct(ends, F32)),
        in_specs=smem + whole(1) + [in_hbm, in_hbm] + whole(3),
        out_specs=(in_hbm, whole(1)[0]),
        scratch_shapes=[
            pltpu.VMEM((PEERS, 3 * COMP, LANES), F32),
            pltpu.VMEM((3, EL, NODES), F32),
            pltpu.VMEM((NODES, LANES), F32),
            pltpu.VMEM(ends, F32),
            pltpu.SemaphoreType.DMA((3, 2)),
            pltpu.SemaphoreType.DMA((3, tiles)),
        ],
        compiler_params=params(20),
        cost_estimate=cost(3),
        name="place",
    )(
        peers,
        slots,
        recv,
        pltpu.with_memory_space_constraint(base, pltpu.HBM),
        below_x,
        above_x,
        low,
    )
    out = pl.pallas_call(
        lines_kernel,
        out_shape=struct((3, EL, NODES), F32),
        in_specs=whole(2) + [anywhere],
        out_specs=anywhere,
        scratch_shapes=[
            pltpu.VMEM((NODES, LANES), F32),
            pltpu.VMEM(ends, F32),
            pltpu.SemaphoreType.DMA((3, tiles)),
        ],
        input_output_aliases={2: 0},
        compiler_params=params(10),
        cost_estimate=cost(1),
        name="lines",
    )(ends_out, above_y, inner)
    return jnp.transpose(out, (1, 0, 2)), particles_next


def solution(mesh):
    return jax.shard_map(
        body,
        mesh=mesh,
        in_specs=(P(AXES, None, None), P(AXES, None), P(AXES), P(AXES)),
        out_specs=(P(AXES, None, None), P(AXES, None)),
        check_vma=False,
    )
```

```python
import functools

import jax
import jax.numpy as jnp
import numpy as np
from jax import lax
from jax.experimental import pallas as pl
from jax.experimental.pallas import tpu as pltpu
from jax.sharding import PartitionSpec as P

NP = 8
SLOTS = 16
CAP = 4
PEERS = 64
BX = 4
BY = 8
BZ = 16
NODES = NP**3
EL = BX * BY * BZ
MOVERS = PEERS * CAP
LANES = 128
PARTS = 8 * SLOTS
HEAD = 6
COMP = 16
AXES = ("ex", "ey")
POINTS = [
    -1.0,
    -0.8717401485096066,
    -0.5917001814331423,
    -0.2092992179024789,
    0.2092992179024789,
    0.5917001814331423,
    0.8717401485096066,
    1.0,
]
F32 = jnp.float32
BF16 = jnp.bfloat16
MIB = 1024 * 1024


def iota(shape, axis):
    return lax.broadcasted_iota(jnp.int32, shape, axis)


def split(x):
    high = x.astype(BF16)
    return high, (x - high.astype(F32)).astype(BF16)


def picked(onehot, x):
    high, low = split(x)
    return jnp.dot(
        jnp.concatenate([onehot, onehot], axis=1),
        jnp.concatenate([high, low], axis=0),
        preferred_element_type=F32,
    )


def as_column(row):
    return jnp.broadcast_to(row, (LANES, EL)).T


def pack_positions(place, rank):
    target = place // EL
    moving = target != rank
    key = jnp.where(moving, target, -1).astype(F32)
    key_col = as_column(key)
    order = []
    for j in range(EL // LANES):
        piece = key[:, j * LANES : (j + 1) * LANES]
        earlier = iota((EL, LANES), 0) < iota((EL, LANES), 1) + j * LANES
        same = (key_col == piece) & earlier
        order.append(jnp.sum(same.astype(F32), axis=0, keepdims=True))
    order = jnp.concatenate(order, axis=1).astype(jnp.int32)
    return jnp.where(moving, target * CAP + order, -1)


def interleave(first, second):
    devices = first.shape[0] // CAP
    low = iota((devices // 2, 8, LANES), 1) < CAP
    first = first.reshape(devices // 2, 8, LANES)
    second = second.reshape(devices // 2, 8, LANES)
    even = jnp.where(low, first, pltpu.roll(second, CAP, 1))
    odd = jnp.where(low, pltpu.roll(first, CAP, 1), second)
    return jnp.stack([even, odd], axis=1).reshape(devices, 8, LANES)


def deinterleave(blocks):
    devices = blocks.shape[0]
    pairs = blocks.reshape(devices // 2, 2, 8, LANES)
    even, odd = pairs[:, 0], pairs[:, 1]
    low = iota((devices // 2, 8, LANES), 1) < CAP
    first = jnp.where(low, even, pltpu.roll(odd, CAP, 1))
    second = jnp.where(low, pltpu.roll(even, CAP, 1), odd)
    return first.reshape(devices * CAP, LANES), second.reshape(devices * CAP, LANES)


def picked_row(row, onehot):
    high, low = split(jnp.broadcast_to(row.astype(F32), (8, row.shape[1])))
    dims = (((1,), (1,)), ((), ()))
    out = lax.dot_general(high, onehot, dims, preferred_element_type=F32)
    out = out + lax.dot_general(low, onehot, dims, preferred_element_type=F32)
    return out[0:1]


def interp_kernel(moves, *refs):
    rank_ref, place_ref, count_ref, fields_ref, part_ref = refs[:5]
    out_refs = refs[5:7]
    tp_ref, push_ref, basis_ref, t_ref, work_ref, count_row_ref, held_ref = refs[7:14]
    place_held, count_held, part_held, arrived = refs[14:]
    tiles = MOVERS // LANES
    pairs = [(place_ref, place_held), (count_ref, count_held), (part_ref, part_held)]
    pairs += [(fields_ref.at[f], held_ref.at[f]) for f in range(3)]
    copies = [pltpu.make_async_copy(*pair, arrived.at[i]) for i, pair in enumerate(pairs)]
    for copy in copies:
        copy.start()
    earlier = (iota((EL, EL), 0) < iota((EL, EL), 1)).astype(BF16)
    copies[0].wait()
    place = place_held[...]
    moving = place // EL != rank_ref[0]
    chosen = moving if moves else jnp.logical_not(moving)
    order = jnp.dot(
        jnp.broadcast_to(chosen.astype(F32), (8, EL)).astype(BF16),
        earlier,
        preferred_element_type=F32,
    )[0:1]
    key = jnp.where(chosen, order.astype(jnp.int32), -1)
    onehot = (iota((MOVERS, EL), 0) == key).astype(BF16)
    copies[1].wait()
    count_row_ref[...] = picked_row(count_held[...], onehot).astype(jnp.int32)
    slot_row = picked_row(place % EL + 1, onehot)
    if moves:
        send_ref, position_ref = out_refs
        devices = send_ref.shape[0] // HEAD
        position = pack_positions(place, rank_ref[0])
        position_ref[...] = position
        goes_to = picked_row(position, onehot).astype(jnp.int32)
        goes_to = goes_to % CAP * devices + goes_to // CAP
        scatter = (iota((devices * CAP, MOVERS), 0) == goes_to).astype(BF16)
    copies[2].wait()
    records = picked(onehot, part_held[...])
    for t in range(tiles):
        tp_ref[t] = records[t * LANES : (t + 1) * LANES, :].T

    def make_basis(t, carry):
        for d in range(3):
            rows = lagrange_rows(tp_ref[t, d * SLOTS : (d + 1) * SLOTS, :])
            for n in range(NP):
                basis_ref[t, d, n * SLOTS : (n + 1) * SLOTS, :] = rows[n]
        return carry

    def gather(f):
        copies[3 + f].wait()
        rows = picked(onehot, held_ref[f])
        for t in range(tiles):
            for j in range(NODES // LANES):
                cols = slice(j * LANES, (j + 1) * LANES)
                t_ref[f, t, cols, :] = rows[t * LANES : (t + 1) * LANES, cols].T

    for t in range(tiles):
        make_basis(t, 0)
    gather(0)

    def step(t, f):
        def basis(which, n, p):
            return basis_ref[t, which, pl.ds(n * SLOTS + p, 1), :]

        total = [None] * SLOTS
        for pair in range(NP // 2):
            nodes = [
                [t_ref[f, t, pl.ds(a * 64 + (2 * pair + i) * 8, 8), :] for a in range(NP)]
                for i in range(2)
            ]
            for p in range(SLOTS):
                sums = [None, None]
                for a in range(NP):
                    weight = basis(0, a, p)
                    for i in range(2):
                        term = nodes[i][a] * weight
                        sums[i] = term if sums[i] is None else sums[i] + term
                for i in range(2):
                    term = sums[i] * basis(1, 2 * pair + i, p)
                    total[p] = term if total[p] is None else total[p] + term
        for p in range(SLOTS):
            along_z = basis_ref[t, 2, pl.ds(p, NP, stride=SLOTS), :]
            work_ref[p * NP : (p + 1) * NP, :] = total[p] * along_z
        fluid = work_ref[pl.ds(0, SLOTS, stride=NP), :]
        for c in range(1, NP):
            fluid = fluid + work_ref[pl.ds(c, SLOTS, stride=NP), :]
        where = pl.ds(pl.multiple_of((3 + f) * SLOTS, SLOTS), SLOTS)
        velocity = tp_ref[t, where, :]
        ratio = tp_ref[t, 6 * SLOTS : 7 * SLOTS, :]
        mass = tp_ref[t, 7 * SLOTS : 8 * SLOTS, :]
        count = count_row_ref[:, pl.ds(pl.multiple_of(t * LANES, LANES), LANES)]
        drag = jnp.where(iota((SLOTS, LANES), 0) < count, ratio * (fluid - velocity), 0.0)
        tp_ref[t, where, :] = velocity + drag
        push_ref[t, pl.ds(pl.multiple_of((1 + f) * SLOTS, SLOTS), SLOTS), :] = -(mass * drag)
        return f

    for f in range(3):
        if f:
            gather(f)
        lax.fori_loop(0, tiles, step, f)

    heads = []
    for t in range(tiles):
        rows = slice(t * LANES, (t + 1) * LANES)
        push_ref[t, 0:SLOTS, :] = jnp.broadcast_to(slot_row[:, rows], (SLOTS, LANES))
        push_ref[t, 4 * SLOTS :, :] = jnp.zeros((LANES - 4 * SLOTS, LANES), F32)
        heads.append(jnp.concatenate([tp_ref[t].T, push_ref[t].T], axis=1))
    head = jnp.concatenate(heads, axis=0)
    if moves:
        send_ref, position_ref = out_refs
        devices = send_ref.shape[0] // HEAD
        rows = picked(scatter, head)
        lane = iota((devices, LANES), 1)
        for q in range(CAP):
            mine = slice(q * devices, (q + 1) * devices)
            send_ref[pl.ds(q, devices, stride=HEAD), :] = rows[mine, :LANES]
            if q % 2:
                both = jnp.where(lane < LANES // 2, before, pltpu.roll(rows[mine, LANES:], LANES // 2, 1))
                send_ref[pl.ds(CAP + q // 2, devices, stride=HEAD), :] = both
            before = rows[mine, LANES:]
    else:
        head_ref, slot_ref = out_refs
        head_ref[...] = head
        slot_ref[...] = slot_row.astype(jnp.int32)


def pack_kernel(position_ref, fields_ref, out_ref):
    devices = out_ref.shape[0]
    onehot = (iota((devices * CAP, EL), 0) == position_ref[...]).astype(BF16)
    for f in range(3):
        rows = picked(onehot, fields_ref[f])
        for h in range(2):
            at = COMP * f + 8 * h
            left = 2 * h * LANES
            out_ref[:, at : at + 8, :] = interleave(
                rows[:, left : left + LANES], rows[:, left + LANES : left + 2 * LANES]
            )


def lagrange_rows(coord):
    diffs = [coord - p for p in POINTS]
    left = [None] * NP
    right = [None] * NP
    for i in range(1, NP):
        left[i] = diffs[i - 1] if i == 1 else left[i - 1] * diffs[i - 1]
    for i in range(NP - 2, -1, -1):
        right[i] = diffs[i + 1] if i == NP - 2 else right[i + 1] * diffs[i + 1]
    out = []
    for i in range(NP):
        scale = 1.0
        for m in range(NP):
            if m != i:
                scale /= POINTS[i] - POINTS[m]
        if i == 0:
            term = right[0]
        elif i == NP - 1:
            term = left[i]
        else:
            term = left[i] * right[i]
        out.append(term * float(scale))
    return out


def gaussian_rows(coord):
    return [jnp.exp(-((p - coord) ** 2) * (0.5 / 0.35**2)) for p in POINTS]


def shift_z(x):
    n = x.shape[0] // NP
    x = x.reshape(n, NP, LANES)
    node = iota((n, NP, LANES), 1)
    bz = iota((n, NP, LANES), 2) % BZ
    down = pltpu.roll(pltpu.roll(x, 1, 1), 1, 2)
    up = pltpu.roll(pltpu.roll(x, NP - 1, 1), LANES - 1, 2)
    x = x + jnp.where((node == 0) & (bz > 0), down, 0.0)
    x = x + jnp.where((node == NP - 1) & (bz < BZ - 1), up, 0.0)
    return x.reshape(n * NP, LANES)


def force_kernel(
    head_ref,
    stay_slot_ref,
    recv_ref,
    force_ref,
    xup_ref,
    xdn_ref,
    yup_ref,
    ydn_ref,
    left_ref,
    right_ref,
    part_ref,
    slot_ref,
    peers_ref,
    tp_ref,
    push_ref,
    basis_ref,
    work_ref,
):
    tiles = EL // LANES
    devices = recv_ref.shape[0] // HEAD
    particles, extra = [], []
    for q in range(CAP):
        particles.append(recv_ref[pl.ds(q, devices, stride=HEAD), :])
        both = recv_ref[pl.ds(CAP + q // 2, devices, stride=HEAD), :]
        extra.append(pltpu.roll(both, LANES // 2, 1) if q % 2 else both)
    particles = jnp.concatenate(particles, axis=0)
    extra = jnp.concatenate(extra, axis=0)
    slot_row = extra.T[0:1, :].astype(jnp.int32)
    at = iota((devices * CAP, devices * CAP), 0)
    turned = at // devices + at % devices * CAP == iota((devices * CAP, devices * CAP), 1)
    high, low = split(jnp.broadcast_to(slot_row.astype(F32), (8, devices * CAP)))
    order = turned.astype(BF16)
    row = jnp.dot(high, order, preferred_element_type=F32)
    row = row + jnp.dot(low, order, preferred_element_type=F32)
    row = row[0:1].astype(jnp.int32)
    filled = row > 0
    earlier = (iota((devices * CAP, devices * CAP), 0) < iota((devices * CAP, devices * CAP), 1)).astype(BF16)
    rank = jnp.dot(
        jnp.broadcast_to(filled.astype(F32), (8, devices * CAP)).astype(BF16),
        earlier,
        preferred_element_type=F32,
    )[0:1]
    key = jnp.where(filled, rank.astype(jnp.int32), -1)
    packed = (iota((MOVERS, devices * CAP), 0) == key).astype(BF16)
    slot_ref[...] = picked_row(row, packed).astype(jnp.int32)
    peers_ref[...] = picked_row(iota((1, devices * CAP), 1) // CAP, packed).astype(jnp.int32)
    slots = jnp.concatenate([slot_row, stay_slot_ref[...]], axis=1)
    onehot = (iota((EL, EL + MOVERS), 0) + 1 == slots).astype(BF16)
    arrived = jnp.concatenate([particles, extra], axis=1)
    both = picked(onehot, jnp.concatenate([arrived, head_ref[...]], axis=0))
    record = both[:, :LANES]
    push = both[:, LANES:]
    part_ref[...] = record
    for t in range(tiles):
        rows = slice(t * LANES, (t + 1) * LANES)
        tp_ref[t] = record[rows].T
        push_ref[t] = push[rows].T

    def make_basis(t, carry):
        for d in range(3):
            rows = gaussian_rows(tp_ref[t, d * SLOTS : (d + 1) * SLOTS, :])
            for n in range(NP):
                basis_ref[t, d, n * SLOTS : (n + 1) * SLOTS, :] = rows[n]
        return carry

    lax.fori_loop(0, tiles, make_basis, 0)

    def step(index, carry):
        f = index // tiles
        t = index % tiles

        def basis(which, n, p):
            return basis_ref[t, which, pl.ds(n * SLOTS + p, 1), :]

        for p in range(SLOTS):
            along_z = basis_ref[t, 2, pl.ds(p, NP, stride=SLOTS), :]
            value = push_ref[t, pl.ds((1 + f) * SLOTS + p, 1), :]
            work_ref[p * NP : (p + 1) * NP, :] = (0.5 * value) * along_z
        for pair in range(NP // 2):
            acc = [[None] * NP for _ in range(2)]
            for p in range(SLOTS):
                base = work_ref[p * NP : (p + 1) * NP, :]
                lines = [base * basis(1, 2 * pair + i, p) for i in range(2)]
                for a in range(NP):
                    weight = basis(0, a, p)
                    for i in range(2):
                        term = lines[i] * weight
                        acc[i][a] = term if acc[i][a] is None else acc[i][a] + term
            for i in range(2):
                for a in range(NP):
                    force_ref[f, t, pl.ds(a * 64 + (2 * pair + i) * 8, 8), :] = acc[i][a]
        return carry

    lax.fori_loop(0, 3 * tiles, step, 0)

    lane = iota((NP, LANES), 1)
    bz = iota((64, LANES), 1) % BZ
    for f in range(3):
        xup_ref[f] = force_ref[f, tiles - 1, 448:512, :]
        xdn_ref[f] = force_ref[f, 0, 0:64, :]
        left_ref[f] = pltpu.roll(force_ref[f, tiles - 1, 504:512, :], BZ, 1)
        right_ref[f] = pltpu.roll(force_ref[f, 0, 56:64, :], BZ, 1)
        for t in range(tiles - 1):
            summed = force_ref[f, t, 448:512, :] + force_ref[f, t + 1, 0:64, :]
            force_ref[f, t, 448:512, :] = summed
            force_ref[f, t + 1, 0:64, :] = summed
        for a in range(NP):
            first = slice(a * 64, a * 64 + 8)
            last = slice(a * 64 + 56, a * 64 + 64)
            up_line = jnp.zeros((NP, LANES), F32)
            down_line = jnp.zeros((NP, LANES), F32)
            for t in range(tiles):
                upper = force_ref[f, t, last, :]
                lower = force_ref[f, t, first, :]
                take = lane // BZ == t
                up_line = jnp.where(take, pltpu.roll(upper, 16 * t + 16, 1), up_line)
                moved = pltpu.roll(lower, 16 * t, 1) if t else lower
                down_line = jnp.where(take, moved, down_line)
                force_ref[f, t, first, :] = lower + jnp.where(
                    lane >= BZ, pltpu.roll(upper, BZ, 1), 0.0
                )
                force_ref[f, t, last, :] = upper + jnp.where(
                    lane < LANES - BZ, pltpu.roll(lower, LANES - BZ, 1), 0.0
                )
            yup_ref[f, a * 8 : a * 8 + 8, :] = up_line
            ydn_ref[f, a * 8 : a * 8 + 8, :] = down_line
        for t in range(tiles):
            lower = force_ref[f, t, pl.ds(0, 64, stride=NP), :]
            upper = force_ref[f, t, pl.ds(NP - 1, 64, stride=NP), :]
            force_ref[f, t, pl.ds(0, 64, stride=NP), :] = lower + jnp.where(
                bz > 0, pltpu.roll(upper, 1, 1), 0.0
            )
            force_ref[f, t, pl.ds(NP - 1, 64, stride=NP), :] = upper + jnp.where(
                bz < BZ - 1, pltpu.roll(lower, LANES - 1, 1), 0.0
            )


def edge_kernel(below_ref, above_ref, ydn_ref, yb_ref, cb_ref, ca_ref, token_ref, down_ref, low_ref):
    lane = iota((NP, LANES), 1)
    first = lane < BZ
    last = (lane >= 3 * BZ) & (lane < 4 * BZ)
    for f in range(3):
        down_ref[f] = ydn_ref[f]
        down_ref[f, 0:8, :] += jnp.where(first, below_ref[f, 0:8, :], 0.0)
        down_ref[f, 56:64, :] += jnp.where(last, pltpu.roll(above_ref[f, 0:8, :], 3 * BZ, 1), 0.0)
        low_ref[f] = yb_ref[f]
        low_ref[f, 0:8, :] += jnp.where(first, cb_ref[f], 0.0)
        low_ref[f, 56:64, :] += jnp.where(last, pltpu.roll(ca_ref[f], 3 * BZ, 1), 0.0)


def face_delta(face):
    lane = iota((NP, LANES), 1)
    upper = face[56:64]
    lower = face[0:8]
    new_lower = lower + jnp.where(lane >= BZ, pltpu.roll(upper, BZ, 1), 0.0)
    new_upper = upper + jnp.where(lane < LANES - BZ, pltpu.roll(lower, LANES - BZ, 1), 0.0)
    return shift_z(0.5 * jnp.concatenate([new_lower, face[8:56], new_upper], axis=0))


def face_delta(face):
    lane = iota((NP, LANES), 1)
    upper = face[56:64]
    lower = face[0:8]
    new_lower = lower + jnp.where(lane >= BZ, pltpu.roll(upper, BZ, 1), 0.0)
    new_upper = upper + jnp.where(lane < LANES - BZ, pltpu.roll(lower, LANES - BZ, 1), 0.0)
    return shift_z(jnp.concatenate([new_lower, face[8:56], new_upper], axis=0))


def base_kernel(rank_ref, place_ref, fields_ref, force_ref, out_ref, token_ref):
    tiles = EL // LANES
    stay_col = as_column((place_ref[...] // EL == rank_ref[0]).astype(F32)) > 0
    for f in range(3):
        for t in range(tiles):
            rows = slice(t * LANES, (t + 1) * LANES)
            for j in range(NODES // LANES):
                cols = slice(j * LANES, (j + 1) * LANES)
                own = jnp.where(stay_col[rows], fields_ref[f, rows, cols], 0.0)
                out_ref[f, rows, cols] = own + force_ref[f, t, cols, :].T
    token_ref[...] = jnp.zeros((8, LANES), F32)


def lines_of(values, node, line_ref):
    values = shift_z(jnp.where(iota((64, LANES), 1) < BX * BZ, values, 0.0))
    for a in range(NP):
        at = a * 64 + node * 8
        line_ref[at : at + 8, :] = values[a * 8 : a * 8 + 8]
    cols = [line_ref[j * LANES : (j + 1) * LANES, :].T for j in range(NODES // LANES)]
    return jnp.concatenate(cols, axis=1)[: BX * BZ]


def place_kernel(
    peers_ref,
    slot_ref,
    recv_ref,
    base_ref,
    xb_ref,
    xa_ref,
    low_ref,
    out_ref,
    ends_ref,
    recv_held,
    held_ref,
    line_ref,
    lows_ref,
    arrived,
    left,
):
    tiles = EL // LANES

    peers = peers_ref[...]
    for c in range(PEERS):
        block = recv_ref.at[peers[0, CAP * c]]
        pltpu.make_async_copy(block, recv_held.at[c], arrived.at[0, 0]).start()
    whole_recv = pltpu.make_async_copy(recv_ref.at[pl.ds(0, PEERS)], recv_held, arrived.at[0, 0])
    loads = []
    for f in range(3):
        loads.append(pltpu.make_async_copy(base_ref.at[f], held_ref.at[f], arrived.at[f, 1]))
        loads[f].start()
    onehot = (iota((EL, MOVERS), 0) + 1 == slot_ref[...]).astype(BF16)
    blank = jnp.zeros((64, LANES), F32)
    line_ref[...] = jnp.zeros((NODES, LANES), F32)
    for f in range(3):
        lows_ref[f] = lines_of(low_ref[f], 0, line_ref)
    copies = []
    for f in range(3):
        if f == 0:
            whole_recv.wait()
        pieces = []
        for h in range(2):
            pieces += list(deinterleave(recv_held[:, COMP * f + 8 * h : COMP * f + 8 * h + 8, :]))
        rows = picked(onehot, jnp.concatenate(pieces, axis=1))
        loads[f].wait()
        held_ref[f] += rows
        delta = jnp.concatenate([face_delta(xb_ref[f]), blank], axis=0)
        held_ref[f, 0:LANES, 0:LANES] += delta.T
        delta = jnp.concatenate([blank, face_delta(xa_ref[f])], axis=0)
        held_ref[f, EL - LANES :, NODES - LANES :] += delta.T
        for t in range(tiles):
            mine = slice(t * BZ, (t + 1) * BZ)
            held_ref[f, t * LANES : t * LANES + BZ, :] += lows_ref[f, mine, :]
            inner = pl.ds(t * LANES, LANES - BZ)
            copies.append(
                pltpu.make_async_copy(held_ref.at[f, inner], out_ref.at[f, inner], left.at[f, t])
            )
            copies[-1].start()
            last = (t + 1) * LANES
            ends_ref[f, mine, :] = held_ref[f, last - BZ : last, :]
    for copy in copies:
        copy.wait()


def lines_kernel(ends_ref, ya_ref, inner_ref, out_ref, line_ref, held_ref, left):
    tiles = EL // LANES
    line_ref[...] = jnp.zeros((NODES, LANES), F32)
    copies = []
    for f in range(3):
        held_ref[f] = ends_ref[f] + lines_of(ya_ref[f], NP - 1, line_ref)
        for t in range(tiles):
            at = pl.ds((t + 1) * LANES - BZ, BZ)
            mine = pl.ds(t * BZ, BZ)
            copies.append(
                pltpu.make_async_copy(held_ref.at[f, mine], out_ref.at[f, at], left.at[f, t])
            )
            copies[-1].start()
    for copy in copies:
        copy.wait()


def passed_along(x, along_ex, along_ey):
    rows, cols = lax.axis_size("ex"), lax.axis_size("ey")
    pairs = []
    for i in range(rows):
        for j in range(cols):
            to_i, to_j = i + along_ex, j + along_ey
            if 0 <= to_i < rows and 0 <= to_j < cols:
                pairs.append((i * cols + j, to_i * cols + to_j))
    return lax.ppermute(x, AXES, pairs)


def whole(n):
    return [pl.BlockSpec(memory_space=pltpu.VMEM)] * n


def params(mib):
    return pltpu.CompilerParams(vmem_limit_bytes=mib * MIB)


def cost(micros):
    return pl.CostEstimate(flops=0, bytes_accessed=int(micros * 3_000_000), transcendentals=0)


def body(fields, particles, counts, new_place):
    devices = lax.axis_size(AXES)
    rank = lax.axis_index(AXES).astype(jnp.int32).reshape(1)
    fields = jnp.transpose(fields, (1, 0, 2))
    place = new_place.reshape(1, EL)
    counts = counts.reshape(1, EL)
    smem = [pl.BlockSpec(memory_space=pltpu.SMEM)]
    anywhere = pl.BlockSpec(memory_space=pl.ANY)
    in_hbm = pl.BlockSpec(memory_space=pltpu.HBM)
    struct = jax.ShapeDtypeStruct
    tiles = EL // LANES
    tile_scratch = pltpu.VMEM((tiles, LANES, LANES), F32)
    basis_scratch = pltpu.VMEM((tiles, 3, LANES, LANES), F32)
    work_scratch = pltpu.VMEM((LANES, LANES), F32)
    half = MOVERS // LANES

    def interp(moves, out_shape, mib, name):
        return pl.pallas_call(
            functools.partial(interp_kernel, moves),
            out_shape=out_shape,
            in_specs=smem + [anywhere] * 4,
            out_specs=tuple(whole(2)),
            scratch_shapes=[
                pltpu.VMEM((half, LANES, LANES), F32),
                pltpu.VMEM((half, LANES, LANES), F32),
                pltpu.VMEM((half, 3, LANES, LANES), F32),
                pltpu.VMEM((3, half, NODES, LANES), F32),
                work_scratch,
                pltpu.VMEM((1, MOVERS), jnp.int32),
                pltpu.VMEM((3, EL, NODES), F32),
                pltpu.VMEM((1, EL), jnp.int32),
                pltpu.VMEM((1, EL), jnp.int32),
                pltpu.VMEM((EL, PARTS), F32),
                pltpu.SemaphoreType.DMA((6,)),
            ],
            compiler_params=params(mib),
            cost_estimate=cost(6),
            name=name,
        )(rank, place, counts, fields, particles)

    send_head, position = interp(
        True, (struct((devices * HEAD, LANES), F32), struct((1, EL), jnp.int32)), 58, "moving"
    )
    head, stay_slots = interp(
        False, (struct((MOVERS, 2 * LANES), F32), struct((1, MOVERS), jnp.int32)), 40, "staying"
    )
    recv_head = lax.all_to_all(send_head.reshape(-1), AXES, split_axis=0, concat_axis=0, tiled=True)
    recv_head = recv_head.reshape(devices * HEAD, LANES)
    send = pl.pallas_call(
        pack_kernel,
        out_shape=struct((devices, 3 * COMP, LANES), F32),
        in_specs=whole(2),
        out_specs=whole(1)[0],
        compiler_params=params(58),
        cost_estimate=cost(5),
        name="pack",
    )(position, fields)
    recv = lax.all_to_all(send, AXES, split_axis=0, concat_axis=0, tiled=True)
    face = struct((3, 64, LANES), F32)
    corner = struct((3, NP, LANES), F32)
    force, xup, xdn, yup, ydn, left, right, particles_next, slots, peers = pl.pallas_call(
        force_kernel,
        out_shape=(
            struct((3, tiles, NODES, LANES), F32),
            face,
            face,
            face,
            face,
            corner,
            corner,
            struct((EL, PARTS), F32),
            struct((1, MOVERS), jnp.int32),
            struct((1, MOVERS), jnp.int32),
        ),
        in_specs=whole(3),
        out_specs=tuple(whole(10)),
        scratch_shapes=[tile_scratch, tile_scratch, basis_scratch, work_scratch],
        compiler_params=params(40),
        cost_estimate=cost(8),
        name="force",
    )(head, stay_slots, recv_head)
    base, token = pl.pallas_call(
        base_kernel,
        out_shape=(pltpu.HBM((3, EL, NODES), F32), struct((8, LANES), F32)),
        in_specs=smem + whole(3),
        out_specs=tuple(whole(2)),
        compiler_params=params(20),
        cost_estimate=cost(5),
        name="base",
    )(rank, place, fields, force)
    below_x = passed_along(xup, 1, 0)
    above_x = passed_along(xdn, -1, 0)
    below_y = passed_along(yup, 0, 1)
    corner_below = passed_along(left, 1, 1)
    corner_above = passed_along(right, -1, 1)
    down, low = pl.pallas_call(
        edge_kernel,
        out_shape=(face, face),
        in_specs=whole(7),
        out_specs=tuple(whole(2)),
        compiler_params=params(8),
        cost_estimate=cost(1),
        name="edge",
    )(below_x, above_x, ydn, below_y, corner_below, corner_above, token)
    above_y = passed_along(down, 0, -1)
    ends = (3, tiles * BZ, NODES)
    inner, ends_out = pl.pallas_call(
        place_kernel,
        out_shape=(struct((3, EL, NODES), F32), struct(ends, F32)),
        in_specs=whole(2) + [in_hbm, in_hbm] + whole(3),
        out_specs=(in_hbm, whole(1)[0]),
        scratch_shapes=[
            pltpu.VMEM((PEERS, 3 * COMP, LANES), F32),
            pltpu.VMEM((3, EL, NODES), F32),
            pltpu.VMEM((NODES, LANES), F32),
            pltpu.VMEM(ends, F32),
            pltpu.SemaphoreType.DMA((3, 2)),
            pltpu.SemaphoreType.DMA((3, tiles)),
        ],
        compiler_params=params(20),
        cost_estimate=cost(3),
        name="place",
    )(
        peers,
        slots,
        recv,
        pltpu.with_memory_space_constraint(base, pltpu.HBM),
        below_x,
        above_x,
        low,
    )
    out = pl.pallas_call(
        lines_kernel,
        out_shape=struct((3, EL, NODES), F32),
        in_specs=whole(2) + [anywhere],
        out_specs=anywhere,
        scratch_shapes=[
            pltpu.VMEM((NODES, LANES), F32),
            pltpu.VMEM(ends, F32),
            pltpu.SemaphoreType.DMA((3, tiles)),
        ],
        input_output_aliases={2: 0},
        compiler_params=params(10),
        cost_estimate=cost(1),
        name="lines",
    )(ends_out, above_y, inner)
    return jnp.transpose(out, (1, 0, 2)), particles_next


def solution(mesh):
    return jax.shard_map(
        body,
        mesh=mesh,
        in_specs=(P(AXES, None, None), P(AXES, None), P(AXES), P(AXES)),
        out_specs=(P(AXES, None, None), P(AXES, None)),
        check_vma=False,
    )
```

```python
import functools

import jax
import jax.numpy as jnp
import numpy as np
from jax import lax
from jax.experimental import pallas as pl
from jax.experimental.pallas import tpu as pltpu
from jax.sharding import PartitionSpec as P

NP = 8
SLOTS = 16
CAP = 4
PEERS = 64
N_EX = 16
N_EY = 8
ORDER = ("ey", "ex")
BX = 4
BY = 8
BZ = 16
NODES = NP**3
EL = BX * BY * BZ
MOVERS = PEERS * CAP
LANES = 128
PARTS = 8 * SLOTS
HEAD = 6
COMP = 16
AXES = ("ex", "ey")
POINTS = [
    -1.0,
    -0.8717401485096066,
    -0.5917001814331423,
    -0.2092992179024789,
    0.2092992179024789,
    0.5917001814331423,
    0.8717401485096066,
    1.0,
]
F32 = jnp.float32
BF16 = jnp.bfloat16
MIB = 1024 * 1024


def iota(shape, axis):
    return lax.broadcasted_iota(jnp.int32, shape, axis)


def split(x):
    high = x.astype(BF16)
    return high, (x - high.astype(F32)).astype(BF16)


def picked(onehot, x):
    high, low = split(x)
    return jnp.dot(
        jnp.concatenate([onehot, onehot], axis=1),
        jnp.concatenate([high, low], axis=0),
        preferred_element_type=F32,
    )


def as_column(row):
    return jnp.broadcast_to(row, (LANES, EL)).T


def pack_positions(place, rank):
    target = place // EL
    moving = target != rank
    key = jnp.where(moving, target, -1).astype(F32)
    key_col = as_column(key)
    order = []
    for j in range(EL // LANES):
        piece = key[:, j * LANES : (j + 1) * LANES]
        earlier = iota((EL, LANES), 0) < iota((EL, LANES), 1) + j * LANES
        same = (key_col == piece) & earlier
        order.append(jnp.sum(same.astype(F32), axis=0, keepdims=True))
    order = jnp.concatenate(order, axis=1).astype(jnp.int32)
    block = target % N_EY * N_EX + target // N_EY
    return jnp.where(moving, block * CAP + order, -1)


def interleave(first, second):
    devices = first.shape[0] // CAP
    low = iota((devices // 2, 8, LANES), 1) < CAP
    first = first.reshape(devices // 2, 8, LANES)
    second = second.reshape(devices // 2, 8, LANES)
    even = jnp.where(low, first, pltpu.roll(second, CAP, 1))
    odd = jnp.where(low, pltpu.roll(first, CAP, 1), second)
    return jnp.stack([even, odd], axis=1).reshape(devices, 8, LANES)


def deinterleave(blocks):
    devices = blocks.shape[0]
    pairs = blocks.reshape(devices // 2, 2, 8, LANES)
    even, odd = pairs[:, 0], pairs[:, 1]
    low = iota((devices // 2, 8, LANES), 1) < CAP
    first = jnp.where(low, even, pltpu.roll(odd, CAP, 1))
    second = jnp.where(low, pltpu.roll(even, CAP, 1), odd)
    return first.reshape(devices * CAP, LANES), second.reshape(devices * CAP, LANES)


def picked_row(row, onehot):
    high, low = split(jnp.broadcast_to(row.astype(F32), (8, row.shape[1])))
    dims = (((1,), (1,)), ((), ()))
    out = lax.dot_general(high, onehot, dims, preferred_element_type=F32)
    out = out + lax.dot_general(low, onehot, dims, preferred_element_type=F32)
    return out[0:1]


def interp_kernel(moves, *refs):
    rank_ref, place_ref, count_ref, fields_ref, part_ref = refs[:5]
    out_refs = refs[5:7]
    tp_ref, push_ref, basis_ref, t_ref, work_ref, count_row_ref, held_ref = refs[7:14]
    place_held, count_held, part_held, arrived = refs[14:]
    tiles = MOVERS // LANES
    pairs = [(place_ref, place_held), (count_ref, count_held), (part_ref, part_held)]
    pairs += [(fields_ref.at[f], held_ref.at[f]) for f in range(3)]
    copies = [pltpu.make_async_copy(*pair, arrived.at[i]) for i, pair in enumerate(pairs)]
    for copy in copies:
        copy.start()
    earlier = (iota((EL, EL), 0) < iota((EL, EL), 1)).astype(BF16)
    copies[0].wait()
    place = place_held[...]
    moving = place // EL != rank_ref[0]
    chosen = moving if moves else jnp.logical_not(moving)
    order = jnp.dot(
        jnp.broadcast_to(chosen.astype(F32), (8, EL)).astype(BF16),
        earlier,
        preferred_element_type=F32,
    )[0:1]
    key = jnp.where(chosen, order.astype(jnp.int32), -1)
    onehot = (iota((MOVERS, EL), 0) == key).astype(BF16)
    copies[1].wait()
    count_row_ref[...] = picked_row(count_held[...], onehot).astype(jnp.int32)
    slot_row = picked_row(place % EL + 1, onehot)
    if moves:
        send_ref, position_ref = out_refs
        devices = send_ref.shape[0] // HEAD
        position = pack_positions(place, rank_ref[0])
        position_ref[...] = position
        goes_to = picked_row(position, onehot).astype(jnp.int32)
        goes_to = goes_to % CAP * devices + goes_to // CAP
        scatter = (iota((devices * CAP, MOVERS), 0) == goes_to).astype(BF16)
    copies[2].wait()
    records = picked(onehot, part_held[...])
    for t in range(tiles):
        tp_ref[t] = records[t * LANES : (t + 1) * LANES, :].T

    def make_basis(t, carry):
        for d in range(3):
            rows = lagrange_rows(tp_ref[t, d * SLOTS : (d + 1) * SLOTS, :])
            for n in range(NP):
                basis_ref[t, d, n * SLOTS : (n + 1) * SLOTS, :] = rows[n]
        return carry

    def gather(f):
        copies[3 + f].wait()
        rows = picked(onehot, held_ref[f])
        for t in range(tiles):
            for j in range(NODES // LANES):
                cols = slice(j * LANES, (j + 1) * LANES)
                t_ref[f, t, cols, :] = rows[t * LANES : (t + 1) * LANES, cols].T

    for t in range(tiles):
        make_basis(t, 0)
    gather(0)

    def step(t, f):
        def basis(which, n, p):
            return basis_ref[t, which, pl.ds(n * SLOTS + p, 1), :]

        total = [None] * SLOTS
        for pair in range(NP // 2):
            nodes = [
                [t_ref[f, t, pl.ds(a * 64 + (2 * pair + i) * 8, 8), :] for a in range(NP)]
                for i in range(2)
            ]
            for p in range(SLOTS):
                sums = [None, None]
                for a in range(NP):
                    weight = basis(0, a, p)
                    for i in range(2):
                        term = nodes[i][a] * weight
                        sums[i] = term if sums[i] is None else sums[i] + term
                for i in range(2):
                    term = sums[i] * basis(1, 2 * pair + i, p)
                    total[p] = term if total[p] is None else total[p] + term
        for p in range(SLOTS):
            along_z = basis_ref[t, 2, pl.ds(p, NP, stride=SLOTS), :]
            work_ref[p * NP : (p + 1) * NP, :] = total[p] * along_z
        fluid = work_ref[pl.ds(0, SLOTS, stride=NP), :]
        for c in range(1, NP):
            fluid = fluid + work_ref[pl.ds(c, SLOTS, stride=NP), :]
        where = pl.ds(pl.multiple_of((3 + f) * SLOTS, SLOTS), SLOTS)
        velocity = tp_ref[t, where, :]
        ratio = tp_ref[t, 6 * SLOTS : 7 * SLOTS, :]
        mass = tp_ref[t, 7 * SLOTS : 8 * SLOTS, :]
        count = count_row_ref[:, pl.ds(pl.multiple_of(t * LANES, LANES), LANES)]
        drag = jnp.where(iota((SLOTS, LANES), 0) < count, ratio * (fluid - velocity), 0.0)
        tp_ref[t, where, :] = velocity + drag
        push_ref[t, pl.ds(pl.multiple_of((1 + f) * SLOTS, SLOTS), SLOTS), :] = -(mass * drag)
        return f

    for f in range(3):
        if f:
            gather(f)
        lax.fori_loop(0, tiles, step, f)

    heads = []
    for t in range(tiles):
        rows = slice(t * LANES, (t + 1) * LANES)
        push_ref[t, 0:SLOTS, :] = jnp.broadcast_to(slot_row[:, rows], (SLOTS, LANES))
        push_ref[t, 4 * SLOTS :, :] = jnp.zeros((LANES - 4 * SLOTS, LANES), F32)
        heads.append(jnp.concatenate([tp_ref[t].T, push_ref[t].T], axis=1))
    head = jnp.concatenate(heads, axis=0)
    if moves:
        send_ref, position_ref = out_refs
        devices = send_ref.shape[0] // HEAD
        rows = picked(scatter, head)
        lane = iota((devices, LANES), 1)
        for q in range(CAP):
            mine = slice(q * devices, (q + 1) * devices)
            send_ref[pl.ds(q, devices, stride=HEAD), :] = rows[mine, :LANES]
            if q % 2:
                both = jnp.where(lane < LANES // 2, before, pltpu.roll(rows[mine, LANES:], LANES // 2, 1))
                send_ref[pl.ds(CAP + q // 2, devices, stride=HEAD), :] = both
            before = rows[mine, LANES:]
    else:
        head_ref, slot_ref = out_refs
        head_ref[...] = head
        slot_ref[...] = slot_row.astype(jnp.int32)


def pack_kernel(position_ref, fields_ref, out_ref):
    devices = out_ref.shape[0]
    onehot = (iota((devices * CAP, EL), 0) == position_ref[...]).astype(BF16)
    for f in range(3):
        rows = picked(onehot, fields_ref[f])
        for h in range(2):
            at = COMP * f + 8 * h
            left = 2 * h * LANES
            out_ref[:, at : at + 8, :] = interleave(
                rows[:, left : left + LANES], rows[:, left + LANES : left + 2 * LANES]
            )


def lagrange_rows(coord):
    diffs = [coord - p for p in POINTS]
    left = [None] * NP
    right = [None] * NP
    for i in range(1, NP):
        left[i] = diffs[i - 1] if i == 1 else left[i - 1] * diffs[i - 1]
    for i in range(NP - 2, -1, -1):
        right[i] = diffs[i + 1] if i == NP - 2 else right[i + 1] * diffs[i + 1]
    out = []
    for i in range(NP):
        scale = 1.0
        for m in range(NP):
            if m != i:
                scale /= POINTS[i] - POINTS[m]
        if i == 0:
            term = right[0]
        elif i == NP - 1:
            term = left[i]
        else:
            term = left[i] * right[i]
        out.append(term * float(scale))
    return out


def gaussian_rows(coord):
    return [jnp.exp(-((p - coord) ** 2) * (0.5 / 0.35**2)) for p in POINTS]


def shift_z(x):
    n = x.shape[0] // NP
    x = x.reshape(n, NP, LANES)
    node = iota((n, NP, LANES), 1)
    bz = iota((n, NP, LANES), 2) % BZ
    down = pltpu.roll(pltpu.roll(x, 1, 1), 1, 2)
    up = pltpu.roll(pltpu.roll(x, NP - 1, 1), LANES - 1, 2)
    x = x + jnp.where((node == 0) & (bz > 0), down, 0.0)
    x = x + jnp.where((node == NP - 1) & (bz < BZ - 1), up, 0.0)
    return x.reshape(n * NP, LANES)


def force_kernel(
    head_ref,
    stay_slot_ref,
    recv_ref,
    force_ref,
    xup_ref,
    xdn_ref,
    yup_ref,
    ydn_ref,
    left_ref,
    right_ref,
    part_ref,
    slot_ref,
    peers_ref,
    tp_ref,
    push_ref,
    basis_ref,
    work_ref,
):
    tiles = EL // LANES
    devices = recv_ref.shape[0] // HEAD
    particles, extra = [], []
    for q in range(CAP):
        particles.append(recv_ref[pl.ds(q, devices, stride=HEAD), :])
        both = recv_ref[pl.ds(CAP + q // 2, devices, stride=HEAD), :]
        extra.append(pltpu.roll(both, LANES // 2, 1) if q % 2 else both)
    particles = jnp.concatenate(particles, axis=0)
    extra = jnp.concatenate(extra, axis=0)
    slot_row = extra.T[0:1, :].astype(jnp.int32)
    at = iota((devices * CAP, devices * CAP), 0)
    turned = at // devices + at % devices * CAP == iota((devices * CAP, devices * CAP), 1)
    high, low = split(jnp.broadcast_to(slot_row.astype(F32), (8, devices * CAP)))
    order = turned.astype(BF16)
    row = jnp.dot(high, order, preferred_element_type=F32)
    row = row + jnp.dot(low, order, preferred_element_type=F32)
    row = row[0:1].astype(jnp.int32)
    filled = row > 0
    earlier = (iota((devices * CAP, devices * CAP), 0) < iota((devices * CAP, devices * CAP), 1)).astype(BF16)
    rank = jnp.dot(
        jnp.broadcast_to(filled.astype(F32), (8, devices * CAP)).astype(BF16),
        earlier,
        preferred_element_type=F32,
    )[0:1]
    key = jnp.where(filled, rank.astype(jnp.int32), -1)
    packed = (iota((MOVERS, devices * CAP), 0) == key).astype(BF16)
    slot_ref[...] = picked_row(row, packed).astype(jnp.int32)
    peers_ref[...] = picked_row(iota((1, devices * CAP), 1) // CAP, packed).astype(jnp.int32)
    slots = jnp.concatenate([slot_row, stay_slot_ref[...]], axis=1)
    onehot = (iota((EL, EL + MOVERS), 0) + 1 == slots).astype(BF16)
    arrived = jnp.concatenate([particles, extra], axis=1)
    both = picked(onehot, jnp.concatenate([arrived, head_ref[...]], axis=0))
    record = both[:, :LANES]
    push = both[:, LANES:]
    part_ref[...] = record
    for t in range(tiles):
        rows = slice(t * LANES, (t + 1) * LANES)
        tp_ref[t] = record[rows].T
        push_ref[t] = push[rows].T

    def make_basis(t, carry):
        for d in range(3):
            rows = gaussian_rows(tp_ref[t, d * SLOTS : (d + 1) * SLOTS, :])
            for n in range(NP):
                basis_ref[t, d, n * SLOTS : (n + 1) * SLOTS, :] = rows[n]
        return carry

    lax.fori_loop(0, tiles, make_basis, 0)

    def step(index, carry):
        f = index // tiles
        t = index % tiles

        def basis(which, n, p):
            return basis_ref[t, which, pl.ds(n * SLOTS + p, 1), :]

        for p in range(SLOTS):
            along_z = basis_ref[t, 2, pl.ds(p, NP, stride=SLOTS), :]
            value = push_ref[t, pl.ds((1 + f) * SLOTS + p, 1), :]
            work_ref[p * NP : (p + 1) * NP, :] = (0.5 * value) * along_z
        for pair in range(NP // 2):
            acc = [[None] * NP for _ in range(2)]
            for p in range(SLOTS):
                base = work_ref[p * NP : (p + 1) * NP, :]
                lines = [base * basis(1, 2 * pair + i, p) for i in range(2)]
                for a in range(NP):
                    weight = basis(0, a, p)
                    for i in range(2):
                        term = lines[i] * weight
                        acc[i][a] = term if acc[i][a] is None else acc[i][a] + term
            for i in range(2):
                for a in range(NP):
                    force_ref[f, t, pl.ds(a * 64 + (2 * pair + i) * 8, 8), :] = acc[i][a]
        return carry

    lax.fori_loop(0, 3 * tiles, step, 0)

    lane = iota((NP, LANES), 1)
    bz = iota((64, LANES), 1) % BZ
    for f in range(3):
        xup_ref[f] = force_ref[f, tiles - 1, 448:512, :]
        xdn_ref[f] = force_ref[f, 0, 0:64, :]
        left_ref[f] = pltpu.roll(force_ref[f, tiles - 1, 504:512, :], BZ, 1)
        right_ref[f] = pltpu.roll(force_ref[f, 0, 56:64, :], BZ, 1)
        for t in range(tiles - 1):
            summed = force_ref[f, t, 448:512, :] + force_ref[f, t + 1, 0:64, :]
            force_ref[f, t, 448:512, :] = summed
            force_ref[f, t + 1, 0:64, :] = summed
        for a in range(NP):
            first = slice(a * 64, a * 64 + 8)
            last = slice(a * 64 + 56, a * 64 + 64)
            up_line = jnp.zeros((NP, LANES), F32)
            down_line = jnp.zeros((NP, LANES), F32)
            for t in range(tiles):
                upper = force_ref[f, t, last, :]
                lower = force_ref[f, t, first, :]
                take = lane // BZ == t
                up_line = jnp.where(take, pltpu.roll(upper, 16 * t + 16, 1), up_line)
                moved = pltpu.roll(lower, 16 * t, 1) if t else lower
                down_line = jnp.where(take, moved, down_line)
                force_ref[f, t, first, :] = lower + jnp.where(
                    lane >= BZ, pltpu.roll(upper, BZ, 1), 0.0
                )
                force_ref[f, t, last, :] = upper + jnp.where(
                    lane < LANES - BZ, pltpu.roll(lower, LANES - BZ, 1), 0.0
                )
            yup_ref[f, a * 8 : a * 8 + 8, :] = up_line
            ydn_ref[f, a * 8 : a * 8 + 8, :] = down_line
        for t in range(tiles):
            lower = force_ref[f, t, pl.ds(0, 64, stride=NP), :]
            upper = force_ref[f, t, pl.ds(NP - 1, 64, stride=NP), :]
            force_ref[f, t, pl.ds(0, 64, stride=NP), :] = lower + jnp.where(
                bz > 0, pltpu.roll(upper, 1, 1), 0.0
            )
            force_ref[f, t, pl.ds(NP - 1, 64, stride=NP), :] = upper + jnp.where(
                bz < BZ - 1, pltpu.roll(lower, LANES - 1, 1), 0.0
            )


def edge_kernel(below_ref, above_ref, ydn_ref, yb_ref, cb_ref, ca_ref, token_ref, down_ref, low_ref):
    lane = iota((NP, LANES), 1)
    first = lane < BZ
    last = (lane >= 3 * BZ) & (lane < 4 * BZ)
    for f in range(3):
        down_ref[f] = ydn_ref[f]
        down_ref[f, 0:8, :] += jnp.where(first, below_ref[f, 0:8, :], 0.0)
        down_ref[f, 56:64, :] += jnp.where(last, pltpu.roll(above_ref[f, 0:8, :], 3 * BZ, 1), 0.0)
        low_ref[f] = yb_ref[f]
        low_ref[f, 0:8, :] += jnp.where(first, cb_ref[f], 0.0)
        low_ref[f, 56:64, :] += jnp.where(last, pltpu.roll(ca_ref[f], 3 * BZ, 1), 0.0)


def face_delta(face):
    lane = iota((NP, LANES), 1)
    upper = face[56:64]
    lower = face[0:8]
    new_lower = lower + jnp.where(lane >= BZ, pltpu.roll(upper, BZ, 1), 0.0)
    new_upper = upper + jnp.where(lane < LANES - BZ, pltpu.roll(lower, LANES - BZ, 1), 0.0)
    return shift_z(0.5 * jnp.concatenate([new_lower, face[8:56], new_upper], axis=0))


def face_delta(face):
    lane = iota((NP, LANES), 1)
    upper = face[56:64]
    lower = face[0:8]
    new_lower = lower + jnp.where(lane >= BZ, pltpu.roll(upper, BZ, 1), 0.0)
    new_upper = upper + jnp.where(lane < LANES - BZ, pltpu.roll(lower, LANES - BZ, 1), 0.0)
    return shift_z(jnp.concatenate([new_lower, face[8:56], new_upper], axis=0))


def base_kernel(rank_ref, place_ref, fields_ref, force_ref, out_ref, token_ref):
    tiles = EL // LANES
    stay_col = as_column((place_ref[...] // EL == rank_ref[0]).astype(F32)) > 0
    for f in range(3):
        for t in range(tiles):
            rows = slice(t * LANES, (t + 1) * LANES)
            for j in range(NODES // LANES):
                cols = slice(j * LANES, (j + 1) * LANES)
                own = jnp.where(stay_col[rows], fields_ref[f, rows, cols], 0.0)
                out_ref[f, rows, cols] = own + force_ref[f, t, cols, :].T
    token_ref[...] = jnp.zeros((8, LANES), F32)


def lines_of(values, node, line_ref):
    values = shift_z(jnp.where(iota((64, LANES), 1) < BX * BZ, values, 0.0))
    for a in range(NP):
        at = a * 64 + node * 8
        line_ref[at : at + 8, :] = values[a * 8 : a * 8 + 8]
    cols = [line_ref[j * LANES : (j + 1) * LANES, :].T for j in range(NODES // LANES)]
    return jnp.concatenate(cols, axis=1)[: BX * BZ]


def place_kernel(
    peers_ref,
    slot_ref,
    recv_ref,
    base_ref,
    xb_ref,
    xa_ref,
    low_ref,
    out_ref,
    ends_ref,
    recv_held,
    held_ref,
    line_ref,
    lows_ref,
    arrived,
    left,
):
    tiles = EL // LANES

    peers = peers_ref[...]
    for c in range(PEERS):
        block = recv_ref.at[peers[0, CAP * c]]
        pltpu.make_async_copy(block, recv_held.at[c], arrived.at[0, 0]).start()
    whole_recv = pltpu.make_async_copy(recv_ref.at[pl.ds(0, PEERS)], recv_held, arrived.at[0, 0])
    loads = []
    for f in range(3):
        loads.append(pltpu.make_async_copy(base_ref.at[f], held_ref.at[f], arrived.at[f, 1]))
        loads[f].start()
    onehot = (iota((EL, MOVERS), 0) + 1 == slot_ref[...]).astype(BF16)
    blank = jnp.zeros((64, LANES), F32)
    line_ref[...] = jnp.zeros((NODES, LANES), F32)
    for f in range(3):
        lows_ref[f] = lines_of(low_ref[f], 0, line_ref)
    copies = []
    for f in range(3):
        if f == 0:
            whole_recv.wait()
        pieces = []
        for h in range(2):
            pieces += list(deinterleave(recv_held[:, COMP * f + 8 * h : COMP * f + 8 * h + 8, :]))
        rows = picked(onehot, jnp.concatenate(pieces, axis=1))
        loads[f].wait()
        held_ref[f] += rows
        delta = jnp.concatenate([face_delta(xb_ref[f]), blank], axis=0)
        held_ref[f, 0:LANES, 0:LANES] += delta.T
        delta = jnp.concatenate([blank, face_delta(xa_ref[f])], axis=0)
        held_ref[f, EL - LANES :, NODES - LANES :] += delta.T
        for t in range(tiles):
            mine = slice(t * BZ, (t + 1) * BZ)
            held_ref[f, t * LANES : t * LANES + BZ, :] += lows_ref[f, mine, :]
            inner = pl.ds(t * LANES, LANES - BZ)
            copies.append(
                pltpu.make_async_copy(held_ref.at[f, inner], out_ref.at[f, inner], left.at[f, t])
            )
            copies[-1].start()
            last = (t + 1) * LANES
            ends_ref[f, mine, :] = held_ref[f, last - BZ : last, :]
    for copy in copies:
        copy.wait()


def lines_kernel(ends_ref, ya_ref, inner_ref, out_ref, line_ref, held_ref, left):
    tiles = EL // LANES
    line_ref[...] = jnp.zeros((NODES, LANES), F32)
    copies = []
    for f in range(3):
        held_ref[f] = ends_ref[f] + lines_of(ya_ref[f], NP - 1, line_ref)
        for t in range(tiles):
            at = pl.ds((t + 1) * LANES - BZ, BZ)
            mine = pl.ds(t * BZ, BZ)
            copies.append(
                pltpu.make_async_copy(held_ref.at[f, mine], out_ref.at[f, at], left.at[f, t])
            )
            copies[-1].start()
    for copy in copies:
        copy.wait()


def passed_along(x, along_ex, along_ey):
    rows, cols = lax.axis_size("ex"), lax.axis_size("ey")
    pairs = []
    for i in range(rows):
        for j in range(cols):
            to_i, to_j = i + along_ex, j + along_ey
            if 0 <= to_i < rows and 0 <= to_j < cols:
                pairs.append((i * cols + j, to_i * cols + to_j))
    return lax.ppermute(x, AXES, pairs)


def whole(n):
    return [pl.BlockSpec(memory_space=pltpu.VMEM)] * n


def params(mib):
    return pltpu.CompilerParams(vmem_limit_bytes=mib * MIB)


def cost(micros):
    return pl.CostEstimate(flops=0, bytes_accessed=int(micros * 3_000_000), transcendentals=0)


def body(fields, particles, counts, new_place):
    devices = lax.axis_size(AXES)
    rank = lax.axis_index(AXES).astype(jnp.int32).reshape(1)
    fields = jnp.transpose(fields, (1, 0, 2))
    place = new_place.reshape(1, EL)
    counts = counts.reshape(1, EL)
    smem = [pl.BlockSpec(memory_space=pltpu.SMEM)]
    anywhere = pl.BlockSpec(memory_space=pl.ANY)
    in_hbm = pl.BlockSpec(memory_space=pltpu.HBM)
    struct = jax.ShapeDtypeStruct
    tiles = EL // LANES
    tile_scratch = pltpu.VMEM((tiles, LANES, LANES), F32)
    basis_scratch = pltpu.VMEM((tiles, 3, LANES, LANES), F32)
    work_scratch = pltpu.VMEM((LANES, LANES), F32)
    half = MOVERS // LANES

    def interp(moves, out_shape, mib, name):
        return pl.pallas_call(
            functools.partial(interp_kernel, moves),
            out_shape=out_shape,
            in_specs=smem + [anywhere] * 4,
            out_specs=tuple(whole(2)),
            scratch_shapes=[
                pltpu.VMEM((half, LANES, LANES), F32),
                pltpu.VMEM((half, LANES, LANES), F32),
                pltpu.VMEM((half, 3, LANES, LANES), F32),
                pltpu.VMEM((3, half, NODES, LANES), F32),
                work_scratch,
                pltpu.VMEM((1, MOVERS), jnp.int32),
                pltpu.VMEM((3, EL, NODES), F32),
                pltpu.VMEM((1, EL), jnp.int32),
                pltpu.VMEM((1, EL), jnp.int32),
                pltpu.VMEM((EL, PARTS), F32),
                pltpu.SemaphoreType.DMA((6,)),
            ],
            compiler_params=params(mib),
            cost_estimate=cost(6),
            name=name,
        )(rank, place, counts, fields, particles)

    send_head, position = interp(
        True, (struct((devices * HEAD, LANES), F32), struct((1, EL), jnp.int32)), 58, "moving"
    )
    head, stay_slots = interp(
        False, (struct((MOVERS, 2 * LANES), F32), struct((1, MOVERS), jnp.int32)), 40, "staying"
    )
    recv_head = lax.all_to_all(send_head.reshape(-1), ORDER, split_axis=0, concat_axis=0, tiled=True)
    recv_head = recv_head.reshape(devices * HEAD, LANES)
    send = pl.pallas_call(
        pack_kernel,
        out_shape=struct((devices, 3 * COMP, LANES), F32),
        in_specs=whole(2),
        out_specs=whole(1)[0],
        compiler_params=params(58),
        cost_estimate=cost(5),
        name="pack",
    )(position, fields)
    recv = lax.all_to_all(send, ORDER, split_axis=0, concat_axis=0, tiled=True)
    face = struct((3, 64, LANES), F32)
    corner = struct((3, NP, LANES), F32)
    force, xup, xdn, yup, ydn, left, right, particles_next, slots, peers = pl.pallas_call(
        force_kernel,
        out_shape=(
            struct((3, tiles, NODES, LANES), F32),
            face,
            face,
            face,
            face,
            corner,
            corner,
            struct((EL, PARTS), F32),
            struct((1, MOVERS), jnp.int32),
            struct((1, MOVERS), jnp.int32),
        ),
        in_specs=whole(3),
        out_specs=tuple(whole(10)),
        scratch_shapes=[tile_scratch, tile_scratch, basis_scratch, work_scratch],
        compiler_params=params(40),
        cost_estimate=cost(8),
        name="force",
    )(head, stay_slots, recv_head)
    base, token = pl.pallas_call(
        base_kernel,
        out_shape=(pltpu.HBM((3, EL, NODES), F32), struct((8, LANES), F32)),
        in_specs=smem + whole(3),
        out_specs=tuple(whole(2)),
        compiler_params=params(20),
        cost_estimate=cost(5),
        name="base",
    )(rank, place, fields, force)
    below_x = passed_along(xup, 1, 0)
    above_x = passed_along(xdn, -1, 0)
    below_y = passed_along(yup, 0, 1)
    corner_below = passed_along(left, 1, 1)
    corner_above = passed_along(right, -1, 1)
    down, low = pl.pallas_call(
        edge_kernel,
        out_shape=(face, face),
        in_specs=whole(7),
        out_specs=tuple(whole(2)),
        compiler_params=params(8),
        cost_estimate=cost(1),
        name="edge",
    )(below_x, above_x, ydn, below_y, corner_below, corner_above, token)
    above_y = passed_along(down, 0, -1)
    ends = (3, tiles * BZ, NODES)
    inner, ends_out = pl.pallas_call(
        place_kernel,
        out_shape=(struct((3, EL, NODES), F32), struct(ends, F32)),
        in_specs=whole(2) + [in_hbm, in_hbm] + whole(3),
        out_specs=(in_hbm, whole(1)[0]),
        scratch_shapes=[
            pltpu.VMEM((PEERS, 3 * COMP, LANES), F32),
            pltpu.VMEM((3, EL, NODES), F32),
            pltpu.VMEM((NODES, LANES), F32),
            pltpu.VMEM(ends, F32),
            pltpu.SemaphoreType.DMA((3, 2)),
            pltpu.SemaphoreType.DMA((3, tiles)),
        ],
        compiler_params=params(20),
        cost_estimate=cost(3),
        name="place",
    )(
        peers,
        slots,
        recv,
        pltpu.with_memory_space_constraint(base, pltpu.HBM),
        below_x,
        above_x,
        low,
    )
    out = pl.pallas_call(
        lines_kernel,
        out_shape=struct((3, EL, NODES), F32),
        in_specs=whole(2) + [anywhere],
        out_specs=anywhere,
        scratch_shapes=[
            pltpu.VMEM((NODES, LANES), F32),
            pltpu.VMEM(ends, F32),
            pltpu.SemaphoreType.DMA((3, tiles)),
        ],
        input_output_aliases={2: 0},
        compiler_params=params(10),
        cost_estimate=cost(1),
        name="lines",
    )(ends_out, above_y, inner)
    return jnp.transpose(out, (1, 0, 2)), particles_next


def solution(mesh):
    return jax.shard_map(
        body,
        mesh=mesh,
        in_specs=(P(AXES, None, None), P(AXES, None), P(AXES), P(AXES)),
        out_specs=(P(AXES, None, None), P(AXES, None)),
        check_vma=False,
    )
```

```python
import functools

import jax
import jax.numpy as jnp
import numpy as np
from jax import lax
from jax.experimental import pallas as pl
from jax.experimental.pallas import tpu as pltpu
from jax.sharding import PartitionSpec as P

NP = 8
SLOTS = 16
CAP = 4
PEERS = 64
N_EX = 16
N_EY = 8
STEP = 37
BACK = 45
ORDER = [[k * BACK % (N_EX * N_EY) for k in range(N_EX * N_EY)]]
BX = 4
BY = 8
BZ = 16
NODES = NP**3
EL = BX * BY * BZ
MOVERS = PEERS * CAP
LANES = 128
PARTS = 8 * SLOTS
HEAD = 6
COMP = 16
AXES = ("ex", "ey")
POINTS = [
    -1.0,
    -0.8717401485096066,
    -0.5917001814331423,
    -0.2092992179024789,
    0.2092992179024789,
    0.5917001814331423,
    0.8717401485096066,
    1.0,
]
F32 = jnp.float32
BF16 = jnp.bfloat16
MIB = 1024 * 1024


def iota(shape, axis):
    return lax.broadcasted_iota(jnp.int32, shape, axis)


def split(x):
    high = x.astype(BF16)
    return high, (x - high.astype(F32)).astype(BF16)


def picked(onehot, x):
    high, low = split(x)
    return jnp.dot(
        jnp.concatenate([onehot, onehot], axis=1),
        jnp.concatenate([high, low], axis=0),
        preferred_element_type=F32,
    )


def as_column(row):
    return jnp.broadcast_to(row, (LANES, EL)).T


def pack_positions(place, rank):
    target = place // EL
    moving = target != rank
    key = jnp.where(moving, target, -1).astype(F32)
    key_col = as_column(key)
    order = []
    for j in range(EL // LANES):
        piece = key[:, j * LANES : (j + 1) * LANES]
        earlier = iota((EL, LANES), 0) < iota((EL, LANES), 1) + j * LANES
        same = (key_col == piece) & earlier
        order.append(jnp.sum(same.astype(F32), axis=0, keepdims=True))
    order = jnp.concatenate(order, axis=1).astype(jnp.int32)
    block = target * STEP % (N_EX * N_EY)
    return jnp.where(moving, block * CAP + order, -1)


def interleave(first, second):
    devices = first.shape[0] // CAP
    low = iota((devices // 2, 8, LANES), 1) < CAP
    first = first.reshape(devices // 2, 8, LANES)
    second = second.reshape(devices // 2, 8, LANES)
    even = jnp.where(low, first, pltpu.roll(second, CAP, 1))
    odd = jnp.where(low, pltpu.roll(first, CAP, 1), second)
    return jnp.stack([even, odd], axis=1).reshape(devices, 8, LANES)


def deinterleave(blocks):
    devices = blocks.shape[0]
    pairs = blocks.reshape(devices // 2, 2, 8, LANES)
    even, odd = pairs[:, 0], pairs[:, 1]
    low = iota((devices // 2, 8, LANES), 1) < CAP
    first = jnp.where(low, even, pltpu.roll(odd, CAP, 1))
    second = jnp.where(low, pltpu.roll(even, CAP, 1), odd)
    return first.reshape(devices * CAP, LANES), second.reshape(devices * CAP, LANES)


def picked_row(row, onehot):
    high, low = split(jnp.broadcast_to(row.astype(F32), (8, row.shape[1])))
    dims = (((1,), (1,)), ((), ()))
    out = lax.dot_general(high, onehot, dims, preferred_element_type=F32)
    out = out + lax.dot_general(low, onehot, dims, preferred_element_type=F32)
    return out[0:1]


def interp_kernel(moves, *refs):
    rank_ref, place_ref, count_ref, fields_ref, part_ref = refs[:5]
    out_refs = refs[5:7]
    tp_ref, push_ref, basis_ref, t_ref, work_ref, count_row_ref, held_ref = refs[7:14]
    place_held, count_held, part_held, arrived = refs[14:]
    tiles = MOVERS // LANES
    pairs = [(place_ref, place_held), (count_ref, count_held), (part_ref, part_held)]
    pairs += [(fields_ref.at[f], held_ref.at[f]) for f in range(3)]
    copies = [pltpu.make_async_copy(*pair, arrived.at[i]) for i, pair in enumerate(pairs)]
    for copy in copies:
        copy.start()
    earlier = (iota((EL, EL), 0) < iota((EL, EL), 1)).astype(BF16)
    copies[0].wait()
    place = place_held[...]
    moving = place // EL != rank_ref[0]
    chosen = moving if moves else jnp.logical_not(moving)
    order = jnp.dot(
        jnp.broadcast_to(chosen.astype(F32), (8, EL)).astype(BF16),
        earlier,
        preferred_element_type=F32,
    )[0:1]
    key = jnp.where(chosen, order.astype(jnp.int32), -1)
    onehot = (iota((MOVERS, EL), 0) == key).astype(BF16)
    copies[1].wait()
    count_row_ref[...] = picked_row(count_held[...], onehot).astype(jnp.int32)
    slot_row = picked_row(place % EL + 1, onehot)
    if moves:
        send_ref, position_ref = out_refs
        devices = send_ref.shape[0] // HEAD
        position = pack_positions(place, rank_ref[0])
        position_ref[...] = position
        goes_to = picked_row(position, onehot).astype(jnp.int32)
        goes_to = goes_to % CAP * devices + goes_to // CAP
        scatter = (iota((devices * CAP, MOVERS), 0) == goes_to).astype(BF16)
    copies[2].wait()
    records = picked(onehot, part_held[...])
    for t in range(tiles):
        tp_ref[t] = records[t * LANES : (t + 1) * LANES, :].T

    def make_basis(t, carry):
        for d in range(3):
            rows = lagrange_rows(tp_ref[t, d * SLOTS : (d + 1) * SLOTS, :])
            for n in range(NP):
                basis_ref[t, d, n * SLOTS : (n + 1) * SLOTS, :] = rows[n]
        return carry

    def gather(f):
        copies[3 + f].wait()
        rows = picked(onehot, held_ref[f])
        for t in range(tiles):
            for j in range(NODES // LANES):
                cols = slice(j * LANES, (j + 1) * LANES)
                t_ref[f, t, cols, :] = rows[t * LANES : (t + 1) * LANES, cols].T

    for t in range(tiles):
        make_basis(t, 0)
    gather(0)

    def step(t, f):
        def basis(which, n, p):
            return basis_ref[t, which, pl.ds(n * SLOTS + p, 1), :]

        total = [None] * SLOTS
        for pair in range(NP // 2):
            nodes = [
                [t_ref[f, t, pl.ds(a * 64 + (2 * pair + i) * 8, 8), :] for a in range(NP)]
                for i in range(2)
            ]
            for p in range(SLOTS):
                sums = [None, None]
                for a in range(NP):
                    weight = basis(0, a, p)
                    for i in range(2):
                        term = nodes[i][a] * weight
                        sums[i] = term if sums[i] is None else sums[i] + term
                for i in range(2):
                    term = sums[i] * basis(1, 2 * pair + i, p)
                    total[p] = term if total[p] is None else total[p] + term
        for p in range(SLOTS):
            along_z = basis_ref[t, 2, pl.ds(p, NP, stride=SLOTS), :]
            work_ref[p * NP : (p + 1) * NP, :] = total[p] * along_z
        fluid = work_ref[pl.ds(0, SLOTS, stride=NP), :]
        for c in range(1, NP):
            fluid = fluid + work_ref[pl.ds(c, SLOTS, stride=NP), :]
        where = pl.ds(pl.multiple_of((3 + f) * SLOTS, SLOTS), SLOTS)
        velocity = tp_ref[t, where, :]
        ratio = tp_ref[t, 6 * SLOTS : 7 * SLOTS, :]
        mass = tp_ref[t, 7 * SLOTS : 8 * SLOTS, :]
        count = count_row_ref[:, pl.ds(pl.multiple_of(t * LANES, LANES), LANES)]
        drag = jnp.where(iota((SLOTS, LANES), 0) < count, ratio * (fluid - velocity), 0.0)
        tp_ref[t, where, :] = velocity + drag
        push_ref[t, pl.ds(pl.multiple_of((1 + f) * SLOTS, SLOTS), SLOTS), :] = -(mass * drag)
        return f

    for f in range(3):
        if f:
            gather(f)
        lax.fori_loop(0, tiles, step, f)

    heads = []
    for t in range(tiles):
        rows = slice(t * LANES, (t + 1) * LANES)
        push_ref[t, 0:SLOTS, :] = jnp.broadcast_to(slot_row[:, rows], (SLOTS, LANES))
        push_ref[t, 4 * SLOTS :, :] = jnp.zeros((LANES - 4 * SLOTS, LANES), F32)
        heads.append(jnp.concatenate([tp_ref[t].T, push_ref[t].T], axis=1))
    head = jnp.concatenate(heads, axis=0)
    if moves:
        send_ref, position_ref = out_refs
        devices = send_ref.shape[0] // HEAD
        rows = picked(scatter, head)
        lane = iota((devices, LANES), 1)
        for q in range(CAP):
            mine = slice(q * devices, (q + 1) * devices)
            send_ref[pl.ds(q, devices, stride=HEAD), :] = rows[mine, :LANES]
            if q % 2:
                both = jnp.where(lane < LANES // 2, before, pltpu.roll(rows[mine, LANES:], LANES // 2, 1))
                send_ref[pl.ds(CAP + q // 2, devices, stride=HEAD), :] = both
            before = rows[mine, LANES:]
    else:
        head_ref, slot_ref = out_refs
        head_ref[...] = head
        slot_ref[...] = slot_row.astype(jnp.int32)


def pack_kernel(position_ref, fields_ref, out_ref):
    devices = out_ref.shape[0]
    onehot = (iota((devices * CAP, EL), 0) == position_ref[...]).astype(BF16)
    for f in range(3):
        rows = picked(onehot, fields_ref[f])
        for h in range(2):
            at = COMP * f + 8 * h
            left = 2 * h * LANES
            out_ref[:, at : at + 8, :] = interleave(
                rows[:, left : left + LANES], rows[:, left + LANES : left + 2 * LANES]
            )


def lagrange_rows(coord):
    diffs = [coord - p for p in POINTS]
    left = [None] * NP
    right = [None] * NP
    for i in range(1, NP):
        left[i] = diffs[i - 1] if i == 1 else left[i - 1] * diffs[i - 1]
    for i in range(NP - 2, -1, -1):
        right[i] = diffs[i + 1] if i == NP - 2 else right[i + 1] * diffs[i + 1]
    out = []
    for i in range(NP):
        scale = 1.0
        for m in range(NP):
            if m != i:
                scale /= POINTS[i] - POINTS[m]
        if i == 0:
            term = right[0]
        elif i == NP - 1:
            term = left[i]
        else:
            term = left[i] * right[i]
        out.append(term * float(scale))
    return out


def gaussian_rows(coord):
    return [jnp.exp(-((p - coord) ** 2) * (0.5 / 0.35**2)) for p in POINTS]


def shift_z(x):
    n = x.shape[0] // NP
    x = x.reshape(n, NP, LANES)
    node = iota((n, NP, LANES), 1)
    bz = iota((n, NP, LANES), 2) % BZ
    down = pltpu.roll(pltpu.roll(x, 1, 1), 1, 2)
    up = pltpu.roll(pltpu.roll(x, NP - 1, 1), LANES - 1, 2)
    x = x + jnp.where((node == 0) & (bz > 0), down, 0.0)
    x = x + jnp.where((node == NP - 1) & (bz < BZ - 1), up, 0.0)
    return x.reshape(n * NP, LANES)


def force_kernel(
    head_ref,
    stay_slot_ref,
    recv_ref,
    force_ref,
    xup_ref,
    xdn_ref,
    yup_ref,
    ydn_ref,
    left_ref,
    right_ref,
    part_ref,
    slot_ref,
    peers_ref,
    tp_ref,
    push_ref,
    basis_ref,
    work_ref,
):
    tiles = EL // LANES
    devices = recv_ref.shape[0] // HEAD
    particles, extra = [], []
    for q in range(CAP):
        particles.append(recv_ref[pl.ds(q, devices, stride=HEAD), :])
        both = recv_ref[pl.ds(CAP + q // 2, devices, stride=HEAD), :]
        extra.append(pltpu.roll(both, LANES // 2, 1) if q % 2 else both)
    particles = jnp.concatenate(particles, axis=0)
    extra = jnp.concatenate(extra, axis=0)
    slot_row = extra.T[0:1, :].astype(jnp.int32)
    at = iota((devices * CAP, devices * CAP), 0)
    turned = at // devices + at % devices * CAP == iota((devices * CAP, devices * CAP), 1)
    high, low = split(jnp.broadcast_to(slot_row.astype(F32), (8, devices * CAP)))
    order = turned.astype(BF16)
    row = jnp.dot(high, order, preferred_element_type=F32)
    row = row + jnp.dot(low, order, preferred_element_type=F32)
    row = row[0:1].astype(jnp.int32)
    filled = row > 0
    earlier = (iota((devices * CAP, devices * CAP), 0) < iota((devices * CAP, devices * CAP), 1)).astype(BF16)
    rank = jnp.dot(
        jnp.broadcast_to(filled.astype(F32), (8, devices * CAP)).astype(BF16),
        earlier,
        preferred_element_type=F32,
    )[0:1]
    key = jnp.where(filled, rank.astype(jnp.int32), -1)
    packed = (iota((MOVERS, devices * CAP), 0) == key).astype(BF16)
    slot_ref[...] = picked_row(row, packed).astype(jnp.int32)
    peers_ref[...] = picked_row(iota((1, devices * CAP), 1) // CAP, packed).astype(jnp.int32)
    slots = jnp.concatenate([slot_row, stay_slot_ref[...]], axis=1)
    onehot = (iota((EL, EL + MOVERS), 0) + 1 == slots).astype(BF16)
    arrived = jnp.concatenate([particles, extra], axis=1)
    both = picked(onehot, jnp.concatenate([arrived, head_ref[...]], axis=0))
    record = both[:, :LANES]
    push = both[:, LANES:]
    part_ref[...] = record
    for t in range(tiles):
        rows = slice(t * LANES, (t + 1) * LANES)
        tp_ref[t] = record[rows].T
        push_ref[t] = push[rows].T

    def make_basis(t, carry):
        for d in range(3):
            rows = gaussian_rows(tp_ref[t, d * SLOTS : (d + 1) * SLOTS, :])
            for n in range(NP):
                basis_ref[t, d, n * SLOTS : (n + 1) * SLOTS, :] = rows[n]
        return carry

    lax.fori_loop(0, tiles, make_basis, 0)

    def step(index, carry):
        f = index // tiles
        t = index % tiles

        def basis(which, n, p):
            return basis_ref[t, which, pl.ds(n * SLOTS + p, 1), :]

        for p in range(SLOTS):
            along_z = basis_ref[t, 2, pl.ds(p, NP, stride=SLOTS), :]
            value = push_ref[t, pl.ds((1 + f) * SLOTS + p, 1), :]
            work_ref[p * NP : (p + 1) * NP, :] = (0.5 * value) * along_z
        for pair in range(NP // 2):
            acc = [[None] * NP for _ in range(2)]
            for p in range(SLOTS):
                base = work_ref[p * NP : (p + 1) * NP, :]
                lines = [base * basis(1, 2 * pair + i, p) for i in range(2)]
                for a in range(NP):
                    weight = basis(0, a, p)
                    for i in range(2):
                        term = lines[i] * weight
                        acc[i][a] = term if acc[i][a] is None else acc[i][a] + term
            for i in range(2):
                for a in range(NP):
                    force_ref[f, t, pl.ds(a * 64 + (2 * pair + i) * 8, 8), :] = acc[i][a]
        return carry

    lax.fori_loop(0, 3 * tiles, step, 0)

    lane = iota((NP, LANES), 1)
    bz = iota((64, LANES), 1) % BZ
    for f in range(3):
        xup_ref[f] = force_ref[f, tiles - 1, 448:512, :]
        xdn_ref[f] = force_ref[f, 0, 0:64, :]
        left_ref[f] = pltpu.roll(force_ref[f, tiles - 1, 504:512, :], BZ, 1)
        right_ref[f] = pltpu.roll(force_ref[f, 0, 56:64, :], BZ, 1)
        for t in range(tiles - 1):
            summed = force_ref[f, t, 448:512, :] + force_ref[f, t + 1, 0:64, :]
            force_ref[f, t, 448:512, :] = summed
            force_ref[f, t + 1, 0:64, :] = summed
        for a in range(NP):
            first = slice(a * 64, a * 64 + 8)
            last = slice(a * 64 + 56, a * 64 + 64)
            up_line = jnp.zeros((NP, LANES), F32)
            down_line = jnp.zeros((NP, LANES), F32)
            for t in range(tiles):
                upper = force_ref[f, t, last, :]
                lower = force_ref[f, t, first, :]
                take = lane // BZ == t
                up_line = jnp.where(take, pltpu.roll(upper, 16 * t + 16, 1), up_line)
                moved = pltpu.roll(lower, 16 * t, 1) if t else lower
                down_line = jnp.where(take, moved, down_line)
                force_ref[f, t, first, :] = lower + jnp.where(
                    lane >= BZ, pltpu.roll(upper, BZ, 1), 0.0
                )
                force_ref[f, t, last, :] = upper + jnp.where(
                    lane < LANES - BZ, pltpu.roll(lower, LANES - BZ, 1), 0.0
                )
            yup_ref[f, a * 8 : a * 8 + 8, :] = up_line
            ydn_ref[f, a * 8 : a * 8 + 8, :] = down_line
        for t in range(tiles):
            lower = force_ref[f, t, pl.ds(0, 64, stride=NP), :]
            upper = force_ref[f, t, pl.ds(NP - 1, 64, stride=NP), :]
            force_ref[f, t, pl.ds(0, 64, stride=NP), :] = lower + jnp.where(
                bz > 0, pltpu.roll(upper, 1, 1), 0.0
            )
            force_ref[f, t, pl.ds(NP - 1, 64, stride=NP), :] = upper + jnp.where(
                bz < BZ - 1, pltpu.roll(lower, LANES - 1, 1), 0.0
            )


def edge_kernel(below_ref, above_ref, ydn_ref, yb_ref, cb_ref, ca_ref, token_ref, down_ref, low_ref):
    lane = iota((NP, LANES), 1)
    first = lane < BZ
    last = (lane >= 3 * BZ) & (lane < 4 * BZ)
    for f in range(3):
        down_ref[f] = ydn_ref[f]
        down_ref[f, 0:8, :] += jnp.where(first, below_ref[f, 0:8, :], 0.0)
        down_ref[f, 56:64, :] += jnp.where(last, pltpu.roll(above_ref[f, 0:8, :], 3 * BZ, 1), 0.0)
        low_ref[f] = yb_ref[f]
        low_ref[f, 0:8, :] += jnp.where(first, cb_ref[f], 0.0)
        low_ref[f, 56:64, :] += jnp.where(last, pltpu.roll(ca_ref[f], 3 * BZ, 1), 0.0)


def face_delta(face):
    lane = iota((NP, LANES), 1)
    upper = face[56:64]
    lower = face[0:8]
    new_lower = lower + jnp.where(lane >= BZ, pltpu.roll(upper, BZ, 1), 0.0)
    new_upper = upper + jnp.where(lane < LANES - BZ, pltpu.roll(lower, LANES - BZ, 1), 0.0)
    return shift_z(0.5 * jnp.concatenate([new_lower, face[8:56], new_upper], axis=0))


def face_delta(face):
    lane = iota((NP, LANES), 1)
    upper = face[56:64]
    lower = face[0:8]
    new_lower = lower + jnp.where(lane >= BZ, pltpu.roll(upper, BZ, 1), 0.0)
    new_upper = upper + jnp.where(lane < LANES - BZ, pltpu.roll(lower, LANES - BZ, 1), 0.0)
    return shift_z(jnp.concatenate([new_lower, face[8:56], new_upper], axis=0))


def base_kernel(rank_ref, place_ref, fields_ref, force_ref, out_ref, token_ref):
    tiles = EL // LANES
    stay_col = as_column((place_ref[...] // EL == rank_ref[0]).astype(F32)) > 0
    for f in range(3):
        for t in range(tiles):
            rows = slice(t * LANES, (t + 1) * LANES)
            for j in range(NODES // LANES):
                cols = slice(j * LANES, (j + 1) * LANES)
                own = jnp.where(stay_col[rows], fields_ref[f, rows, cols], 0.0)
                out_ref[f, rows, cols] = own + force_ref[f, t, cols, :].T
    token_ref[...] = jnp.zeros((8, LANES), F32)


def lines_of(values, node, line_ref):
    values = shift_z(jnp.where(iota((64, LANES), 1) < BX * BZ, values, 0.0))
    for a in range(NP):
        at = a * 64 + node * 8
        line_ref[at : at + 8, :] = values[a * 8 : a * 8 + 8]
    cols = [line_ref[j * LANES : (j + 1) * LANES, :].T for j in range(NODES // LANES)]
    return jnp.concatenate(cols, axis=1)[: BX * BZ]


def place_kernel(
    peers_ref,
    slot_ref,
    recv_ref,
    base_ref,
    xb_ref,
    xa_ref,
    low_ref,
    out_ref,
    ends_ref,
    recv_held,
    held_ref,
    line_ref,
    lows_ref,
    arrived,
    left,
):
    tiles = EL // LANES

    peers = peers_ref[...]
    for c in range(PEERS):
        block = recv_ref.at[peers[0, CAP * c]]
        pltpu.make_async_copy(block, recv_held.at[c], arrived.at[0, 0]).start()
    whole_recv = pltpu.make_async_copy(recv_ref.at[pl.ds(0, PEERS)], recv_held, arrived.at[0, 0])
    loads = []
    for f in range(3):
        loads.append(pltpu.make_async_copy(base_ref.at[f], held_ref.at[f], arrived.at[f, 1]))
        loads[f].start()
    onehot = (iota((EL, MOVERS), 0) + 1 == slot_ref[...]).astype(BF16)
    blank = jnp.zeros((64, LANES), F32)
    line_ref[...] = jnp.zeros((NODES, LANES), F32)
    for f in range(3):
        lows_ref[f] = lines_of(low_ref[f], 0, line_ref)
    copies = []
    for f in range(3):
        if f == 0:
            whole_recv.wait()
        pieces = []
        for h in range(2):
            pieces += list(deinterleave(recv_held[:, COMP * f + 8 * h : COMP * f + 8 * h + 8, :]))
        rows = picked(onehot, jnp.concatenate(pieces, axis=1))
        loads[f].wait()
        held_ref[f] += rows
        delta = jnp.concatenate([face_delta(xb_ref[f]), blank], axis=0)
        held_ref[f, 0:LANES, 0:LANES] += delta.T
        delta = jnp.concatenate([blank, face_delta(xa_ref[f])], axis=0)
        held_ref[f, EL - LANES :, NODES - LANES :] += delta.T
        for t in range(tiles):
            mine = slice(t * BZ, (t + 1) * BZ)
            held_ref[f, t * LANES : t * LANES + BZ, :] += lows_ref[f, mine, :]
            inner = pl.ds(t * LANES, LANES - BZ)
            copies.append(
                pltpu.make_async_copy(held_ref.at[f, inner], out_ref.at[f, inner], left.at[f, t])
            )
            copies[-1].start()
            last = (t + 1) * LANES
            ends_ref[f, mine, :] = held_ref[f, last - BZ : last, :]
    for copy in copies:
        copy.wait()


def lines_kernel(ends_ref, ya_ref, inner_ref, out_ref, line_ref, held_ref, left):
    tiles = EL // LANES
    line_ref[...] = jnp.zeros((NODES, LANES), F32)
    copies = []
    for f in range(3):
        held_ref[f] = ends_ref[f] + lines_of(ya_ref[f], NP - 1, line_ref)
        for t in range(tiles):
            at = pl.ds((t + 1) * LANES - BZ, BZ)
            mine = pl.ds(t * BZ, BZ)
            copies.append(
                pltpu.make_async_copy(held_ref.at[f, mine], out_ref.at[f, at], left.at[f, t])
            )
            copies[-1].start()
    for copy in copies:
        copy.wait()


def passed_along(x, along_ex, along_ey):
    rows, cols = lax.axis_size("ex"), lax.axis_size("ey")
    pairs = []
    for i in range(rows):
        for j in range(cols):
            to_i, to_j = i + along_ex, j + along_ey
            if 0 <= to_i < rows and 0 <= to_j < cols:
                pairs.append((i * cols + j, to_i * cols + to_j))
    return lax.ppermute(x, AXES, pairs)


def whole(n):
    return [pl.BlockSpec(memory_space=pltpu.VMEM)] * n


def params(mib):
    return pltpu.CompilerParams(vmem_limit_bytes=mib * MIB)


def cost(micros):
    return pl.CostEstimate(flops=0, bytes_accessed=int(micros * 3_000_000), transcendentals=0)


def body(fields, particles, counts, new_place):
    devices = lax.axis_size(AXES)
    rank = lax.axis_index(AXES).astype(jnp.int32).reshape(1)
    fields = jnp.transpose(fields, (1, 0, 2))
    place = new_place.reshape(1, EL)
    counts = counts.reshape(1, EL)
    smem = [pl.BlockSpec(memory_space=pltpu.SMEM)]
    anywhere = pl.BlockSpec(memory_space=pl.ANY)
    in_hbm = pl.BlockSpec(memory_space=pltpu.HBM)
    struct = jax.ShapeDtypeStruct
    tiles = EL // LANES
    tile_scratch = pltpu.VMEM((tiles, LANES, LANES), F32)
    basis_scratch = pltpu.VMEM((tiles, 3, LANES, LANES), F32)
    work_scratch = pltpu.VMEM((LANES, LANES), F32)
    half = MOVERS // LANES

    def interp(moves, out_shape, mib, name):
        return pl.pallas_call(
            functools.partial(interp_kernel, moves),
            out_shape=out_shape,
            in_specs=smem + [anywhere] * 4,
            out_specs=tuple(whole(2)),
            scratch_shapes=[
                pltpu.VMEM((half, LANES, LANES), F32),
                pltpu.VMEM((half, LANES, LANES), F32),
                pltpu.VMEM((half, 3, LANES, LANES), F32),
                pltpu.VMEM((3, half, NODES, LANES), F32),
                work_scratch,
                pltpu.VMEM((1, MOVERS), jnp.int32),
                pltpu.VMEM((3, EL, NODES), F32),
                pltpu.VMEM((1, EL), jnp.int32),
                pltpu.VMEM((1, EL), jnp.int32),
                pltpu.VMEM((EL, PARTS), F32),
                pltpu.SemaphoreType.DMA((6,)),
            ],
            compiler_params=params(mib),
            cost_estimate=cost(6),
            name=name,
        )(rank, place, counts, fields, particles)

    send_head, position = interp(
        True, (struct((devices * HEAD, LANES), F32), struct((1, EL), jnp.int32)), 58, "moving"
    )
    head, stay_slots = interp(
        False, (struct((MOVERS, 2 * LANES), F32), struct((1, MOVERS), jnp.int32)), 40, "staying"
    )
    recv_head = lax.all_to_all(send_head.reshape(-1), AXES, split_axis=0, concat_axis=0, tiled=True, axis_index_groups=ORDER)
    recv_head = recv_head.reshape(devices * HEAD, LANES)
    send = pl.pallas_call(
        pack_kernel,
        out_shape=struct((devices, 3 * COMP, LANES), F32),
        in_specs=whole(2),
        out_specs=whole(1)[0],
        compiler_params=params(58),
        cost_estimate=cost(5),
        name="pack",
    )(position, fields)
    recv = lax.all_to_all(send, AXES, split_axis=0, concat_axis=0, tiled=True, axis_index_groups=ORDER)
    face = struct((3, 64, LANES), F32)
    corner = struct((3, NP, LANES), F32)
    force, xup, xdn, yup, ydn, left, right, particles_next, slots, peers = pl.pallas_call(
        force_kernel,
        out_shape=(
            struct((3, tiles, NODES, LANES), F32),
            face,
            face,
            face,
            face,
            corner,
            corner,
            struct((EL, PARTS), F32),
            struct((1, MOVERS), jnp.int32),
            struct((1, MOVERS), jnp.int32),
        ),
        in_specs=whole(3),
        out_specs=tuple(whole(10)),
        scratch_shapes=[tile_scratch, tile_scratch, basis_scratch, work_scratch],
        compiler_params=params(40),
        cost_estimate=cost(8),
        name="force",
    )(head, stay_slots, recv_head)
    base, token = pl.pallas_call(
        base_kernel,
        out_shape=(pltpu.HBM((3, EL, NODES), F32), struct((8, LANES), F32)),
        in_specs=smem + whole(3),
        out_specs=tuple(whole(2)),
        compiler_params=params(20),
        cost_estimate=cost(5),
        name="base",
    )(rank, place, fields, force)
    below_x = passed_along(xup, 1, 0)
    above_x = passed_along(xdn, -1, 0)
    below_y = passed_along(yup, 0, 1)
    corner_below = passed_along(left, 1, 1)
    corner_above = passed_along(right, -1, 1)
    down, low = pl.pallas_call(
        edge_kernel,
        out_shape=(face, face),
        in_specs=whole(7),
        out_specs=tuple(whole(2)),
        compiler_params=params(8),
        cost_estimate=cost(1),
        name="edge",
    )(below_x, above_x, ydn, below_y, corner_below, corner_above, token)
    above_y = passed_along(down, 0, -1)
    ends = (3, tiles * BZ, NODES)
    inner, ends_out = pl.pallas_call(
        place_kernel,
        out_shape=(struct((3, EL, NODES), F32), struct(ends, F32)),
        in_specs=whole(2) + [in_hbm, in_hbm] + whole(3),
        out_specs=(in_hbm, whole(1)[0]),
        scratch_shapes=[
            pltpu.VMEM((PEERS, 3 * COMP, LANES), F32),
            pltpu.VMEM((3, EL, NODES), F32),
            pltpu.VMEM((NODES, LANES), F32),
            pltpu.VMEM(ends, F32),
            pltpu.SemaphoreType.DMA((3, 2)),
            pltpu.SemaphoreType.DMA((3, tiles)),
        ],
        compiler_params=params(20),
        cost_estimate=cost(3),
        name="place",
    )(
        peers,
        slots,
        recv,
        pltpu.with_memory_space_constraint(base, pltpu.HBM),
        below_x,
        above_x,
        low,
    )
    out = pl.pallas_call(
        lines_kernel,
        out_shape=struct((3, EL, NODES), F32),
        in_specs=whole(2) + [anywhere],
        out_specs=anywhere,
        scratch_shapes=[
            pltpu.VMEM((NODES, LANES), F32),
            pltpu.VMEM(ends, F32),
            pltpu.SemaphoreType.DMA((3, tiles)),
        ],
        input_output_aliases={2: 0},
        compiler_params=params(10),
        cost_estimate=cost(1),
        name="lines",
    )(ends_out, above_y, inner)
    return jnp.transpose(out, (1, 0, 2)), particles_next


def solution(mesh):
    return jax.shard_map(
        body,
        mesh=mesh,
        in_specs=(P(AXES, None, None), P(AXES, None), P(AXES), P(AXES)),
        out_specs=(P(AXES, None, None), P(AXES, None)),
        check_vma=False,
    )
```

```python
import functools

import jax
import jax.numpy as jnp
import numpy as np
from jax import lax
from jax.experimental import pallas as pl
from jax.experimental.pallas import tpu as pltpu
from jax.sharding import PartitionSpec as P

NP = 8
SLOTS = 16
CAP = 4
PEERS = 64
N_EX = 16
N_EY = 8
ORDER = ("ey", "ex")
BX = 4
BY = 8
BZ = 16
NODES = NP**3
EL = BX * BY * BZ
MOVERS = PEERS * CAP
LANES = 128
PARTS = 8 * SLOTS
HEAD = 6
COMP = 16
AXES = ("ex", "ey")
POINTS = [
    -1.0,
    -0.8717401485096066,
    -0.5917001814331423,
    -0.2092992179024789,
    0.2092992179024789,
    0.5917001814331423,
    0.8717401485096066,
    1.0,
]
F32 = jnp.float32
BF16 = jnp.bfloat16
MIB = 1024 * 1024


def iota(shape, axis):
    return lax.broadcasted_iota(jnp.int32, shape, axis)


def split(x):
    high = x.astype(BF16)
    return high, (x - high.astype(F32)).astype(BF16)


def picked(onehot, x):
    high, low = split(x)
    return jnp.dot(
        jnp.concatenate([onehot, onehot], axis=1),
        jnp.concatenate([high, low], axis=0),
        preferred_element_type=F32,
    )


def as_column(row):
    return jnp.broadcast_to(row, (LANES, EL)).T


def pack_positions(place, rank):
    target = place // EL
    moving = target != rank
    key = jnp.where(moving, target, -1).astype(F32)
    key_col = as_column(key)
    order = []
    for j in range(EL // LANES):
        piece = key[:, j * LANES : (j + 1) * LANES]
        earlier = iota((EL, LANES), 0) < iota((EL, LANES), 1) + j * LANES
        same = (key_col == piece) & earlier
        order.append(jnp.sum(same.astype(F32), axis=0, keepdims=True))
    order = jnp.concatenate(order, axis=1).astype(jnp.int32)
    block = target % N_EY * N_EX + target // N_EY
    return jnp.where(moving, block * CAP + order, -1)


def interleave(first, second):
    devices = first.shape[0] // CAP
    low = iota((devices // 2, 8, LANES), 1) < CAP
    first = first.reshape(devices // 2, 8, LANES)
    second = second.reshape(devices // 2, 8, LANES)
    even = jnp.where(low, first, pltpu.roll(second, CAP, 1))
    odd = jnp.where(low, pltpu.roll(first, CAP, 1), second)
    return jnp.stack([even, odd], axis=1).reshape(devices, 8, LANES)


def deinterleave(blocks):
    devices = blocks.shape[0]
    pairs = blocks.reshape(devices // 2, 2, 8, LANES)
    even, odd = pairs[:, 0], pairs[:, 1]
    low = iota((devices // 2, 8, LANES), 1) < CAP
    first = jnp.where(low, even, pltpu.roll(odd, CAP, 1))
    second = jnp.where(low, pltpu.roll(even, CAP, 1), odd)
    return first.reshape(devices * CAP, LANES), second.reshape(devices * CAP, LANES)


def picked_row(row, onehot):
    high, low = split(jnp.broadcast_to(row.astype(F32), (8, row.shape[1])))
    dims = (((1,), (1,)), ((), ()))
    out = lax.dot_general(high, onehot, dims, preferred_element_type=F32)
    out = out + lax.dot_general(low, onehot, dims, preferred_element_type=F32)
    return out[0:1]


def interp_kernel(moves, *refs):
    rank_ref, place_ref, count_ref, fields_ref, part_ref = refs[:5]
    out_refs = refs[5:7]
    tp_ref, push_ref, basis_ref, t_ref, work_ref, count_row_ref, held_ref = refs[7:14]
    place_held, count_held, part_held, arrived = refs[14:18]
    node_refs = refs[18:]
    tiles = MOVERS // LANES
    pairs = [(place_ref, place_held), (count_ref, count_held), (part_ref, part_held)]
    pairs += [(fields_ref.at[f], held_ref.at[f]) for f in range(3)]
    copies = [pltpu.make_async_copy(*pair, arrived.at[i]) for i, pair in enumerate(pairs)]
    for copy in copies:
        copy.start()
    earlier = (iota((EL, EL), 0) < iota((EL, EL), 1)).astype(BF16)
    copies[0].wait()
    place = place_held[...]
    moving = place // EL != rank_ref[0]
    chosen = moving if moves else jnp.logical_not(moving)
    order = jnp.dot(
        jnp.broadcast_to(chosen.astype(F32), (8, EL)).astype(BF16),
        earlier,
        preferred_element_type=F32,
    )[0:1]
    key = jnp.where(chosen, order.astype(jnp.int32), -1)
    onehot = (iota((MOVERS, EL), 0) == key).astype(BF16)
    copies[1].wait()
    count_row_ref[...] = picked_row(count_held[...], onehot).astype(jnp.int32)
    slot_row = picked_row(place % EL + 1, onehot)
    if moves:
        send_ref, position_ref = out_refs
        devices = send_ref.shape[0] // HEAD
        position = pack_positions(place, rank_ref[0])
        position_ref[...] = position
        goes_to = picked_row(position, onehot).astype(jnp.int32)
        goes_to = goes_to % CAP * devices + goes_to // CAP
        scatter = (iota((devices * CAP, MOVERS), 0) == goes_to).astype(BF16)
    copies[2].wait()
    records = picked(onehot, part_held[...])
    for t in range(tiles):
        tp_ref[t] = records[t * LANES : (t + 1) * LANES, :].T

    def make_basis(t, carry):
        for d in range(3):
            rows = lagrange_rows(tp_ref[t, d * SLOTS : (d + 1) * SLOTS, :])
            for n in range(NP):
                basis_ref[t, d, n * SLOTS : (n + 1) * SLOTS, :] = rows[n]
        return carry

    def gather(f):
        copies[3 + f].wait()
        rows = picked(onehot, held_ref[f])
        for t in range(tiles):
            for j in range(NODES // LANES):
                cols = slice(j * LANES, (j + 1) * LANES)
                node_refs[f][t, cols, :] = rows[t * LANES : (t + 1) * LANES, cols].T

    for t in range(tiles):
        make_basis(t, 0)
    gather(0)

    def step(t, f):
        def basis(which, n, p):
            return basis_ref[t, which, pl.ds(n * SLOTS + p, 1), :]

        total = [None] * SLOTS
        for pair in range(NP // 2):
            nodes = [
                [node_refs[f][t, pl.ds(a * 64 + (2 * pair + i) * 8, 8), :] for a in range(NP)]
                for i in range(2)
            ]
            for p in range(SLOTS):
                sums = [None, None]
                for a in range(NP):
                    weight = basis(0, a, p)
                    for i in range(2):
                        term = nodes[i][a] * weight
                        sums[i] = term if sums[i] is None else sums[i] + term
                for i in range(2):
                    term = sums[i] * basis(1, 2 * pair + i, p)
                    total[p] = term if total[p] is None else total[p] + term
        for p in range(SLOTS):
            along_z = basis_ref[t, 2, pl.ds(p, NP, stride=SLOTS), :]
            work_ref[p * NP : (p + 1) * NP, :] = total[p] * along_z
        fluid = work_ref[pl.ds(0, SLOTS, stride=NP), :]
        for c in range(1, NP):
            fluid = fluid + work_ref[pl.ds(c, SLOTS, stride=NP), :]
        where = pl.ds(pl.multiple_of((3 + f) * SLOTS, SLOTS), SLOTS)
        velocity = tp_ref[t, where, :]
        ratio = tp_ref[t, 6 * SLOTS : 7 * SLOTS, :]
        mass = tp_ref[t, 7 * SLOTS : 8 * SLOTS, :]
        count = count_row_ref[:, pl.ds(pl.multiple_of(t * LANES, LANES), LANES)]
        drag = jnp.where(iota((SLOTS, LANES), 0) < count, ratio * (fluid - velocity), 0.0)
        tp_ref[t, where, :] = velocity + drag
        push_ref[t, pl.ds(pl.multiple_of((1 + f) * SLOTS, SLOTS), SLOTS), :] = -(mass * drag)
        return f

    for f in range(3):
        step(0, f)
        if f < 2:
            gather(f + 1)
        step(1, f)

    heads = []
    for t in range(tiles):
        rows = slice(t * LANES, (t + 1) * LANES)
        push_ref[t, 0:SLOTS, :] = jnp.broadcast_to(slot_row[:, rows], (SLOTS, LANES))
        push_ref[t, 4 * SLOTS :, :] = jnp.zeros((LANES - 4 * SLOTS, LANES), F32)
        heads.append(jnp.concatenate([tp_ref[t].T, push_ref[t].T], axis=1))
    head = jnp.concatenate(heads, axis=0)
    if moves:
        send_ref, position_ref = out_refs
        devices = send_ref.shape[0] // HEAD
        rows = picked(scatter, head)
        lane = iota((devices, LANES), 1)
        for q in range(CAP):
            mine = slice(q * devices, (q + 1) * devices)
            send_ref[pl.ds(q, devices, stride=HEAD), :] = rows[mine, :LANES]
            if q % 2:
                both = jnp.where(lane < LANES // 2, before, pltpu.roll(rows[mine, LANES:], LANES // 2, 1))
                send_ref[pl.ds(CAP + q // 2, devices, stride=HEAD), :] = both
            before = rows[mine, LANES:]
    else:
        head_ref, slot_ref = out_refs
        head_ref[...] = head
        slot_ref[...] = slot_row.astype(jnp.int32)


def pack_kernel(position_ref, fields_ref, out_ref):
    devices = out_ref.shape[0]
    onehot = (iota((devices * CAP, EL), 0) == position_ref[...]).astype(BF16)
    for f in range(3):
        rows = picked(onehot, fields_ref[f])
        for h in range(2):
            at = COMP * f + 8 * h
            left = 2 * h * LANES
            out_ref[:, at : at + 8, :] = interleave(
                rows[:, left : left + LANES], rows[:, left + LANES : left + 2 * LANES]
            )


def lagrange_rows(coord):
    diffs = [coord - p for p in POINTS]
    left = [None] * NP
    right = [None] * NP
    for i in range(1, NP):
        left[i] = diffs[i - 1] if i == 1 else left[i - 1] * diffs[i - 1]
    for i in range(NP - 2, -1, -1):
        right[i] = diffs[i + 1] if i == NP - 2 else right[i + 1] * diffs[i + 1]
    out = []
    for i in range(NP):
        scale = 1.0
        for m in range(NP):
            if m != i:
                scale /= POINTS[i] - POINTS[m]
        if i == 0:
            term = right[0]
        elif i == NP - 1:
            term = left[i]
        else:
            term = left[i] * right[i]
        out.append(term * float(scale))
    return out


def gaussian_rows(coord):
    return [jnp.exp(-((p - coord) ** 2) * (0.5 / 0.35**2)) for p in POINTS]


def shift_z(x):
    n = x.shape[0] // NP
    x = x.reshape(n, NP, LANES)
    node = iota((n, NP, LANES), 1)
    bz = iota((n, NP, LANES), 2) % BZ
    down = pltpu.roll(pltpu.roll(x, 1, 1), 1, 2)
    up = pltpu.roll(pltpu.roll(x, NP - 1, 1), LANES - 1, 2)
    x = x + jnp.where((node == 0) & (bz > 0), down, 0.0)
    x = x + jnp.where((node == NP - 1) & (bz < BZ - 1), up, 0.0)
    return x.reshape(n * NP, LANES)


def force_kernel(
    head_ref,
    stay_slot_ref,
    recv_ref,
    force_ref,
    xup_ref,
    xdn_ref,
    yup_ref,
    ydn_ref,
    left_ref,
    right_ref,
    part_ref,
    slot_ref,
    peers_ref,
    tp_ref,
    push_ref,
    basis_ref,
    work_ref,
):
    tiles = EL // LANES
    devices = recv_ref.shape[0] // HEAD
    particles, extra = [], []
    for q in range(CAP):
        particles.append(recv_ref[pl.ds(q, devices, stride=HEAD), :])
        both = recv_ref[pl.ds(CAP + q // 2, devices, stride=HEAD), :]
        extra.append(pltpu.roll(both, LANES // 2, 1) if q % 2 else both)
    particles = jnp.concatenate(particles, axis=0)
    extra = jnp.concatenate(extra, axis=0)
    slot_row = extra.T[0:1, :].astype(jnp.int32)
    at = iota((devices * CAP, devices * CAP), 0)
    turned = at // devices + at % devices * CAP == iota((devices * CAP, devices * CAP), 1)
    high, low = split(jnp.broadcast_to(slot_row.astype(F32), (8, devices * CAP)))
    order = turned.astype(BF16)
    row = jnp.dot(high, order, preferred_element_type=F32)
    row = row + jnp.dot(low, order, preferred_element_type=F32)
    row = row[0:1].astype(jnp.int32)
    filled = row > 0
    earlier = (iota((devices * CAP, devices * CAP), 0) < iota((devices * CAP, devices * CAP), 1)).astype(BF16)
    rank = jnp.dot(
        jnp.broadcast_to(filled.astype(F32), (8, devices * CAP)).astype(BF16),
        earlier,
        preferred_element_type=F32,
    )[0:1]
    key = jnp.where(filled, rank.astype(jnp.int32), -1)
    packed = (iota((MOVERS, devices * CAP), 0) == key).astype(BF16)
    slot_ref[...] = picked_row(row, packed).astype(jnp.int32)
    peers_ref[...] = picked_row(iota((1, devices * CAP), 1) // CAP, packed).astype(jnp.int32)
    slots = jnp.concatenate([slot_row, stay_slot_ref[...]], axis=1)
    onehot = (iota((EL, EL + MOVERS), 0) + 1 == slots).astype(BF16)
    arrived = jnp.concatenate([particles, extra], axis=1)
    both = picked(onehot, jnp.concatenate([arrived, head_ref[...]], axis=0))
    record = both[:, :LANES]
    push = both[:, LANES:]
    part_ref[...] = record
    for t in range(tiles):
        rows = slice(t * LANES, (t + 1) * LANES)
        tp_ref[t] = record[rows].T
        push_ref[t] = push[rows].T

    def make_basis(t, carry):
        for d in range(3):
            rows = gaussian_rows(tp_ref[t, d * SLOTS : (d + 1) * SLOTS, :])
            for n in range(NP):
                basis_ref[t, d, n * SLOTS : (n + 1) * SLOTS, :] = rows[n]
        return carry

    lax.fori_loop(0, tiles, make_basis, 0)

    def step(index, carry):
        f = index // tiles
        t = index % tiles

        def basis(which, n, p):
            return basis_ref[t, which, pl.ds(n * SLOTS + p, 1), :]

        for p in range(SLOTS):
            along_z = basis_ref[t, 2, pl.ds(p, NP, stride=SLOTS), :]
            value = push_ref[t, pl.ds((1 + f) * SLOTS + p, 1), :]
            work_ref[p * NP : (p + 1) * NP, :] = (0.5 * value) * along_z
        for pair in range(NP // 2):
            acc = [[None] * NP for _ in range(2)]
            for p in range(SLOTS):
                base = work_ref[p * NP : (p + 1) * NP, :]
                lines = [base * basis(1, 2 * pair + i, p) for i in range(2)]
                for a in range(NP):
                    weight = basis(0, a, p)
                    for i in range(2):
                        term = lines[i] * weight
                        acc[i][a] = term if acc[i][a] is None else acc[i][a] + term
            for i in range(2):
                for a in range(NP):
                    force_ref[f, t, pl.ds(a * 64 + (2 * pair + i) * 8, 8), :] = acc[i][a]
        return carry

    lax.fori_loop(0, 3 * tiles, step, 0)

    lane = iota((NP, LANES), 1)
    bz = iota((64, LANES), 1) % BZ
    for f in range(3):
        xup_ref[f] = force_ref[f, tiles - 1, 448:512, :]
        xdn_ref[f] = force_ref[f, 0, 0:64, :]
        left_ref[f] = pltpu.roll(force_ref[f, tiles - 1, 504:512, :], BZ, 1)
        right_ref[f] = pltpu.roll(force_ref[f, 0, 56:64, :], BZ, 1)
        for t in range(tiles - 1):
            summed = force_ref[f, t, 448:512, :] + force_ref[f, t + 1, 0:64, :]
            force_ref[f, t, 448:512, :] = summed
            force_ref[f, t + 1, 0:64, :] = summed
        for a in range(NP):
            first = slice(a * 64, a * 64 + 8)
            last = slice(a * 64 + 56, a * 64 + 64)
            up_line = jnp.zeros((NP, LANES), F32)
            down_line = jnp.zeros((NP, LANES), F32)
            for t in range(tiles):
                upper = force_ref[f, t, last, :]
                lower = force_ref[f, t, first, :]
                take = lane // BZ == t
                up_line = jnp.where(take, pltpu.roll(upper, 16 * t + 16, 1), up_line)
                moved = pltpu.roll(lower, 16 * t, 1) if t else lower
                down_line = jnp.where(take, moved, down_line)
                force_ref[f, t, first, :] = lower + jnp.where(
                    lane >= BZ, pltpu.roll(upper, BZ, 1), 0.0
                )
                force_ref[f, t, last, :] = upper + jnp.where(
                    lane < LANES - BZ, pltpu.roll(lower, LANES - BZ, 1), 0.0
                )
            yup_ref[f, a * 8 : a * 8 + 8, :] = up_line
            ydn_ref[f, a * 8 : a * 8 + 8, :] = down_line
        for t in range(tiles):
            lower = force_ref[f, t, pl.ds(0, 64, stride=NP), :]
            upper = force_ref[f, t, pl.ds(NP - 1, 64, stride=NP), :]
            force_ref[f, t, pl.ds(0, 64, stride=NP), :] = lower + jnp.where(
                bz > 0, pltpu.roll(upper, 1, 1), 0.0
            )
            force_ref[f, t, pl.ds(NP - 1, 64, stride=NP), :] = upper + jnp.where(
                bz < BZ - 1, pltpu.roll(lower, LANES - 1, 1), 0.0
            )


def edge_kernel(below_ref, above_ref, ydn_ref, yb_ref, cb_ref, ca_ref, token_ref, down_ref, low_ref):
    lane = iota((NP, LANES), 1)
    first = lane < BZ
    last = (lane >= 3 * BZ) & (lane < 4 * BZ)
    for f in range(3):
        down_ref[f] = ydn_ref[f]
        down_ref[f, 0:8, :] += jnp.where(first, below_ref[f, 0:8, :], 0.0)
        down_ref[f, 56:64, :] += jnp.where(last, pltpu.roll(above_ref[f, 0:8, :], 3 * BZ, 1), 0.0)
        low_ref[f] = yb_ref[f]
        low_ref[f, 0:8, :] += jnp.where(first, cb_ref[f], 0.0)
        low_ref[f, 56:64, :] += jnp.where(last, pltpu.roll(ca_ref[f], 3 * BZ, 1), 0.0)


def face_delta(face):
    lane = iota((NP, LANES), 1)
    upper = face[56:64]
    lower = face[0:8]
    new_lower = lower + jnp.where(lane >= BZ, pltpu.roll(upper, BZ, 1), 0.0)
    new_upper = upper + jnp.where(lane < LANES - BZ, pltpu.roll(lower, LANES - BZ, 1), 0.0)
    return shift_z(0.5 * jnp.concatenate([new_lower, face[8:56], new_upper], axis=0))


def face_delta(face):
    lane = iota((NP, LANES), 1)
    upper = face[56:64]
    lower = face[0:8]
    new_lower = lower + jnp.where(lane >= BZ, pltpu.roll(upper, BZ, 1), 0.0)
    new_upper = upper + jnp.where(lane < LANES - BZ, pltpu.roll(lower, LANES - BZ, 1), 0.0)
    return shift_z(jnp.concatenate([new_lower, face[8:56], new_upper], axis=0))


def base_kernel(rank_ref, place_ref, fields_ref, force_ref, out_ref, token_ref):
    tiles = EL // LANES
    stay_col = as_column((place_ref[...] // EL == rank_ref[0]).astype(F32)) > 0
    for f in range(3):
        for t in range(tiles):
            rows = slice(t * LANES, (t + 1) * LANES)
            for j in range(NODES // LANES):
                cols = slice(j * LANES, (j + 1) * LANES)
                own = jnp.where(stay_col[rows], fields_ref[f, rows, cols], 0.0)
                out_ref[f, rows, cols] = own + force_ref[f, t, cols, :].T
    token_ref[...] = jnp.zeros((8, LANES), F32)


def lines_of(values, node, line_ref):
    values = shift_z(jnp.where(iota((64, LANES), 1) < BX * BZ, values, 0.0))
    for a in range(NP):
        at = a * 64 + node * 8
        line_ref[at : at + 8, :] = values[a * 8 : a * 8 + 8]
    cols = [line_ref[j * LANES : (j + 1) * LANES, :].T for j in range(NODES // LANES)]
    return jnp.concatenate(cols, axis=1)[: BX * BZ]


def place_kernel(
    peers_ref,
    slot_ref,
    recv_ref,
    base_ref,
    xb_ref,
    xa_ref,
    low_ref,
    out_ref,
    ends_ref,
    recv_held,
    held_ref,
    line_ref,
    lows_ref,
    arrived,
    left,
):
    tiles = EL // LANES

    peers = peers_ref[...]
    for c in range(PEERS):
        block = recv_ref.at[peers[0, CAP * c]]
        pltpu.make_async_copy(block, recv_held.at[c], arrived.at[0, 0]).start()
    whole_recv = pltpu.make_async_copy(recv_ref.at[pl.ds(0, PEERS)], recv_held, arrived.at[0, 0])
    loads = []
    for f in range(3):
        loads.append(pltpu.make_async_copy(base_ref.at[f], held_ref.at[f], arrived.at[f, 1]))
        loads[f].start()
    onehot = (iota((EL, MOVERS), 0) + 1 == slot_ref[...]).astype(BF16)
    blank = jnp.zeros((64, LANES), F32)
    line_ref[...] = jnp.zeros((NODES, LANES), F32)
    for f in range(3):
        lows_ref[f] = lines_of(low_ref[f], 0, line_ref)
    copies = []
    for f in range(3):
        if f == 0:
            whole_recv.wait()
        pieces = []
        for h in range(2):
            pieces += list(deinterleave(recv_held[:, COMP * f + 8 * h : COMP * f + 8 * h + 8, :]))
        rows = picked(onehot, jnp.concatenate(pieces, axis=1))
        loads[f].wait()
        held_ref[f] += rows
        delta = jnp.concatenate([face_delta(xb_ref[f]), blank], axis=0)
        held_ref[f, 0:LANES, 0:LANES] += delta.T
        delta = jnp.concatenate([blank, face_delta(xa_ref[f])], axis=0)
        held_ref[f, EL - LANES :, NODES - LANES :] += delta.T
        for t in range(tiles):
            mine = slice(t * BZ, (t + 1) * BZ)
            held_ref[f, t * LANES : t * LANES + BZ, :] += lows_ref[f, mine, :]
            inner = pl.ds(t * LANES, LANES - BZ)
            copies.append(
                pltpu.make_async_copy(held_ref.at[f, inner], out_ref.at[f, inner], left.at[f, t])
            )
            copies[-1].start()
            last = (t + 1) * LANES
            ends_ref[f, mine, :] = held_ref[f, last - BZ : last, :]
    for copy in copies:
        copy.wait()


def lines_kernel(ends_ref, ya_ref, inner_ref, out_ref, line_ref, held_ref, left):
    tiles = EL // LANES
    line_ref[...] = jnp.zeros((NODES, LANES), F32)
    copies = []
    for f in range(3):
        held_ref[f] = ends_ref[f] + lines_of(ya_ref[f], NP - 1, line_ref)
        for t in range(tiles):
            at = pl.ds((t + 1) * LANES - BZ, BZ)
            mine = pl.ds(t * BZ, BZ)
            copies.append(
                pltpu.make_async_copy(held_ref.at[f, mine], out_ref.at[f, at], left.at[f, t])
            )
            copies[-1].start()
    for copy in copies:
        copy.wait()


def passed_along(x, along_ex, along_ey):
    rows, cols = lax.axis_size("ex"), lax.axis_size("ey")
    pairs = []
    for i in range(rows):
        for j in range(cols):
            to_i, to_j = i + along_ex, j + along_ey
            if 0 <= to_i < rows and 0 <= to_j < cols:
                pairs.append((i * cols + j, to_i * cols + to_j))
    return lax.ppermute(x, AXES, pairs)


def whole(n):
    return [pl.BlockSpec(memory_space=pltpu.VMEM)] * n


def params(mib):
    return pltpu.CompilerParams(vmem_limit_bytes=mib * MIB)


def cost(micros):
    return pl.CostEstimate(flops=0, bytes_accessed=int(micros * 3_000_000), transcendentals=0)


def body(fields, particles, counts, new_place):
    devices = lax.axis_size(AXES)
    rank = lax.axis_index(AXES).astype(jnp.int32).reshape(1)
    fields = jnp.transpose(fields, (1, 0, 2))
    place = new_place.reshape(1, EL)
    counts = counts.reshape(1, EL)
    smem = [pl.BlockSpec(memory_space=pltpu.SMEM)]
    anywhere = pl.BlockSpec(memory_space=pl.ANY)
    in_hbm = pl.BlockSpec(memory_space=pltpu.HBM)
    struct = jax.ShapeDtypeStruct
    tiles = EL // LANES
    tile_scratch = pltpu.VMEM((tiles, LANES, LANES), F32)
    basis_scratch = pltpu.VMEM((tiles, 3, LANES, LANES), F32)
    work_scratch = pltpu.VMEM((LANES, LANES), F32)
    half = MOVERS // LANES

    def interp(moves, out_shape, mib, name):
        return pl.pallas_call(
            functools.partial(interp_kernel, moves),
            out_shape=out_shape,
            in_specs=smem + [anywhere] * 4,
            out_specs=tuple(whole(2)),
            scratch_shapes=[
                pltpu.VMEM((half, LANES, LANES), F32),
                pltpu.VMEM((half, LANES, LANES), F32),
                pltpu.VMEM((half, 3, LANES, LANES), F32),
                pltpu.VMEM((3, half, NODES, LANES), F32),
                work_scratch,
                pltpu.VMEM((1, MOVERS), jnp.int32),
                pltpu.VMEM((3, EL, NODES), F32),
                pltpu.VMEM((1, EL), jnp.int32),
                pltpu.VMEM((1, EL), jnp.int32),
                pltpu.VMEM((EL, PARTS), F32),
                pltpu.SemaphoreType.DMA((6,)),
            ]
            + [pltpu.VMEM((half, NODES, LANES), F32)] * 3,
            compiler_params=params(mib),
            cost_estimate=cost(6),
            name=name,
        )(rank, place, counts, fields, particles)

    send_head, position = interp(
        True, (struct((devices * HEAD, LANES), F32), struct((1, EL), jnp.int32)), 58, "moving"
    )
    head, stay_slots = interp(
        False, (struct((MOVERS, 2 * LANES), F32), struct((1, MOVERS), jnp.int32)), 40, "staying"
    )
    recv_head = lax.all_to_all(send_head.reshape(-1), ORDER, split_axis=0, concat_axis=0, tiled=True)
    recv_head = recv_head.reshape(devices * HEAD, LANES)
    send = pl.pallas_call(
        pack_kernel,
        out_shape=struct((devices, 3 * COMP, LANES), F32),
        in_specs=whole(2),
        out_specs=whole(1)[0],
        compiler_params=params(58),
        cost_estimate=cost(5),
        name="pack",
    )(position, fields)
    recv = lax.all_to_all(send, ORDER, split_axis=0, concat_axis=0, tiled=True)
    face = struct((3, 64, LANES), F32)
    corner = struct((3, NP, LANES), F32)
    force, xup, xdn, yup, ydn, left, right, particles_next, slots, peers = pl.pallas_call(
        force_kernel,
        out_shape=(
            struct((3, tiles, NODES, LANES), F32),
            face,
            face,
            face,
            face,
            corner,
            corner,
            struct((EL, PARTS), F32),
            struct((1, MOVERS), jnp.int32),
            struct((1, MOVERS), jnp.int32),
        ),
        in_specs=whole(3),
        out_specs=tuple(whole(10)),
        scratch_shapes=[tile_scratch, tile_scratch, basis_scratch, work_scratch],
        compiler_params=params(40),
        cost_estimate=cost(8),
        name="force",
    )(head, stay_slots, recv_head)
    base, token = pl.pallas_call(
        base_kernel,
        out_shape=(pltpu.HBM((3, EL, NODES), F32), struct((8, LANES), F32)),
        in_specs=smem + whole(3),
        out_specs=tuple(whole(2)),
        compiler_params=params(20),
        cost_estimate=cost(5),
        name="base",
    )(rank, place, fields, force)
    below_x = passed_along(xup, 1, 0)
    above_x = passed_along(xdn, -1, 0)
    below_y = passed_along(yup, 0, 1)
    corner_below = passed_along(left, 1, 1)
    corner_above = passed_along(right, -1, 1)
    down, low = pl.pallas_call(
        edge_kernel,
        out_shape=(face, face),
        in_specs=whole(7),
        out_specs=tuple(whole(2)),
        compiler_params=params(8),
        cost_estimate=cost(1),
        name="edge",
    )(below_x, above_x, ydn, below_y, corner_below, corner_above, token)
    above_y = passed_along(down, 0, -1)
    ends = (3, tiles * BZ, NODES)
    inner, ends_out = pl.pallas_call(
        place_kernel,
        out_shape=(struct((3, EL, NODES), F32), struct(ends, F32)),
        in_specs=whole(2) + [in_hbm, in_hbm] + whole(3),
        out_specs=(in_hbm, whole(1)[0]),
        scratch_shapes=[
            pltpu.VMEM((PEERS, 3 * COMP, LANES), F32),
            pltpu.VMEM((3, EL, NODES), F32),
            pltpu.VMEM((NODES, LANES), F32),
            pltpu.VMEM(ends, F32),
            pltpu.SemaphoreType.DMA((3, 2)),
            pltpu.SemaphoreType.DMA((3, tiles)),
        ],
        compiler_params=params(20),
        cost_estimate=cost(3),
        name="place",
    )(
        peers,
        slots,
        recv,
        pltpu.with_memory_space_constraint(base, pltpu.HBM),
        below_x,
        above_x,
        low,
    )
    out = pl.pallas_call(
        lines_kernel,
        out_shape=struct((3, EL, NODES), F32),
        in_specs=whole(2) + [anywhere],
        out_specs=anywhere,
        scratch_shapes=[
            pltpu.VMEM((NODES, LANES), F32),
            pltpu.VMEM(ends, F32),
            pltpu.SemaphoreType.DMA((3, tiles)),
        ],
        input_output_aliases={2: 0},
        compiler_params=params(10),
        cost_estimate=cost(1),
        name="lines",
    )(ends_out, above_y, inner)
    return jnp.transpose(out, (1, 0, 2)), particles_next


def solution(mesh):
    return jax.shard_map(
        body,
        mesh=mesh,
        in_specs=(P(AXES, None, None), P(AXES, None), P(AXES), P(AXES)),
        out_specs=(P(AXES, None, None), P(AXES, None)),
        check_vma=False,
    )
```
